128 devices in a mesh: tm: 4 (over x_lo, core), lat: 8 (over z, x_hi), lon: 4 (over y).
Axes of the slice: x: 4 (x_hi: 2, x_lo: 2; x = x_hi * 2 + x_lo), y: 4, z: 4, core: 2. Of those that a mesh axis runs over, the one named last changes fastest.
Arguments:
- forcing: float32 [4, 137, 128, 512], P('tm', None, 'lat', 'lon'), may hold values from -6 to 6
- vertical: float32 [13, 137, 137], replicated, may hold values from -0.5 to 0.5
- lat_factor: float32 [8, 8], replicated, may hold values from -2 to 2
- lon_factor: float32 [32, 32], replicated, may hold values from -1 to 1
Outputs:
- increment: float32 [4, 137, 128, 512], P('tm', None, 'lat', 'lon')
- jump: float32 [4, 137, 128, 512], P('tm', None, 'lat', 'lon')
The draws below stay inside these ranges and needn't reach their ends.
All inputs are finite; a program needn't handle non-finite values.
Results may differ from the reference program's by a relative error of at most 0.0001.
Values sent between devices are 32-bit elements; how exact they have to be, the bound alone decides.
A program may use at most 64 MiB of HBM per device.

```python
import jax
import jax.numpy as jnp
from jax import lax

LEV = 137
LEVELS = 4
BANDS = 13
WINDOWS = 4
NLAT = 128
NLON = 512
NCLAT = 8
NCLON = 32


def levels(own_key, dims, shards, least, top_value):
    def one(axis_at, shards_of):
        steps = jax.random.uniform(jax.random.fold_in(jax.random.fold_in(own_key, 6), axis_at), (shards_of,), jnp.float32, least / len(shards), top_value / len(shards))
        return jnp.repeat(jnp.exp(steps), dims[axis_at] // shards_of).reshape((-1,) + (1,) * (len(dims) - axis_at - 1))

    loudness = one(*shards[0])
    for cut in shards[1:]:
        loudness = loudness * one(*cut)
    return loudness


def centred(rng, dims, deviation, bound, cuts=(), kind=jnp.bfloat16):
    drawn = deviation * jax.random.normal(rng, dims, jnp.float32)
    if cuts:
        drawn = drawn * levels(rng, dims, cuts, -0.22, 0.18)
    return jnp.clip(drawn, -bound, bound).astype(kind)


def setup_inputs(seed: int = 0) -> dict:
    arg_keys = jax.random.split(jax.random.key(seed), 5)
    return {
        "forcing": centred(arg_keys[0], (WINDOWS, LEV, NLAT, NLON), 1.0, 6.0, ((0, 4), (2, 8), (3, 4)), jnp.float32),
        "vertical": centred(arg_keys[1], (BANDS, LEV, LEV), LEV ** -0.5, 0.5, (), jnp.float32),
        "lat_factor": centred(arg_keys[2], (NCLAT, NCLAT), NCLAT ** -0.5, 2.0, (), jnp.float32),
        "lon_factor": centred(arg_keys[3], (NCLON, NCLON), NCLON ** -0.5, 1.0, (), jnp.float32),
    }


HIGH = lax.Precision.HIGHEST


def cut(field, start, stop, axis, stride=1):
    return lax.slice_in_dim(field, start, stop, stride, axis)


def analyse(padded, axis):
    half = (padded.shape[axis] - 4) // 2
    even = cut(padded, 0, 2 * half + 3, axis, 2)
    odd = cut(padded, 1, 2 * half + 4, axis, 2)
    detail_ext = cut(odd, 0, half + 1, axis) - 0.5 * (cut(even, 0, half + 1, axis) + cut(even, 1, half + 2, axis))
    smooth = cut(even, 1, half + 1, axis) + 0.25 * (cut(detail_ext, 0, half, axis) + cut(detail_ext, 1, half + 1, axis))
    return smooth, cut(detail_ext, 1, half + 1, axis)


def synthesise(smooth_pad, detail_pad, axis):
    half = smooth_pad.shape[axis] - 2
    even = cut(smooth_pad, 1, half + 2, axis) - 0.25 * (cut(detail_pad, 0, half + 1, axis) + cut(detail_pad, 1, half + 2, axis))
    odd = cut(detail_pad, 1, half + 1, axis) + 0.5 * (cut(even, 0, half, axis) + cut(even, 1, half + 1, axis))
    both = jnp.stack([cut(even, 0, half, axis), odd], axis=axis + 1)
    return both.reshape(odd.shape[:axis] + (2 * half,) + odd.shape[axis + 1:])


def pad_axis(field, width, axis, wrapped):
    widths = [(0, 0)] * field.ndim
    widths[axis] = (width, width)
    if wrapped:
        return jnp.pad(field, widths, mode="wrap")
    return jnp.pad(field, widths)


def covary(field, vertical, lat_factor, lon_factor):
    smooth = field
    bands = []
    for level in range(LEVELS):
        lon_s, lon_d = analyse(pad_axis(smooth, 2, 2, True), 2)
        pair = jnp.stack([lon_s, lon_d])
        lat_s, lat_d = analyse(pad_axis(pair, 2, 2, False), 2)
        smooth = lat_s[0]
        details = jnp.stack([lat_s[1], lat_d[0], lat_d[1]])
        bands.append(jnp.einsum("bij,bjxy->bixy", vertical[3 * level:3 * level + 3], details, precision=HIGH))
    mixed = jnp.einsum("ab,kbc->kac", lat_factor, smooth, precision=HIGH)
    mixed = jnp.einsum("kac,dc->kad", mixed, lon_factor, precision=HIGH)
    smooth = jnp.einsum("ij,jac->iac", vertical[BANDS - 1], mixed, precision=HIGH)
    for level in range(LEVELS - 1, -1, -1):
        band = bands[level]
        smooth_part = jnp.stack([smooth, band[0]])
        detail_part = jnp.stack([band[1], band[2]])
        lifted = synthesise(pad_axis(smooth_part, 1, 2, False), pad_axis(detail_part, 1, 2, False), 2)
        smooth = synthesise(pad_axis(lifted[0], 1, 2, True), pad_axis(lifted[1], 1, 2, True), 2)
    return smooth


def reference(forcing, vertical, lat_factor, lon_factor):
    increment = lax.map(lambda field: covary(field, vertical, lat_factor, lon_factor), forcing)
    earlier = jnp.concatenate([jnp.zeros_like(increment[:1]), increment[:-1]], axis=0)
    return increment, increment - earlier
```

```python
import numpy as np
import jax
import jax.numpy as jnp
import ml_dtypes
from jax import lax
from jax.experimental import pallas as pl
from jax.experimental.pallas import tpu as pltpu
from jax.sharding import PartitionSpec as P

LEV, LP = 137, 144
ROWS, COLS = 16, 128
BANDS = 13
NLAT_D, NLON_D = 8, 4
MESH = pl.DeviceIdType.MESH
HIGH = lax.Precision.HIGHEST
F32, BF = jnp.float32, jnp.bfloat16

MLAT = {1: 8, 2: 4, 3: 2, 4: 1}
MLON = {1: 64, 2: 32, 3: 16, 4: 8}
DROW = {1: 0, 2: 19, 3: 30, 4: 37}
SROW = {1: 10, 2: 25, 3: 34, 4: 40}
NROWS = 42
PACK = {2: (0, 1, -1, 64), 3: (66, 2, -1, 33), 4: (101, 3, -1, 17)}
CLANE = 100
LEVEL_OF = {}
for _l in (1, 2, 3, 4):
    for _i in range(MLAT[_l] + 2):
        LEVEL_OF[DROW[_l] + _i] = (_l, "D", _i - 1)
    for _i in range(MLAT[_l] + 1):
        LEVEL_OF[SROW[_l] + _i] = (_l, "S", _i)


def lift(seq, size):
    lo, hi = min(seq), max(seq)
    zero = np.zeros(size)
    get = lambda table, i: table.get(i, zero)
    d, s = {}, {}
    for i in range(lo // 2 - 2, hi // 2 + 3):
        d[i] = get(seq, 2 * i + 1) - 0.5 * (get(seq, 2 * i) + get(seq, 2 * i + 2))
    for i in range(lo // 2 - 2, hi // 2 + 3):
        s[i] = get(seq, 2 * i) + 0.25 * (get(d, i - 1) + get(d, i))
    keep = lambda table: {i: v for i, v in table.items() if np.any(v)}
    return keep(s), keep(d)


def message_lanes():
    left, right = {}, {}
    nl = nr = 0
    for j in range(NROWS):
        l, kind, _ = LEVEL_OF[j]
        ql = ["dm1"] if l == 1 else (["sm", "dm1", "dm"] if kind == "D" else ["dm1", "dm"])
        qr = ["d-1", "d0"] if (l == 1 or kind == "S") else ["s0", "d-1", "d0"]
        left[j], right[j] = (nl, ql), (nr, qr)
        nl, nr = nl + len(ql), nr + len(qr)
    assert nl <= CLANE and nr <= CLANE
    return left, right


LEFT, RIGHT = message_lanes()


def lon_tables():
    raw = {i: np.eye(256)[i] for i in range(COLS)}
    smooth, detail = {0: raw}, {}
    for l in range(1, 5):
        smooth[l], detail[l] = lift(smooth[l - 1], 256)
    ext_s = {}
    for l in (2, 3, 4):
        at, depth, lo, hi = PACK[l]
        seq = {i: np.eye(256)[128 + at + i - lo] for i in range(lo, hi + 1)}
        for k in range(l, 5):
            s, d = lift(seq, 256)
            seq = s
            ext_s[l, k] = (s, d)
    zero = np.zeros(256)
    full_s, full_d = {}, {}
    for k in range(1, 5):
        s, d = dict(smooth[k]), dict(detail[k])
        for l in range(2, k + 1):
            for table, more in ((s, ext_s[l, k][0]), (d, ext_s[l, k][1])):
                for i, v in more.items():
                    table[i] = table.get(i, zero) + v
        full_s[k], full_d[k] = s, d
    return smooth, full_s, full_d


def constants():
    smooth, fs, fd = lon_tables()
    zero = np.zeros(256)
    out = {}
    for l in (1, 2, 3, 4):
        m = MLON[l]
        w = np.zeros((256, 256))
        off = 128 if l == 1 else 64
        for i in range(0, m + 1):
            w[:, i] = fs[l].get(i, zero)
        for i in range(-1, m + 1):
            w[:, off + i + 1] = fd[l].get(i, zero)
        out["W", l] = w if l == 1 else w[:, :128]
        g = np.zeros((256, 256))
        pick = {"sm": fs[l].get(m, zero), "dm1": fd[l].get(m - 1, zero), "dm": fd[l].get(m, zero),
                "s0": fs[l].get(0, zero), "d-1": fd[l].get(-1, zero), "d0": fd[l].get(0, zero)}
        z = np.zeros((256, 256))
        for j in range(NROWS):
            if LEVEL_OF[j][0] != l:
                continue
            smooth_too = LEVEL_OF[j][1] == "D"
            for base, (at, names) in ((0, LEFT[j]), (128, RIGHT[j])):
                for q, name in enumerate(names):
                    lane = base + at + q
                    g[:, lane] = pick[name]
                    row = z[lane]
                    if base == 0:
                        if name == "dm1":
                            row[off + 0] += 1.0
                            if l == 1 and smooth_too:
                                row[0] += 0.25
                        if name == "dm":
                            row[off + 1] += 1.0
                            if smooth_too:
                                row[1] += 0.25
                        if name == "sm":
                            row[0] += 1.0
                    else:
                        if name == "s0":
                            row[m] += 1.0
                        if name == "d-1":
                            row[off + m] += 1.0
                            if smooth_too:
                                row[m - 1] += 0.25
                                if l == 1:
                                    row[m] += -1.75
                        if name == "d0":
                            row[off + m + 1] += 1.0
                            if l == 1 and smooth_too:
                                row[m] += 0.25
        out["G", l] = g
        out["Z", l] = z if l == 1 else z[:, :128]
        n_in = 256 if l == 1 else 128
        eye = np.eye(n_in)
        s = {i: eye[i] for i in range(0, m + 1)}
        d = {i: eye[off + i + 1] for i in range(-1, m + 1)}
        e = {i: s[i] - 0.25 * (d[i - 1] + d[i]) for i in range(0, m + 1)}
        t = np.zeros((n_in, 128))
        for i in range(0, m + 1):
            if 2 * i < 128:
                t[:, 2 * i] = e[i]
            if i < m:
                t[:, 2 * i + 1] = d[i] + 0.5 * (e[i] + e[i + 1])
        out["T", l] = t
    for l in (2, 3, 4):
        at, depth, lo, hi = PACK[l]
        sm = np.zeros((128, 128))
        for i in range(lo, hi + 1):
            sm[:, at + i - lo] = smooth[depth][i][:128]
        out["Sm", l] = sm
    m4 = np.zeros((128, 128))
    for lane in range(88):
        m4[:, lane] = smooth[4][lane % 11 - 1][:128]
    out["M4", 0] = m4
    sel = np.zeros((256, 256))
    for rho in range(2):
        for g in range(2):
            for i in range(4):
                for c in range(11):
                    sel[128 * rho + g * 44 + i * 11 + c, 128 * g + CLANE + 11 * rho + c] = 1.0
    out["Sel", 0] = sel
    return out


CONST = constants()


def pack_constants():
    tiles, where = [], {}

    def put(key, a):
        k, n = a.shape
        where[key] = (sum(t.shape[0] for t in tiles), k, n)
        if n < 256:
            a = np.concatenate([a, np.zeros((k, 256 - n), a.dtype)], 1)
        tiles.append(a)

    for key, a in CONST.items():
        if key == ("W", 1) or key == ("G", 1):
            a = a[:128]
        hi = a.astype(ml_dtypes.bfloat16)
        lo = (a - hi.astype(np.float64)).astype(ml_dtypes.bfloat16)
        put(key + ("hi",), hi)
        if np.any(lo.astype(np.float64)):
            put(key + ("lo",), lo)
    return np.concatenate(tiles, 0), where


CB, CWHERE = pack_constants()


def ext_coefficients():
    syms = {("U", 2): 0, ("U", 3): 1, ("U", 4): 2, ("W", 2): 3, ("W", 3): 4, ("W", 4): 5}
    unit = lambda key: np.eye(6)[syms[key]]
    zero = np.zeros(6)
    s = {i: zero for i in range(9)}
    table = {}
    for l in (2, 3, 4):
        m = MLAT[l]
        d = {-1: unit(("U", l)), m: unit(("W", l))}
        for i in range(m):
            d[i] = s[2 * i + 1] - 0.5 * (s[2 * i] + s[2 * i + 2])
        s = {i: s[2 * i] + 0.25 * (d[i - 1] + d[i]) for i in range(m + 1)}
        for i in range(-1, m + 1):
            table[DROW[l] + i + 1] = d[i]
        for i in range(m + 1):
            table[SROW[l] + i] = s[i]
    out = np.zeros((48, 128), np.float32)
    for j, v in table.items():
        for l in (2, 3, 4):
            at, _, lo, hi = PACK[l]
            out[j - 19, at:at + hi - lo + 1] = v[l - 2]
            out[24 + j - 19, at:at + hi - lo + 1] = v[3 + l - 2]
    return out


def gather_expand():
    out = np.zeros((8, 1024), np.float32)
    for a in range(8):
        for lane in range(88):
            col = a + (lane // 11) % 4 - 1
            if 0 <= col < 8:
                out[col, a * 128 + lane] = 1.0
    return out


EXT = ext_coefficients()
EXPAND = gather_expand()


def split(a):
    hi = a.astype(BF)
    return hi, (a - hi.astype(F32)).astype(BF)


def dot(a, b):
    return jnp.dot(a, b, preferred_element_type=F32)


def kernel(x, vert, latf, lonf, cb, ext_c, expand, inc, jump,
           xs, so, rw, lx, up, dn, p2, cm, r_w, r_u, r_pw, r_pu, r_p2u, r_p2w, cbuf,
           vst, vtmp, cf, qm, o1, o2, tmsg, s_l, s_r, s_o, m_l, m_r, m_o,
           bd, sm, ys, prev, send, recv):
    tm, lat, lon = lax.axis_index("tm"), lax.axis_index("lat"), lax.axis_index("lon")
    mu = (lat > 0).astype(F32)
    mw = (lat < NLAT_D - 1).astype(F32)
    mu2 = (lat > 1).astype(F32)
    mw2 = (lat < NLAT_D - 2).astype(F32)

    def at_lat(k):
        return (tm, lax.rem(lat + k + NLAT_D, NLAT_D), lon)

    def at_lon(k):
        return (tm, lat, lax.rem(lon + k + NLON_D, NLON_D))

    def at_tm(k):
        return (lax.rem(tm + k + 4, 4), lat, lon)

    partners = [at_lat(k) for k in range(1, 8)] + [at_lon(k) for k in range(1, 4)] + [at_tm(1), at_tm(-1)]
    barrier = pltpu.get_barrier_semaphore()
    for p in partners:
        pl.semaphore_signal(barrier, inc=1, device_id=p, device_id_type=MESH)

    def const(key):
        at, k, n = CWHERE[key]
        return cb[at:at + k, 0:n]

    def mm(a, name, l):
        hi, lo = split(a)
        w = const((name, l, "hi"))
        out = dot(hi, w) + dot(lo, w)
        if (name, l, "lo") in CWHERE:
            out = out + dot(hi, const((name, l, "lo")))
        return out

    for r in range(ROWS):
        xs[r, 136:144, :] = jnp.zeros((8, COLS), F32)
        xs[r, 0:LEV, :] = x[pl.ds(r, LEV, stride=ROWS), :]

    for i in range(7):
        rw[1 + i] = xs[2 * i + 1] - 0.5 * (xs[2 * i] + xs[2 * i + 2])
    dn[0] = xs[15] - 0.5 * xs[14]
    up[0] = xs[0]
    up[1] = rw[1]

    pl.semaphore_wait(barrier, len(partners))
    sems = iter(range(64))

    def remote(src, dst, dev, slot=None):
        k = next(sems)
        return pltpu.make_async_remote_copy(
            src_ref=src, dst_ref=dst, send_sem=send.at[k],
            recv_sem=recv.at[k], device_id=dev, device_id_type=MESH)

    copies = []

    def go(c):
        c.start()
        copies.append(c)

    go(remote(up.at[pl.ds(0, 2)], r_w, at_lat(-1)))
    go(remote(dn.at[0], r_u, at_lat(1)))

    so[0] = (-0.125 * mu) * xs[0]
    so[1] = 0.875 * xs[0] + 0.25 * rw[1]
    for i in range(1, 7):
        so[1 + i] = xs[2 * i] + 0.25 * (rw[i] + rw[1 + i])
    so[8] = xs[14] + 0.25 * (rw[7] + dn[0])
    so[9] = (0.25 * mw) * dn[0]
    sbase = {1: 0, 2: 10, 3: 17, 4: 22}
    dbase = {2: 26, 3: 32, 4: 36}
    for l in (2, 3, 4):
        m, a, b, d = MLAT[l], sbase[l - 1], sbase[l], dbase[l]
        S = lambda i: so[a + 1 + i]
        so[d] = S(-1) - 0.5 * S(0)
        for i in range(m):
            so[d + 1 + i] = S(2 * i + 1) - 0.5 * (S(2 * i) + S(2 * i + 2))
        so[d + 1 + m] = (-0.5 * S(2 * m)) if l == 2 else S(2 * m + 1) - 0.5 * S(2 * m)
        so[b] = (0.25 * mu) * so[d]
        for i in range(m):
            so[b + 1 + i] = S(2 * i) + 0.25 * (so[d + i] + so[d + 1 + i])
        so[b + 1 + m] = mw * (S(2 * m) + 0.25 * (so[d + m] + so[d + 1 + m]))
        so[b + 2 + m] = (0.25 * mw) * so[d + 1 + m]
    d4 = mm(so[37], "Sm", 4)
    up[2] = mm(so[27], "Sm", 2) + mm(so[33], "Sm", 3) + d4
    dn[1] = mm(so[30], "Sm", 2) + mm(so[34], "Sm", 3) + d4
    p2[0] = mm(so[38], "Sm", 4)
    p2[1] = mm(so[36], "Sm", 4)
    go(remote(up.at[2], r_pw, at_lat(-1)))
    go(remote(dn.at[1], r_pu, at_lat(1)))
    go(remote(p2.at[0], r_p2u, at_lat(2)))
    go(remote(p2.at[1], r_p2w, at_lat(-2)))
    lane = lax.broadcasted_iota(jnp.int32, (1, 128), 1)
    half = LP // 2
    acc = jnp.zeros((half, 128), F32)
    for i in range(4):
        t = mm(so[22 + i], "M4", 0)
        for g in range(2):
            lo = g * 44 + i * 11
            acc = jnp.where((lane >= lo) & (lane < lo + 11), t[g * half:(g + 1) * half], acc)
    cbuf[lat] = acc
    cm[...] = acc
    for k in range(1, 8):
        go(remote(cm, cbuf.at[lat], at_lat(k)))

    vtmp[...] = jnp.zeros((LP, 256), F32)
    for k in range(BANDS):
        vtmp[0:LEV, 0:LEV] = vert[k]
        hi, lo = split(vtmp[...])
        vst[k, 0:LP, :] = hi
        vst[k, LP:2 * LP, :] = lo
    cf[...] = jnp.zeros((16, 1024), F32)
    cf[0:8, :] = jnp.dot(latf[...], expand[...], precision=HIGH, preferred_element_type=F32)
    rowi = lax.broadcasted_iota(jnp.int32, (128, 32), 0)
    coli = lax.broadcasted_iota(jnp.int32, (128, 32), 1)
    place = ((rowi <= 8) & (coli == lax.rem(8 * lon + rowi, 32))).astype(F32)
    ylon = jnp.dot(place, lonf[...], precision=HIGH, preferred_element_type=F32)
    for rho in range(2):
        for n, delta in enumerate((0, -1, 1, 2)):
            c = rowi - (CLANE + 11 * rho)
            pick = ((c >= 0) & (c < 11) & (coli == lax.rem(8 * lon + 8 * delta + 63 + c, 32))).astype(F32)
            q = lax.dot_general(pick, ylon, (((1,), (1,)), ((), ())), precision=HIGH,
                                preferred_element_type=F32)
            hi, lo = split(q)
            qm[0, n * 128:(n + 1) * 128, rho * 128:(rho + 1) * 128] = hi
            qm[1, n * 128:(n + 1) * 128, rho * 128:(rho + 1) * 128] = lo

    for c in copies:
        c.wait()
    copies.clear()

    x16 = lambda: mw * r_w[0]
    rw[0] = mu * r_u[...] - 0.5 * xs[0]
    rw[8] = dn[0] - 0.5 * x16()
    rw[9] = mw * r_w[1]
    for i in range(8):
        rw[10 + i] = xs[2 * i] + 0.25 * (rw[i] + rw[i + 1])
    rw[18] = x16() + (0.25 * mw) * (rw[8] + rw[9])
    raw = lambda j: rw[j] if j < 19 else lx[j - 19, :, 0:128]
    for l in (2, 3, 4):
        m, a, d, b = MLAT[l], SROW[l - 1], DROW[l], SROW[l]
        lx[d - 19, :, 0:128] = so[dbase[l]]
        lx[d + m + 1 - 19, :, 0:128] = so[dbase[l] + m + 1]
        for i in range(m):
            lx[d + 1 + i - 19, :, 0:128] = raw(a + 2 * i + 1) - 0.5 * (raw(a + 2 * i) + raw(a + 2 * i + 2))
        for i in range(m + 1):
            v = raw(a + 2 * i) + 0.25 * (raw(d + i) + raw(d + i + 1))
            lx[b + i - 19, :, 0:128] = mw * v if i == m else v
    r_pu[...] = mu * r_pu[...] + mu2 * r_p2u[...]
    r_pw[...] = mw * r_pw[...] + mw2 * r_p2w[...]
    for j in range(19, NROWS):
        cu, cw = ext_c[j - 19:j - 18, :], ext_c[24 + j - 19:24 + j - 18, :]
        l, kind, i = LEVEL_OF[j]
        if kind == "S" and i == MLAT[l]:
            cu, cw = cu * mw, cw * mw
        lx[j - 19, :, 128:256] = r_pu[...] * cu + r_pw[...] * cw
    rw[0] = mu * rw[0]
    for l in (2, 3, 4):
        lx[DROW[l] - 19] = mu * lx[DROW[l] - 19]

    tt = []
    for rho in range(2):
        c = cf[pl.ds(lat + rho, 1), :]
        tt.append(sum(cbuf[a] * c[:, a * 128:(a + 1) * 128] for a in range(8)))
    u2 = mm(jnp.concatenate(tt, axis=1), "Sel", 0)
    s_o[0:half, :] = u2[:, 0:128]
    s_o[half:LP, :] = u2[:, 128:256]

    groups = {1: (0, 19), 2: (19, 30), 3: (30, 37), 4: (37, 42)}

    def operand(l):
        lo, hi = groups[l]
        if l == 1:
            return rw[...].reshape(19 * LP, 128)
        return lx[lo - 19:hi - 19].reshape((hi - lo) * LP, 256)

    s_l[...] = s_o[...]
    s_r[...] = s_o[...]
    for l in (1, 2, 3, 4):
        lo, hi = groups[l]
        tmsg[0:hi - lo] = mm(operand(l), "G", l).reshape(hi - lo, LP, 256)
        for dst, table, base in ((s_l, LEFT, 0), (s_r, RIGHT, 128)):
            v = dst[...]
            for j in range(lo, hi):
                at, names = table[j]
                v = jnp.where((lane >= at) & (lane < at + len(names)), tmsg[j - lo, :, base:base + 128], v)
            dst[...] = v
    go(remote(s_l, m_l, at_lon(1)))
    go(remote(s_r, m_r, at_lon(-1)))
    go(remote(s_o, m_o, at_lon(2)))

    o1[...] = mm(operand(1), "W", 1).reshape(19, LP, 256)
    for l in (2, 3, 4):
        lo, hi = groups[l]
        o2[lo - 19:hi - 19] = mm(operand(l), "W", l).reshape(hi - lo, LP, 128)

    for c in copies:
        c.wait()
    copies.clear()

    rl_hi, rl_lo = split(m_l[...])
    rr_hi, rr_lo = split(m_r[...])
    rhi = jnp.concatenate([rl_hi, rr_hi], axis=1).astype(F32)
    rlo = jnp.concatenate([rl_lo, rr_lo], axis=1).astype(F32)
    lane2 = lax.broadcasted_iota(jnp.int32, (1, 256), 1)

    def received(j):
        (al, nl), (ar, nr) = LEFT[j], RIGHT[j]
        keep = ((lane2 >= al) & (lane2 < al + len(nl))) | ((lane2 >= 128 + ar) & (lane2 < 128 + ar + len(nr)))
        keep = keep.astype(F32)
        return jnp.concatenate([(rhi * keep).astype(BF), (rlo * keep).astype(BF)], axis=0)

    def vmul(ks, t):
        hi, lo = split(t)
        both = jnp.concatenate([hi, lo], axis=1)
        outs = []
        for k in ks:
            p = dot(vst[k][:, 0:LP], both)
            outs.append(p[0:LP, 0:128] + p[0:LP, 128:256] + p[LP:2 * LP, 0:128])
        return outs

    low = lane < 64
    z1 = const(("Z", 1, "hi"))
    for j in range(0, 19):
        if j < 10:
            p = dot(received(j), z1)
            t = o1[j] + p[0:LP] + p[LP:2 * LP]
            bd[42 + j] = vmul((1,), t[:, 0:128])[0]
            bd[j] = vmul((2,), t[:, 128:256])[0]
        else:
            p = dot(received(j), z1[:, 128:256])
            bd[j] = vmul((0,), o1[j, :, 128:256] + p[0:LP] + p[LP:2 * LP])[0]
    for l in (2, 3, 4):
        z = const(("Z", l, "hi"))
        for j in range(*groups[l]):
            p = dot(received(j), z)
            t = o2[j - 19] + p[0:LP] + p[LP:2 * LP]
            if LEVEL_OF[j][1] == "D":
                a, b = vmul((3 * l - 2, 3 * l - 1), t)
                bd[j] = jnp.where(low, a, b)
            else:
                bd[j] = jnp.where(low, 0.0, vmul((3 * l - 3,), t)[0])

    uhi, ulo = split(jnp.concatenate([s_o[...], m_l[...], m_r[...], m_o[...]], axis=1))
    c = dot(uhi, qm[0]) + dot(ulo, qm[0]) + dot(uhi, qm[1])
    for rho in range(2):
        v = vmul((BANDS - 1,), c[:, rho * 128:(rho + 1) * 128])[0]
        sm[rho] = v * mw if rho else v

    for l in (4, 3, 2):
        m, d, b = MLAT[l], DROW[l], SROW[l]
        for i in range(m + 1):
            s = bd[b + i] + sm[i]
            sm[i] = s - 0.25 * (bd[d + i] + bd[d + i + 1])
        for i in range(2 * m, -1, -1):
            if i % 2:
                h = i // 2
                tmsg[i, :, 0:128] = bd[d + 1 + h] + 0.5 * (sm[h] + sm[h + 1])
            else:
                tmsg[i, :, 0:128] = sm[i // 2]
        n = 2 * m + 1
        out = mm(tmsg[0:n, :, 0:128].reshape(n * LP, 128), "T", l).reshape(n, LP, 128)
        sm[0:n] = out
        sm[2 * m] = mw * sm[2 * m]
    for i in range(9):
        tmsg[2 * i, :, 0:128] = sm[i] - 0.25 * (bd[42 + i] + bd[43 + i])
        tmsg[2 * i, :, 128:256] = bd[10 + i] - 0.25 * (bd[i] + bd[i + 1])
    for i in range(8):
        tmsg[2 * i + 1, :, 0:128] = bd[43 + i] + 0.5 * (tmsg[2 * i, :, 0:128] + tmsg[2 * i + 2, :, 0:128])
        tmsg[2 * i + 1, :, 128:256] = bd[1 + i] + 0.5 * (tmsg[2 * i, :, 128:256] + tmsg[2 * i + 2, :, 128:256])
    for q in range(4):
        y = mm(tmsg[4 * q:4 * q + 4].reshape(4 * LP, 256), "T", 1).reshape(4, LP, 128)
        ys[4 * q:4 * q + 4] = y
        go(remote(ys.at[pl.ds(4 * q, 4)], prev.at[pl.ds(4 * q, 4)], at_tm(1)))
    for r in range(ROWS):
        inc[pl.ds(r, LEV, stride=ROWS), :] = ys[r, 0:LEV, :]
    first = (tm > 0).astype(F32)
    for q in range(4):
        copies[q].wait()
        for r in range(4 * q, 4 * q + 4):
            jump[pl.ds(r, LEV, stride=ROWS), :] = ys[r, 0:LEV, :] - first * prev[r, 0:LEV, :]


def body(forcing, vertical, lat_factor, lon_factor):
    x = forcing.reshape(LEV * ROWS, COLS)
    tile = (LP, 128)
    vm = pl.BlockSpec(memory_space=pltpu.VMEM)
    S = pltpu.VMEM
    scratch = [
        S((ROWS,) + tile, F32), S((39,) + tile, F32), S((19,) + tile, F32), S((23, LP, 256), F32),
        S((3,) + tile, F32), S((2,) + tile, F32), S((2,) + tile, F32), S((LP // 2, 128), F32),
        S((2,) + tile, F32), S(tile, F32), S(tile, F32), S(tile, F32), S(tile, F32), S(tile, F32),
        S((8, LP // 2, 128), F32),
        S((BANDS, 2 * LP, 256), BF), S((LP, 256), F32), S((16, 1024), F32), S((2, 512, 256), BF),
        S((19, LP, 256), F32), S((23,) + tile, F32), S((19, LP, 256), F32),
        S(tile, F32), S(tile, F32), S(tile, F32), S(tile, F32), S(tile, F32), S(tile, F32),
        S((52,) + tile, F32), S((9,) + tile, F32), S((ROWS,) + tile, F32), S((ROWS,) + tile, F32),
        pltpu.SemaphoreType.DMA((24,)), pltpu.SemaphoreType.DMA((24,)),
    ]
    out = jax.ShapeDtypeStruct((LEV * ROWS, COLS), F32)
    inc, jump = pl.pallas_call(
        kernel,
        out_shape=(out, out),
        in_specs=[vm] * 7,
        out_specs=(vm, vm),
        scratch_shapes=scratch,
        compiler_params=pltpu.CompilerParams(
            collective_id=0, has_side_effects=True, vmem_limit_bytes=56 * 1024 * 1024),
    )(x, vertical, lat_factor, lon_factor, jnp.asarray(CB), jnp.asarray(EXT), jnp.asarray(EXPAND))
    shape = (1, LEV, ROWS, COLS)
    return inc.reshape(shape), jump.reshape(shape)


def solution(mesh):
    placed = (P("tm", None, "lat", "lon"), P(), P(), P())
    return jax.shard_map(
        body,
        mesh=mesh,
        in_specs=placed,
        out_specs=(P("tm", None, "lat", "lon"), P("tm", None, "lat", "lon")),
        check_vma=False,
    )
```

```python
import numpy as np
import jax
import jax.numpy as jnp
import ml_dtypes
from jax import lax
from jax.experimental import pallas as pl
from jax.experimental.pallas import tpu as pltpu
from jax.sharding import PartitionSpec as P

LEV, LP = 137, 144
ROWS, COLS = 16, 128
BANDS = 13
NLAT_D, NLON_D = 8, 4
MESH = pl.DeviceIdType.MESH
HIGH = lax.Precision.HIGHEST
F32, BF = jnp.float32, jnp.bfloat16

MLAT = {1: 8, 2: 4, 3: 2, 4: 1}
MLON = {1: 64, 2: 32, 3: 16, 4: 8}
DROW = {1: 0, 2: 19, 3: 30, 4: 37}
SROW = {1: 10, 2: 25, 3: 34, 4: 40}
NROWS = 42
PACK = {2: (0, 1, -1, 64), 3: (66, 2, -1, 33), 4: (101, 3, -1, 17)}
FOLD, WIDE = 16, 9
FOLD_LANES = LP // FOLD * WIDE
LEVEL_OF = {}
for _l in (1, 2, 3, 4):
    for _i in range(MLAT[_l] + 2):
        LEVEL_OF[DROW[_l] + _i] = (_l, "D", _i - 1)
    for _i in range(MLAT[_l] + 1):
        LEVEL_OF[SROW[_l] + _i] = (_l, "S", _i)


def lift(seq, size):
    lo, hi = min(seq), max(seq)
    zero = np.zeros(size)
    get = lambda table, i: table.get(i, zero)
    d, s = {}, {}
    for i in range(lo // 2 - 2, hi // 2 + 3):
        d[i] = get(seq, 2 * i + 1) - 0.5 * (get(seq, 2 * i) + get(seq, 2 * i + 2))
    for i in range(lo // 2 - 2, hi // 2 + 3):
        s[i] = get(seq, 2 * i) + 0.25 * (get(d, i - 1) + get(d, i))
    keep = lambda table: {i: v for i, v in table.items() if np.any(v)}
    return keep(s), keep(d)


def message_lanes():
    left, right = {}, {}
    nl = nr = 0
    for j in range(NROWS):
        l, kind, _ = LEVEL_OF[j]
        ql = ["dm1"] if l == 1 else (["sm", "dm1", "dm"] if kind == "D" else ["dm1", "dm"])
        qr = ["d-1", "d0"] if (l == 1 or kind == "S") else ["s0", "d-1", "d0"]
        left[j], right[j] = (nl, ql), (nr, qr)
        nl, nr = nl + len(ql), nr + len(qr)
    assert nl <= 128 and nr <= 128
    return left, right


LEFT, RIGHT = message_lanes()


def lon_tables():
    raw = {i: np.eye(256)[i] for i in range(COLS)}
    smooth, detail = {0: raw}, {}
    for l in range(1, 5):
        smooth[l], detail[l] = lift(smooth[l - 1], 256)
    ext_s = {}
    for l in (2, 3, 4):
        at, depth, lo, hi = PACK[l]
        seq = {i: np.eye(256)[128 + at + i - lo] for i in range(lo, hi + 1)}
        for k in range(l, 5):
            s, d = lift(seq, 256)
            seq = s
            ext_s[l, k] = (s, d)
    zero = np.zeros(256)
    full_s, full_d = {}, {}
    for k in range(1, 5):
        s, d = dict(smooth[k]), dict(detail[k])
        for l in range(2, k + 1):
            for table, more in ((s, ext_s[l, k][0]), (d, ext_s[l, k][1])):
                for i, v in more.items():
                    table[i] = table.get(i, zero) + v
        full_s[k], full_d[k] = s, d
    return smooth, full_s, full_d


def constants():
    smooth, fs, fd = lon_tables()
    zero = np.zeros(256)
    out = {}
    for l in (1, 2, 3, 4):
        m = MLON[l]
        w = np.zeros((256, 256))
        off = 128 if l == 1 else 64
        for i in range(0, m + 1):
            w[:, i] = fs[l].get(i, zero)
        for i in range(-1, m + 1):
            w[:, off + i + 1] = fd[l].get(i, zero)
        out["W", l] = w if l == 1 else w[:, :128]
        g = np.zeros((256, 256))
        pick = {"sm": fs[l].get(m, zero), "dm1": fd[l].get(m - 1, zero), "dm": fd[l].get(m, zero),
                "s0": fs[l].get(0, zero), "d-1": fd[l].get(-1, zero), "d0": fd[l].get(0, zero)}
        z = np.zeros((256, 256))
        for j in range(NROWS):
            if LEVEL_OF[j][0] != l:
                continue
            smooth_too = LEVEL_OF[j][1] == "D"
            for base, (at, names) in ((0, LEFT[j]), (128, RIGHT[j])):
                for q, name in enumerate(names):
                    lane = base + at + q
                    g[:, lane] = pick[name]
                    row = z[lane]
                    if base == 0:
                        if name == "dm1":
                            row[off + 0] += 1.0
                            if l == 1 and smooth_too:
                                row[0] += 0.25
                        if name == "dm":
                            row[off + 1] += 1.0
                            if smooth_too:
                                row[1] += 0.25
                        if name == "sm":
                            row[0] += 1.0
                    else:
                        if name == "s0":
                            row[m] += 1.0
                        if name == "d-1":
                            row[off + m] += 1.0
                            if smooth_too:
                                row[m - 1] += 0.25
                                if l == 1:
                                    row[m] += -1.75
                        if name == "d0":
                            row[off + m + 1] += 1.0
                            if l == 1 and smooth_too:
                                row[m] += 0.25
        out["G", l] = g
        out["Z", l] = z if l == 1 else z[:, :128]
        n_in = 256 if l == 1 else 128
        eye = np.eye(n_in)
        s = {i: eye[i] for i in range(0, m + 1)}
        d = {i: eye[off + i + 1] for i in range(-1, m + 1)}
        e = {i: s[i] - 0.25 * (d[i - 1] + d[i]) for i in range(0, m + 1)}
        t = np.zeros((n_in, 128))
        for i in range(0, m + 1):
            if 2 * i < 128:
                t[:, 2 * i] = e[i]
            if i < m:
                t[:, 2 * i + 1] = d[i] + 0.5 * (e[i] + e[i + 1])
        out["T", l] = t
    for l in (2, 3, 4):
        at, depth, lo, hi = PACK[l]
        sm = np.zeros((128, 128))
        for i in range(lo, hi + 1):
            sm[:, at + i - lo] = smooth[depth][i][:128]
        out["Sm", l] = sm
    c4 = np.zeros((256, 128))
    for c in range(11):
        c4[:, c] = fs[4].get(c - 1, zero)
    out["C4", 0] = c4
    return out


CONST = constants()


def pack_constants():
    tiles, where = [], {}

    def put(key, a):
        k, n = a.shape
        where[key] = (sum(t.shape[0] for t in tiles), k, n)
        if n < 256:
            a = np.concatenate([a, np.zeros((k, 256 - n), a.dtype)], 1)
        tiles.append(a)

    for key, a in CONST.items():
        if key == ("W", 1) or key == ("G", 1):
            a = a[:128]
        hi = a.astype(ml_dtypes.bfloat16)
        lo = (a - hi.astype(np.float64)).astype(ml_dtypes.bfloat16)
        put(key + ("hi",), hi)
        if np.any(lo.astype(np.float64)):
            put(key + ("lo",), lo)
    return np.concatenate(tiles, 0), where


CB, CWHERE = pack_constants()


def ext_coefficients():
    syms = {("U", 2): 0, ("U", 3): 1, ("U", 4): 2, ("W", 2): 3, ("W", 3): 4, ("W", 4): 5}
    unit = lambda key: np.eye(6)[syms[key]]
    zero = np.zeros(6)
    s = {i: zero for i in range(9)}
    table = {}
    for l in (2, 3, 4):
        m = MLAT[l]
        d = {-1: unit(("U", l)), m: unit(("W", l))}
        for i in range(m):
            d[i] = s[2 * i + 1] - 0.5 * (s[2 * i] + s[2 * i + 2])
        s = {i: s[2 * i] + 0.25 * (d[i - 1] + d[i]) for i in range(m + 1)}
        for i in range(-1, m + 1):
            table[DROW[l] + i + 1] = d[i]
        for i in range(m + 1):
            table[SROW[l] + i] = s[i]
    out = np.zeros((48, 128), np.float32)
    for j, v in table.items():
        for l in (2, 3, 4):
            at, _, lo, hi = PACK[l]
            out[j - 19, at:at + hi - lo + 1] = v[l - 2]
            out[24 + j - 19, at:at + hi - lo + 1] = v[3 + l - 2]
    return out


EXT = ext_coefficients()


def split(a):
    hi = a.astype(BF)
    return hi, (a - hi.astype(F32)).astype(BF)


def dot(a, b):
    return jnp.dot(a, b, preferred_element_type=F32)


def kernel(x_hbm, vert_hbm, latf_hbm, lonf_hbm, cb_hbm, ext_hbm, inc_hbm, jump_hbm,
           x, vert, latf, lonf, cb, ext_c, inc, jump,
           xs, so, rw, lx, up, dn, p2, r_w, r_u, r_pw, r_pu, r_p2u, r_p2w,
           vst, vtmp, pm, o1, o2, tmsg, s_l, s_r, m_l, m_r, sf, mf, cbuf,
           bd, sm, ys, prev, send, recv, load):
    tm, lat, lon = lax.axis_index("tm"), lax.axis_index("lat"), lax.axis_index("lon")
    mu = (lat > 0).astype(F32)
    mw = (lat < NLAT_D - 1).astype(F32)
    mu2 = (lat > 1).astype(F32)
    mw2 = (lat < NLAT_D - 2).astype(F32)

    def at_lat(k):
        return (tm, lax.rem(lat + k + NLAT_D, NLAT_D), lon)

    def at_lon(k):
        return (tm, lat, lax.rem(lon + k + NLON_D, NLON_D))

    def at_tm(k):
        return (lax.rem(tm + k + 4, 4), lat, lon)

    partners = [at_lat(k) for k in range(1, 8)] + [at_lon(k) for k in range(1, 4)] + [at_tm(1), at_tm(-1)]
    barrier = pltpu.get_barrier_semaphore()
    for p in partners:
        pl.semaphore_signal(barrier, inc=1, device_id=p, device_id_type=MESH)

    loads = {}
    for n, (name, src, dst) in enumerate((("x", x_hbm, x), ("cb", cb_hbm, cb), ("ext", ext_hbm, ext_c),
                                          ("lonf", lonf_hbm, lonf), ("latf", latf_hbm, latf),
                                          ("vert", vert_hbm, vert))):
        loads[name] = pltpu.make_async_copy(src, dst, load.at[n])
        loads[name].start()

    def const(key):
        at, k, n = CWHERE[key]
        return cb[at:at + k, 0:n]

    def mm(a, name, l):
        hi, lo = split(a)
        w = const((name, l, "hi"))
        out = dot(hi, w) + dot(lo, w)
        if (name, l, "lo") in CWHERE:
            out = out + dot(hi, const((name, l, "lo")))
        return out

    loads["x"].wait()
    for r in range(ROWS):
        xs[r, 136:144, :] = jnp.zeros((8, COLS), F32)
        xs[r, 0:LEV, :] = x[pl.ds(r, LEV, stride=ROWS), :]

    for i in range(7):
        rw[1 + i] = xs[2 * i + 1] - 0.5 * (xs[2 * i] + xs[2 * i + 2])
    dn[0] = xs[15] - 0.5 * xs[14]
    up[0] = xs[0]
    up[1] = rw[1]

    sems = iter(range(64))

    def remote(src, dst, dev, slot=None):
        k = next(sems)
        return pltpu.make_async_remote_copy(
            src_ref=src, dst_ref=dst, send_sem=send.at[k],
            recv_sem=recv.at[k], device_id=dev, device_id_type=MESH)

    copies = []

    def go(c):
        c.start()
        copies.append(c)

    so[0] = (-0.125 * mu) * xs[0]
    so[1] = 0.875 * xs[0] + 0.25 * rw[1]
    for i in range(1, 7):
        so[1 + i] = xs[2 * i] + 0.25 * (rw[i] + rw[1 + i])
    so[8] = xs[14] + 0.25 * (rw[7] + dn[0])
    so[9] = (0.25 * mw) * dn[0]
    sbase = {1: 0, 2: 10, 3: 17, 4: 22}
    dbase = {2: 26, 3: 32, 4: 36}
    for l in (2, 3, 4):
        m, a, b, d = MLAT[l], sbase[l - 1], sbase[l], dbase[l]
        S = lambda i: so[a + 1 + i]
        so[d] = S(-1) - 0.5 * S(0)
        for i in range(m):
            so[d + 1 + i] = S(2 * i + 1) - 0.5 * (S(2 * i) + S(2 * i + 2))
        so[d + 1 + m] = (-0.5 * S(2 * m)) if l == 2 else S(2 * m + 1) - 0.5 * S(2 * m)
        so[b] = (0.25 * mu) * so[d]
        for i in range(m):
            so[b + 1 + i] = S(2 * i) + 0.25 * (so[d + i] + so[d + 1 + i])
        so[b + 1 + m] = mw * (S(2 * m) + 0.25 * (so[d + m] + so[d + 1 + m]))
        so[b + 2 + m] = (0.25 * mw) * so[d + 1 + m]
    loads["cb"].wait()
    d4 = mm(so[37], "Sm", 4)
    up[2] = mm(so[27], "Sm", 2) + mm(so[33], "Sm", 3) + d4
    dn[1] = mm(so[30], "Sm", 2) + mm(so[34], "Sm", 3) + d4
    p2[0] = mm(so[38], "Sm", 4)
    p2[1] = mm(so[36], "Sm", 4)
    pl.semaphore_wait(barrier, len(partners))
    go(remote(up.at[pl.ds(0, 2)], r_w, at_lat(-1)))
    go(remote(dn.at[0], r_u, at_lat(1)))
    go(remote(up.at[2], r_pw, at_lat(-1)))
    go(remote(dn.at[1], r_pu, at_lat(1)))
    go(remote(p2.at[0], r_p2u, at_lat(2)))
    go(remote(p2.at[1], r_p2w, at_lat(-2)))
    lane = lax.broadcasted_iota(jnp.int32, (1, 128), 1)

    for name in ("ext", "lonf", "latf", "vert"):
        loads[name].wait()
    vtmp[...] = jnp.zeros((LP, 256), F32)
    for k in range(BANDS):
        vtmp[0:LEV, 0:LEV] = vert[k]
        hi, lo = split(vtmp[...])
        vst[k, 0:LP, :] = hi
        vst[k, LP:2 * LP, :] = lo
    rowi = lax.broadcasted_iota(jnp.int32, (128, 32), 0)
    coli = lax.broadcasted_iota(jnp.int32, (128, 32), 1)
    mine = ((rowi < 11) & (coli == lax.rem(8 * lon + 31 + rowi, 32))).astype(F32)
    for k in range(NLON_D):
        theirs = (rowi < FOLD_LANES) & (coli == lax.rem(8 * (lon + k) + lax.rem(rowi, WIDE), 32))
        part = jnp.dot(theirs.astype(F32), lonf[...], precision=HIGH, preferred_element_type=F32)
        part = lax.dot_general(mine, part, (((1,), (1,)), ((), ())), precision=HIGH,
                               preferred_element_type=F32)
        c4 = const(("C4", 0, "hi")).astype(F32) + const(("C4", 0, "lo")).astype(F32)
        hi, lo = split(jnp.dot(c4, part, precision=HIGH, preferred_element_type=F32))
        pm[0, :, k * 128:(k + 1) * 128] = hi
        pm[1, :, k * 128:(k + 1) * 128] = lo

    for c in copies:
        c.wait()
    copies.clear()

    x16 = lambda: mw * r_w[0]
    rw[0] = mu * r_u[...] - 0.5 * xs[0]
    rw[8] = dn[0] - 0.5 * x16()
    rw[9] = mw * r_w[1]
    for i in range(8):
        rw[10 + i] = xs[2 * i] + 0.25 * (rw[i] + rw[i + 1])
    rw[18] = x16() + (0.25 * mw) * (rw[8] + rw[9])
    raw = lambda j: rw[j] if j < 19 else lx[j - 19, :, 0:128]
    for l in (2, 3, 4):
        m, a, d, b = MLAT[l], SROW[l - 1], DROW[l], SROW[l]
        lx[d - 19, :, 0:128] = so[dbase[l]]
        lx[d + m + 1 - 19, :, 0:128] = so[dbase[l] + m + 1]
        for i in range(m):
            lx[d + 1 + i - 19, :, 0:128] = raw(a + 2 * i + 1) - 0.5 * (raw(a + 2 * i) + raw(a + 2 * i + 2))
        for i in range(m + 1):
            v = raw(a + 2 * i) + 0.25 * (raw(d + i) + raw(d + i + 1))
            lx[b + i - 19, :, 0:128] = mw * v if i == m else v
    r_pu[...] = mu * r_pu[...] + mu2 * r_p2u[...]
    r_pw[...] = mw * r_pw[...] + mw2 * r_p2w[...]
    for j in range(19, NROWS):
        cu, cw = ext_c[j - 19:j - 18, :], ext_c[24 + j - 19:24 + j - 18, :]
        l, kind, i = LEVEL_OF[j]
        if kind == "S" and i == MLAT[l]:
            cu, cw = cu * mw, cw * mw
        lx[j - 19, :, 128:256] = r_pu[...] * cu + r_pw[...] * cw
    rw[0] = mu * rw[0]
    for l in (2, 3, 4):
        lx[DROW[l] - 19] = mu * lx[DROW[l] - 19]

    hi, lo = split(lx[SROW[4] - 19])
    fold = dot(hi, pm[0]) + dot(lo, pm[0]) + dot(hi, pm[1])
    for k in range(NLON_D):
        acc = jnp.zeros((FOLD, 128), F32)
        for g in range(LP // FOLD):
            acc = jnp.where((lane >= g * WIDE) & (lane < (g + 1) * WIDE),
                            fold[g * FOLD:(g + 1) * FOLD, k * 128:(k + 1) * 128], acc)
        sf[k] = acc
    for k in range(1, NLON_D):
        go(remote(sf.at[k], mf.at[k], at_lon(k)))
    coarse = copies[:]
    copies.clear()

    groups = {1: (0, 19), 2: (19, 30), 3: (30, 37), 4: (37, 42)}

    def operand(l):
        lo, hi = groups[l]
        if l == 1:
            return rw[...].reshape(19 * LP, 128)
        return lx[lo - 19:hi - 19].reshape((hi - lo) * LP, 256)

    s_l[...] = jnp.zeros((LP, 128), F32)
    s_r[...] = jnp.zeros((LP, 128), F32)
    for l in (1, 2, 3, 4):
        lo, hi = groups[l]
        tmsg[0:hi - lo] = mm(operand(l), "G", l).reshape(hi - lo, LP, 256)
        for dst, table, base in ((s_l, LEFT, 0), (s_r, RIGHT, 128)):
            v = dst[...]
            for j in range(lo, hi):
                at, names = table[j]
                v = jnp.where((lane >= at) & (lane < at + len(names)), tmsg[j - lo, :, base:base + 128], v)
            dst[...] = v
    go(remote(s_l, m_l, at_lon(1)))
    go(remote(s_r, m_r, at_lon(-1)))

    for c in coarse:
        c.wait()
    row = sf[0] + mf[1] + mf[2] + mf[3]
    sf[0] = row
    cbuf[lat] = row
    round2 = copies[:]
    copies.clear()
    for k in range(1, NLAT_D):
        go(remote(sf.at[0], cbuf.at[lat], at_lat(k)))
    coarse = copies[:]
    copies.clear()

    o1[...] = mm(operand(1), "W", 1).reshape(19, LP, 256)
    for l in (2, 3, 4):
        lo, hi = groups[l]
        o2[lo - 19:hi - 19] = mm(operand(l), "W", l).reshape(hi - lo, LP, 128)

    for c in round2:
        c.wait()

    rl_hi, rl_lo = split(m_l[...])
    rr_hi, rr_lo = split(m_r[...])
    rhi = jnp.concatenate([rl_hi, rr_hi], axis=1).astype(F32)
    rlo = jnp.concatenate([rl_lo, rr_lo], axis=1).astype(F32)
    lane2 = lax.broadcasted_iota(jnp.int32, (1, 256), 1)

    def received(j):
        (al, nl), (ar, nr) = LEFT[j], RIGHT[j]
        keep = ((lane2 >= al) & (lane2 < al + len(nl))) | ((lane2 >= 128 + ar) & (lane2 < 128 + ar + len(nr)))
        keep = keep.astype(F32)
        return jnp.concatenate([(rhi * keep).astype(BF), (rlo * keep).astype(BF)], axis=0)

    def vmul(ks, t):
        hi, lo = split(t)
        both = jnp.concatenate([hi, lo], axis=1)
        outs = []
        for k in ks:
            p = dot(vst[k][:, 0:LP], both)
            outs.append(p[0:LP, 0:128] + p[0:LP, 128:256] + p[LP:2 * LP, 0:128])
        return outs

    low = lane < 64
    z1 = const(("Z", 1, "hi"))
    for j in range(0, 19):
        if j < 10:
            p = dot(received(j), z1)
            t = o1[j] + p[0:LP] + p[LP:2 * LP]
            bd[42 + j] = vmul((1,), t[:, 0:128])[0]
            bd[j] = vmul((2,), t[:, 128:256])[0]
        else:
            p = dot(received(j), z1[:, 128:256])
            bd[j] = vmul((0,), o1[j, :, 128:256] + p[0:LP] + p[LP:2 * LP])[0]
    for l in (2, 3, 4):
        z = const(("Z", l, "hi"))
        for j in range(*groups[l]):
            p = dot(received(j), z)
            t = o2[j - 19] + p[0:LP] + p[LP:2 * LP]
            if LEVEL_OF[j][1] == "D":
                a, b = vmul((3 * l - 2, 3 * l - 1), t)
                bd[j] = jnp.where(low, a, b)
            else:
                bd[j] = jnp.where(low, 0.0, vmul((3 * l - 3,), t)[0])

    for c in coarse:
        c.wait()
    for rho in range(2):
        w = latf[pl.ds(jnp.minimum(lat + rho, NLAT_D - 1), 1), :]
        t = sum(cbuf[a] * w[:, a:a + 1] for a in range(NLAT_D))
        parts = [t if g == 0 else pltpu.roll(t, 128 - WIDE * g, 1) for g in range(LP // FOLD)]
        c = jnp.where(lane < WIDE, jnp.concatenate(parts, axis=0), 0.0)
        v = vmul((BANDS - 1,), c)[0]
        sm[rho] = v * mw if rho else v

    for l in (4, 3, 2):
        m, d, b = MLAT[l], DROW[l], SROW[l]
        for i in range(m + 1):
            s = bd[b + i] + sm[i]
            sm[i] = s - 0.25 * (bd[d + i] + bd[d + i + 1])
        for i in range(2 * m, -1, -1):
            if i % 2:
                h = i // 2
                tmsg[i, :, 0:128] = bd[d + 1 + h] + 0.5 * (sm[h] + sm[h + 1])
            else:
                tmsg[i, :, 0:128] = sm[i // 2]
        n = 2 * m + 1
        out = mm(tmsg[0:n, :, 0:128].reshape(n * LP, 128), "T", l).reshape(n, LP, 128)
        sm[0:n] = out
        sm[2 * m] = mw * sm[2 * m]
    for i in range(9):
        tmsg[2 * i, :, 0:128] = sm[i] - 0.25 * (bd[42 + i] + bd[43 + i])
        tmsg[2 * i, :, 128:256] = bd[10 + i] - 0.25 * (bd[i] + bd[i + 1])
    for i in range(8):
        tmsg[2 * i + 1, :, 0:128] = bd[43 + i] + 0.5 * (tmsg[2 * i, :, 0:128] + tmsg[2 * i + 2, :, 0:128])
        tmsg[2 * i + 1, :, 128:256] = bd[1 + i] + 0.5 * (tmsg[2 * i, :, 128:256] + tmsg[2 * i + 2, :, 128:256])
    for q in range(4):
        y = mm(tmsg[4 * q:4 * q + 4].reshape(4 * LP, 256), "T", 1).reshape(4, LP, 128)
        ys[4 * q:4 * q + 4] = y
        go(remote(ys.at[pl.ds(4 * q, 4)], prev.at[pl.ds(4 * q, 4)], at_tm(1)))
    for r in range(ROWS):
        inc[pl.ds(r, LEV, stride=ROWS), :] = ys[r, 0:LEV, :]
    out = pltpu.make_async_copy(inc, inc_hbm, load.at[6])
    out.start()
    first = (tm > 0).astype(F32)
    for q in range(4):
        copies[q].wait()
        for r in range(4 * q, 4 * q + 4):
            jump[pl.ds(r, LEV, stride=ROWS), :] = ys[r, 0:LEV, :] - first * prev[r, 0:LEV, :]
    out2 = pltpu.make_async_copy(jump, jump_hbm, load.at[7])
    out2.start()
    out.wait()
    out2.wait()


def body(forcing, vertical, lat_factor, lon_factor):
    x = forcing.reshape(LEV * ROWS, COLS)
    tile = (LP, 128)
    anywhere = pl.BlockSpec(memory_space=pl.ANY)
    S = pltpu.VMEM
    flat = (LEV * ROWS, COLS)
    scratch = [
        S(flat, F32), S((BANDS, LEV, LEV), F32), S((8, 8), F32), S((32, 32), F32), S(CB.shape, BF), S(EXT.shape, F32),
        S(flat, F32), S(flat, F32),
        S((ROWS,) + tile, F32), S((39,) + tile, F32), S((19,) + tile, F32), S((23, LP, 256), F32),
        S((3,) + tile, F32), S((2,) + tile, F32), S((2,) + tile, F32),
        S((2,) + tile, F32), S(tile, F32), S(tile, F32), S(tile, F32), S(tile, F32), S(tile, F32),
        S((BANDS, 2 * LP, 256), BF), S((LP, 256), F32), S((2, 256, 512), BF),
        S((19, LP, 256), F32), S((23,) + tile, F32), S((19, LP, 256), F32),
        S(tile, F32), S(tile, F32), S(tile, F32), S(tile, F32),
        S((4, FOLD, 128), F32), S((4, FOLD, 128), F32), S((8, FOLD, 128), F32),
        S((52,) + tile, F32), S((9,) + tile, F32), S((ROWS,) + tile, F32), S((ROWS,) + tile, F32),
        pltpu.SemaphoreType.DMA((24,)), pltpu.SemaphoreType.DMA((24,)), pltpu.SemaphoreType.DMA((8,)),
    ]
    out = jax.ShapeDtypeStruct((LEV * ROWS, COLS), F32)
    inc, jump = pl.pallas_call(
        kernel,
        out_shape=(out, out),
        in_specs=[anywhere] * 6,
        out_specs=(anywhere, anywhere),
        scratch_shapes=scratch,
        compiler_params=pltpu.CompilerParams(
            collective_id=0, has_side_effects=True, vmem_limit_bytes=56 * 1024 * 1024),
    )(x, vertical, lat_factor, lon_factor, jnp.asarray(CB), jnp.asarray(EXT))
    shape = (1, LEV, ROWS, COLS)
    return inc.reshape(shape), jump.reshape(shape)


def solution(mesh):
    placed = (P("tm", None, "lat", "lon"), P(), P(), P())
    return jax.shard_map(
        body,
        mesh=mesh,
        in_specs=placed,
        out_specs=(P("tm", None, "lat", "lon"), P("tm", None, "lat", "lon")),
        check_vma=False,
    )
```

```python
import numpy as np
import jax
import jax.numpy as jnp
import ml_dtypes
from jax import lax
from jax.experimental import pallas as pl
from jax.experimental.pallas import tpu as pltpu
from jax.sharding import PartitionSpec as P

LEV, LP = 137, 144
ROWS, COLS = 16, 128
BANDS = 13
NLAT_D, NLON_D = 8, 4
MESH = pl.DeviceIdType.MESH
HIGH = lax.Precision.HIGHEST
F32, BF = jnp.float32, jnp.bfloat16

MLAT = {1: 8, 2: 4, 3: 2, 4: 1}
MLON = {1: 64, 2: 32, 3: 16, 4: 8}
DROW = {1: 0, 2: 19, 3: 30, 4: 37}
SROW = {1: 10, 2: 25, 3: 34, 4: 40}
NROWS = 42
PACK = {2: (0, 1, -1, 64), 3: (66, 2, -1, 33), 4: (101, 3, -1, 17)}
FOLD, WIDE = 16, 9
FOLD_LANES = LP // FOLD * WIDE
LEVEL_OF = {}
for _l in (1, 2, 3, 4):
    for _i in range(MLAT[_l] + 2):
        LEVEL_OF[DROW[_l] + _i] = (_l, "D", _i - 1)
    for _i in range(MLAT[_l] + 1):
        LEVEL_OF[SROW[_l] + _i] = (_l, "S", _i)


def lift(seq, size):
    lo, hi = min(seq), max(seq)
    zero = np.zeros(size)
    get = lambda table, i: table.get(i, zero)
    d, s = {}, {}
    for i in range(lo // 2 - 2, hi // 2 + 3):
        d[i] = get(seq, 2 * i + 1) - 0.5 * (get(seq, 2 * i) + get(seq, 2 * i + 2))
    for i in range(lo // 2 - 2, hi // 2 + 3):
        s[i] = get(seq, 2 * i) + 0.25 * (get(d, i - 1) + get(d, i))
    keep = lambda table: {i: v for i, v in table.items() if np.any(v)}
    return keep(s), keep(d)


def message_lanes():
    left, right = {}, {}
    nl = nr = 0
    for j in range(NROWS):
        l, kind, _ = LEVEL_OF[j]
        ql = ["dm1"] if l == 1 else (["sm", "dm1", "dm"] if kind == "D" else ["dm1", "dm"])
        qr = ["d-1", "d0"] if (l == 1 or kind == "S") else ["s0", "d-1", "d0"]
        left[j], right[j] = (nl, ql), (nr, qr)
        nl, nr = nl + len(ql), nr + len(qr)
    assert nl <= 128 and nr <= 128
    return left, right


LEFT, RIGHT = message_lanes()


def lon_tables():
    raw = {i: np.eye(256)[i] for i in range(COLS)}
    smooth, detail = {0: raw}, {}
    for l in range(1, 5):
        smooth[l], detail[l] = lift(smooth[l - 1], 256)
    ext_s = {}
    for l in (2, 3, 4):
        at, depth, lo, hi = PACK[l]
        seq = {i: np.eye(256)[128 + at + i - lo] for i in range(lo, hi + 1)}
        for k in range(l, 5):
            s, d = lift(seq, 256)
            seq = s
            ext_s[l, k] = (s, d)
    zero = np.zeros(256)
    full_s, full_d = {}, {}
    for k in range(1, 5):
        s, d = dict(smooth[k]), dict(detail[k])
        for l in range(2, k + 1):
            for table, more in ((s, ext_s[l, k][0]), (d, ext_s[l, k][1])):
                for i, v in more.items():
                    table[i] = table.get(i, zero) + v
        full_s[k], full_d[k] = s, d
    return smooth, full_s, full_d


def constants():
    smooth, fs, fd = lon_tables()
    zero = np.zeros(256)
    out = {}
    for l in (1, 2, 3, 4):
        m = MLON[l]
        w = np.zeros((256, 256))
        off = 128 if l == 1 else 64
        for i in range(0, m + 1):
            w[:, i] = fs[l].get(i, zero)
        for i in range(-1, m + 1):
            w[:, off + i + 1] = fd[l].get(i, zero)
        out["W", l] = w if l == 1 else w[:, :128]
        g = np.zeros((256, 256))
        pick = {"sm": fs[l].get(m, zero), "dm1": fd[l].get(m - 1, zero), "dm": fd[l].get(m, zero),
                "s0": fs[l].get(0, zero), "d-1": fd[l].get(-1, zero), "d0": fd[l].get(0, zero)}
        z = np.zeros((256, 256))
        for j in range(NROWS):
            if LEVEL_OF[j][0] != l:
                continue
            smooth_too = LEVEL_OF[j][1] == "D"
            for base, (at, names) in ((0, LEFT[j]), (128, RIGHT[j])):
                for q, name in enumerate(names):
                    lane = base + at + q
                    g[:, lane] = pick[name]
                    row = z[lane]
                    if base == 0:
                        if name == "dm1":
                            row[off + 0] += 1.0
                            if l == 1 and smooth_too:
                                row[0] += 0.25
                        if name == "dm":
                            row[off + 1] += 1.0
                            if smooth_too:
                                row[1] += 0.25
                        if name == "sm":
                            row[0] += 1.0
                    else:
                        if name == "s0":
                            row[m] += 1.0
                        if name == "d-1":
                            row[off + m] += 1.0
                            if smooth_too:
                                row[m - 1] += 0.25
                                if l == 1:
                                    row[m] += -1.75
                        if name == "d0":
                            row[off + m + 1] += 1.0
                            if l == 1 and smooth_too:
                                row[m] += 0.25
        out["G", l] = g
        out["Z", l] = z if l == 1 else z[:, :128]
        n_in = 256 if l == 1 else 128
        eye = np.eye(n_in)
        s = {i: eye[i] for i in range(0, m + 1)}
        d = {i: eye[off + i + 1] for i in range(-1, m + 1)}
        e = {i: s[i] - 0.25 * (d[i - 1] + d[i]) for i in range(0, m + 1)}
        t = np.zeros((n_in, 128))
        for i in range(0, m + 1):
            if 2 * i < 128:
                t[:, 2 * i] = e[i]
            if i < m:
                t[:, 2 * i + 1] = d[i] + 0.5 * (e[i] + e[i + 1])
        out["T", l] = t
    for l in (2, 3, 4):
        at, depth, lo, hi = PACK[l]
        sm = np.zeros((128, 128))
        for i in range(lo, hi + 1):
            sm[:, at + i - lo] = smooth[depth][i][:128]
        out["Sm", l] = sm
    c4 = np.zeros((256, 128))
    for c in range(11):
        c4[:, c] = fs[4].get(c - 1, zero)
    out["C4", 0] = c4
    return out


CONST = constants()


def pack_constants():
    tiles, where = [], {}

    def put(key, a):
        k, n = a.shape
        where[key] = (sum(t.shape[0] for t in tiles), k, n)
        if n < 256:
            a = np.concatenate([a, np.zeros((k, 256 - n), a.dtype)], 1)
        tiles.append(a)

    for key, a in CONST.items():
        if key == ("W", 1) or key == ("G", 1):
            a = a[:128]
        hi = a.astype(ml_dtypes.bfloat16)
        lo = (a - hi.astype(np.float64)).astype(ml_dtypes.bfloat16)
        put(key + ("hi",), hi)
        if np.any(lo.astype(np.float64)):
            put(key + ("lo",), lo)
    return np.concatenate(tiles, 0), where


CB, CWHERE = pack_constants()


def ext_coefficients():
    syms = {("U", 2): 0, ("U", 3): 1, ("U", 4): 2, ("W", 2): 3, ("W", 3): 4, ("W", 4): 5}
    unit = lambda key: np.eye(6)[syms[key]]
    zero = np.zeros(6)
    s = {i: zero for i in range(9)}
    table = {}
    for l in (2, 3, 4):
        m = MLAT[l]
        d = {-1: unit(("U", l)), m: unit(("W", l))}
        for i in range(m):
            d[i] = s[2 * i + 1] - 0.5 * (s[2 * i] + s[2 * i + 2])
        s = {i: s[2 * i] + 0.25 * (d[i - 1] + d[i]) for i in range(m + 1)}
        for i in range(-1, m + 1):
            table[DROW[l] + i + 1] = d[i]
        for i in range(m + 1):
            table[SROW[l] + i] = s[i]
    out = np.zeros((48, 128), np.float32)
    for j, v in table.items():
        for l in (2, 3, 4):
            at, _, lo, hi = PACK[l]
            out[j - 19, at:at + hi - lo + 1] = v[l - 2]
            out[24 + j - 19, at:at + hi - lo + 1] = v[3 + l - 2]
    return out


EXT = ext_coefficients()


def split(a):
    hi = a.astype(BF)
    return hi, (a - hi.astype(F32)).astype(BF)


def dot(a, b):
    return jnp.dot(a, b, preferred_element_type=F32)


def kernel(x_hbm, vert_hbm, latf_hbm, lonf_hbm, cb_hbm, ext_hbm, inc_hbm, jump_hbm,
           x, vert, latf, lonf, cb, ext_c, inc, jump,
           xs, so, rw, lx, up, dn, p2, r_w, r_u, r_pw, r_pu, r_p2u, r_p2w,
           vst, vtmp, pm, o1, o2, tl, tmsg, s_l, s_r, m_l, m_r, sf, mf, cbuf,
           bd, sm, pk, pkp, ys, yz, prev, send, recv, load):
    tm, lat, lon = lax.axis_index("tm"), lax.axis_index("lat"), lax.axis_index("lon")
    mu = (lat > 0).astype(F32)
    mw = (lat < NLAT_D - 1).astype(F32)
    mu2 = (lat > 1).astype(F32)
    mw2 = (lat < NLAT_D - 2).astype(F32)

    def at_lat(k):
        return (tm, lax.rem(lat + k + NLAT_D, NLAT_D), lon)

    def at_lon(k):
        return (tm, lat, lax.rem(lon + k + NLON_D, NLON_D))

    def at_tm(k):
        return (lax.rem(tm + k + 4, 4), lat, lon)

    partners = [at_lat(k) for k in range(1, 8)] + [at_lon(k) for k in range(1, 4)] + [at_tm(1), at_tm(-1)]
    barrier = pltpu.get_barrier_semaphore()
    for p in partners:
        pl.semaphore_signal(barrier, inc=1, device_id=p, device_id_type=MESH)

    loads = {}
    for n, (name, src, dst) in enumerate((("x", x_hbm, x), ("cb", cb_hbm, cb), ("ext", ext_hbm, ext_c),
                                          ("lonf", lonf_hbm, lonf), ("latf", latf_hbm, latf),
                                          ("vert", vert_hbm, vert))):
        loads[name] = pltpu.make_async_copy(src, dst, load.at[n])
        loads[name].start()

    def const(key):
        at, k, n = CWHERE[key]
        return cb[at:at + k, 0:n]

    def mm(a, name, l):
        hi, lo = split(a)
        w = const((name, l, "hi"))
        out = dot(hi, w) + dot(lo, w)
        if (name, l, "lo") in CWHERE:
            out = out + dot(hi, const((name, l, "lo")))
        return out

    loads["x"].wait()
    for r in range(ROWS):
        xs[r, 136:144, :] = jnp.zeros((8, COLS), F32)
        xs[r, 0:LEV, :] = x[pl.ds(r, LEV, stride=ROWS), :]

    for i in range(7):
        rw[1 + i] = xs[2 * i + 1] - 0.5 * (xs[2 * i] + xs[2 * i + 2])
    dn[0] = xs[15] - 0.5 * xs[14]
    up[0] = xs[0]
    up[1] = rw[1]

    sems = iter(range(64))

    def remote(src, dst, dev, slot=None):
        k = next(sems)
        return pltpu.make_async_remote_copy(
            src_ref=src, dst_ref=dst, send_sem=send.at[k],
            recv_sem=recv.at[k], device_id=dev, device_id_type=MESH)

    copies = []

    def go(c):
        c.start()
        copies.append(c)

    so[0] = (-0.125 * mu) * xs[0]
    so[1] = 0.875 * xs[0] + 0.25 * rw[1]
    for i in range(1, 7):
        so[1 + i] = xs[2 * i] + 0.25 * (rw[i] + rw[1 + i])
    so[8] = xs[14] + 0.25 * (rw[7] + dn[0])
    so[9] = (0.25 * mw) * dn[0]
    sbase = {1: 0, 2: 10, 3: 17, 4: 22}
    dbase = {2: 26, 3: 32, 4: 36}
    for l in (2, 3, 4):
        m, a, b, d = MLAT[l], sbase[l - 1], sbase[l], dbase[l]
        S = lambda i: so[a + 1 + i]
        so[d] = S(-1) - 0.5 * S(0)
        for i in range(m):
            so[d + 1 + i] = S(2 * i + 1) - 0.5 * (S(2 * i) + S(2 * i + 2))
        so[d + 1 + m] = (-0.5 * S(2 * m)) if l == 2 else S(2 * m + 1) - 0.5 * S(2 * m)
        so[b] = (0.25 * mu) * so[d]
        for i in range(m):
            so[b + 1 + i] = S(2 * i) + 0.25 * (so[d + i] + so[d + 1 + i])
        so[b + 1 + m] = mw * (S(2 * m) + 0.25 * (so[d + m] + so[d + 1 + m]))
        so[b + 2 + m] = (0.25 * mw) * so[d + 1 + m]
    loads["cb"].wait()
    d4 = mm(so[37], "Sm", 4)
    up[2] = mm(so[27], "Sm", 2) + mm(so[33], "Sm", 3) + d4
    dn[1] = mm(so[30], "Sm", 2) + mm(so[34], "Sm", 3) + d4
    p2[0] = mm(so[38], "Sm", 4)
    p2[1] = mm(so[36], "Sm", 4)
    for i in range(1, 7):
        rw[10 + i] = xs[2 * i] + 0.25 * (rw[i] + rw[i + 1])

    lane = lax.broadcasted_iota(jnp.int32, (1, 128), 1)
    inner, outer = (1, 8, 11, 17), (0, 1, 8, 11, 17, 19)

    def spans(marks):
        return list(zip(marks[0::2], marks[1::2]))

    def operand(lo, hi):
        if hi <= 19:
            return rw[lo:hi].reshape((hi - lo) * LP, 128)
        return lx[lo - 19:hi - 19].reshape((hi - lo) * LP, 256)

    def message(n, groups):
        s_l[n] = jnp.zeros((LP, 128), F32)
        s_r[n] = jnp.zeros((LP, 128), F32)
        for lo, hi in groups:
            tmsg[0:hi - lo] = mm(operand(lo, hi), "G", LEVEL_OF[lo][0]).reshape(hi - lo, LP, 256)
            for dst, table, base in ((s_l, LEFT, 0), (s_r, RIGHT, 128)):
                v = dst[n]
                for j in range(lo, hi):
                    at, names = table[j]
                    v = jnp.where((lane >= at) & (lane < at + len(names)), tmsg[j - lo, :, base:base + 128], v)
                dst[n] = v

    def post(n):
        out = [remote(s_l.at[n], m_l.at[n], at_lon(1)), remote(s_r.at[n], m_r.at[n], at_lon(-1))]
        for c in out:
            c.start()
        return out

    message(0, spans(inner))
    pl.semaphore_wait(barrier, len(partners))
    bulk = [remote(up.at[pl.ds(0, 2)], r_w, at_lat(-1)), remote(dn.at[0], r_u, at_lat(1))]
    for c in bulk:
        c.start()
    lon0 = post(0)
    go(remote(up.at[2], r_pw, at_lat(-1)))
    go(remote(dn.at[1], r_pu, at_lat(1)))
    go(remote(p2.at[0], r_p2u, at_lat(2)))
    go(remote(p2.at[1], r_p2w, at_lat(-2)))
    packs = copies[:]
    copies.clear()

    for name in ("ext", "lonf", "latf", "vert"):
        loads[name].wait()
    vtmp[...] = jnp.zeros((LP, 256), F32)
    for k in range(BANDS):
        vtmp[0:LEV, 0:LEV] = vert[k]
        hi, lo = split(vtmp[...])
        vst[k, 0:LP, :] = hi
        vst[k, LP:2 * LP, :] = lo
    rowi = lax.broadcasted_iota(jnp.int32, (128, 32), 0)
    coli = lax.broadcasted_iota(jnp.int32, (128, 32), 1)
    mine = ((rowi < 11) & (coli == lax.rem(8 * lon + 31 + rowi, 32))).astype(F32)
    for k in range(NLON_D):
        theirs = (rowi < FOLD_LANES) & (coli == lax.rem(8 * (lon + k) + lax.rem(rowi, WIDE), 32))
        part = jnp.dot(theirs.astype(F32), lonf[...], precision=HIGH, preferred_element_type=F32)
        part = lax.dot_general(mine, part, (((1,), (1,)), ((), ())), precision=HIGH,
                               preferred_element_type=F32)
        c4 = const(("C4", 0, "hi")).astype(F32) + const(("C4", 0, "lo")).astype(F32)
        hi, lo = split(jnp.dot(c4, part, precision=HIGH, preferred_element_type=F32))
        pm[0, :, k * 128:(k + 1) * 128] = hi
        pm[1, :, k * 128:(k + 1) * 128] = lo

    low = lane < 64
    z1 = const(("Z", 1, "hi"))
    lane2 = lax.broadcasted_iota(jnp.int32, (1, 256), 1)

    def received(j, rhi, rlo):
        (al, nl), (ar, nr) = LEFT[j], RIGHT[j]
        keep = ((lane2 >= al) & (lane2 < al + len(nl))) | ((lane2 >= 128 + ar) & (lane2 < 128 + ar + len(nr)))
        keep = keep.astype(F32)
        return jnp.concatenate([(rhi * keep).astype(BF), (rlo * keep).astype(BF)], axis=0)

    def vmul(ks, t):
        hi, lo = split(t)
        both = jnp.concatenate([hi, lo], axis=1)
        outs = []
        for k in ks:
            p = dot(vst[k][:, 0:LP], both)
            outs.append(p[0:LP, 0:128] + p[0:LP, 128:256] + p[LP:2 * LP, 0:128])
        return outs

    def arrived(n):
        rl_hi, rl_lo = split(m_l[n])
        rr_hi, rr_lo = split(m_r[n])
        return (jnp.concatenate([rl_hi, rr_hi], axis=1).astype(F32),
                jnp.concatenate([rl_lo, rr_lo], axis=1).astype(F32))

    def own_part(lo, hi):
        if lo < 10:
            o1[lo:hi] = mm(operand(lo, hi), "W", 1).reshape(hi - lo, LP, 256)
        else:
            h, l = split(operand(lo, hi))
            w = const(("W", 1, "hi"))[:, 128:256]
            o1[lo:hi, :, 128:256] = (dot(h, w) + dot(l, w)).reshape(hi - lo, LP, 128)

    def bands1(js, halves):
        for j in js:
            if j < 10:
                p = dot(received(j, *halves), z1)
                t = o1[j] + p[0:LP] + p[LP:2 * LP]
                bd[42 + j] = vmul((1,), t[:, 0:128])[0]
                bd[j] = vmul((2,), t[:, 128:256])[0]
            else:
                p = dot(received(j, *halves), z1[:, 128:256])
                bd[j] = vmul((0,), o1[j, :, 128:256] + p[0:LP] + p[LP:2 * LP])[0]

    def even(i):
        tl[2 * i, :, 0:128] = -0.25 * (bd[42 + i] + bd[43 + i])
        tl[2 * i, :, 128:256] = bd[10 + i] - 0.25 * (bd[i] + bd[i + 1])

    def odd(i):
        tl[2 * i + 1, :, 0:128] = bd[43 + i] + 0.5 * (tl[2 * i, :, 0:128] + tl[2 * i + 2, :, 0:128])
        tl[2 * i + 1, :, 128:256] = bd[1 + i] + 0.5 * (tl[2 * i, :, 128:256] + tl[2 * i + 2, :, 128:256])

    def level1(lo, hi):
        ys[lo:hi] = mm(tl[lo:hi].reshape((hi - lo) * LP, 256), "T", 1).reshape(hi - lo, LP, 128)

    def to_next(src, dst):
        c = remote(src, dst, at_tm(1))

        @pl.when(tm < 3)
        def _():
            c.start()

        return c

    @pl.when(tm == 0)
    def _():
        prev[...] = jnp.zeros((ROWS, LP, 128), F32)
        pkp[...] = jnp.zeros((5, LP, 128), F32)

    for lo, hi in spans(inner):
        own_part(lo, hi)
    for c in lon0:
        c.wait()
    bands1(list(range(1, 8)) + list(range(11, 17)), arrived(0))
    for i in range(1, 7):
        even(i)
    for i in range(1, 6):
        odd(i)
    level1(2, 13)
    shift = [to_next(ys.at[pl.ds(2, 11)], prev.at[pl.ds(2, 11)])]

    for c in bulk:
        c.wait()
    x16 = lambda: mw * r_w[0]
    rw[0] = mu * r_u[...] - 0.5 * xs[0]
    rw[8] = dn[0] - 0.5 * x16()
    rw[9] = mw * r_w[1]
    rw[10] = xs[0] + 0.25 * (rw[0] + rw[1])
    rw[17] = xs[14] + 0.25 * (rw[7] + rw[8])
    rw[18] = x16() + (0.25 * mw) * (rw[8] + rw[9])
    rw[0] = mu * rw[0]
    message(1, spans(outer))
    lon1 = post(1)
    for lo, hi in spans(outer):
        own_part(lo, hi)

    for c in packs:
        c.wait()
    raw = lambda j: rw[j] if j < 19 else lx[j - 19, :, 0:128]
    for l in (2, 3, 4):
        m, a, d, b = MLAT[l], SROW[l - 1], DROW[l], SROW[l]
        lx[d - 19, :, 0:128] = so[dbase[l]]
        lx[d + m + 1 - 19, :, 0:128] = so[dbase[l] + m + 1]
        for i in range(m):
            lx[d + 1 + i - 19, :, 0:128] = raw(a + 2 * i + 1) - 0.5 * (raw(a + 2 * i) + raw(a + 2 * i + 2))
        for i in range(m + 1):
            v = raw(a + 2 * i) + 0.25 * (raw(d + i) + raw(d + i + 1))
            lx[b + i - 19, :, 0:128] = mw * v if i == m else v
    r_pu[...] = mu * r_pu[...] + mu2 * r_p2u[...]
    r_pw[...] = mw * r_pw[...] + mw2 * r_p2w[...]
    for j in range(19, NROWS):
        cu, cw = ext_c[j - 19:j - 18, :], ext_c[24 + j - 19:24 + j - 18, :]
        l, kind, i = LEVEL_OF[j]
        if kind == "S" and i == MLAT[l]:
            cu, cw = cu * mw, cw * mw
        lx[j - 19, :, 128:256] = r_pu[...] * cu + r_pw[...] * cw
    for l in (2, 3, 4):
        lx[DROW[l] - 19] = mu * lx[DROW[l] - 19]

    hi, lo = split(lx[SROW[4] - 19])
    fold = dot(hi, pm[0]) + dot(lo, pm[0]) + dot(hi, pm[1])
    for k in range(NLON_D):
        acc = jnp.zeros((FOLD, 128), F32)
        for g in range(LP // FOLD):
            acc = jnp.where((lane >= g * WIDE) & (lane < (g + 1) * WIDE),
                            fold[g * FOLD:(g + 1) * FOLD, k * 128:(k + 1) * 128], acc)
        sf[k] = acc
    for k in range(1, NLON_D):
        go(remote(sf.at[k], mf.at[k], at_lon(k)))
    coarse = copies[:]
    copies.clear()

    message(2, ((19, 30), (30, 37), (37, 42)))
    lon2 = post(2)

    for c in coarse:
        c.wait()
    row = sf[0] + mf[1] + mf[2] + mf[3]
    sf[0] = row
    cbuf[lat] = row
    for k in range(1, NLAT_D):
        go(remote(sf.at[0], cbuf.at[lat], at_lat(k)))
    coarse = copies[:]
    copies.clear()

    for c in lon1:
        c.wait()
    bands1((0, 8, 9, 10, 17, 18), arrived(1))
    for i in (0, 7, 8):
        even(i)
    for i in (0, 6, 7):
        odd(i)
    level1(0, 2)
    level1(13, 16)
    shift.append(to_next(ys.at[pl.ds(0, 2)], prev.at[pl.ds(0, 2)]))
    shift.append(to_next(ys.at[pl.ds(13, 3)], prev.at[pl.ds(13, 3)]))
    groups = {2: (19, 30), 3: (30, 37), 4: (37, 42)}
    for l in (2, 3, 4):
        lo, hi = groups[l]
        o2[lo - 19:hi - 19] = mm(operand(lo, hi), "W", l).reshape(hi - lo, LP, 128)
    for c in lon2:
        c.wait()
    halves = arrived(2)
    for l in (4, 3, 2):
        z = const(("Z", l, "hi"))
        for j in range(*groups[l]):
            p = dot(received(j, *halves), z)
            t = o2[j - 19] + p[0:LP] + p[LP:2 * LP]
            if LEVEL_OF[j][1] == "D":
                a, b = vmul((3 * l - 2, 3 * l - 1), t)
                bd[j] = jnp.where(low, a, b)
            else:
                bd[j] = jnp.where(low, 0.0, vmul((3 * l - 3,), t)[0])

    for c in coarse:
        c.wait()
    for rho in range(2):
        w = latf[pl.ds(jnp.minimum(lat + rho, NLAT_D - 1), 1), :]
        t = sum(cbuf[a] * w[:, a:a + 1] for a in range(NLAT_D))
        parts = [t if g == 0 else pltpu.roll(t, 128 - WIDE * g, 1) for g in range(LP // FOLD)]
        c = jnp.where(lane < WIDE, jnp.concatenate(parts, axis=0), 0.0)
        v = vmul((BANDS - 1,), c)[0]
        sm[rho] = v * mw if rho else v

    for l in (4, 3, 2):
        m, d, b = MLAT[l], DROW[l], SROW[l]
        for i in range(m + 1):
            s = bd[b + i] + sm[i]
            sm[i] = s - 0.25 * (bd[d + i] + bd[d + i + 1])
        for i in range(2 * m, -1, -1):
            if i % 2:
                h = i // 2
                tmsg[i, :, 0:128] = bd[d + 1 + h] + 0.5 * (sm[h] + sm[h + 1])
            else:
                tmsg[i, :, 0:128] = sm[i // 2]
        n = 2 * m + 1
        out = mm(tmsg[0:n, :, 0:128].reshape(n * LP, 128), "T", l).reshape(n, LP, 128)
        sm[0:n] = out
        sm[2 * m] = mw * sm[2 * m]

    last = sm[8]
    for k in range(9):
        last = jnp.where(lane == 64 + k, sm[k] if k == 0 else pltpu.roll(sm[k], k, 1), last)
    for k in range(4):
        pk[k] = jnp.where(low, sm[k], pltpu.roll(sm[k + 4], 64, 1))
    pk[4] = last
    shift.append(to_next(pk, pkp))

    def lifted(rows):
        w = const(("T", 1, "hi"))[0:128]
        for i in range(8):
            tmsg[2 * i, :, 0:128] = rows[i]
            tmsg[2 * i + 1, :, 0:128] = 0.5 * (rows[i] + rows[i + 1])
        h, l = split(tmsg[0:16, :, 0:128].reshape(16 * LP, 128))
        return (dot(h, w) + dot(l, w)).reshape(ROWS, LP, 128)

    yz[...] = ys[...] + lifted(sm)
    for r in range(ROWS):
        inc[pl.ds(r, LEV, stride=ROWS), :] = yz[r, 0:LEV, :]
    out = pltpu.make_async_copy(inc, inc_hbm, load.at[6])
    out.start()

    def settle(cs):
        for c in cs:
            pl.when(tm > 0)(c.wait_recv)

    settle(shift[:3])
    yz[...] = yz[...] - prev[...]
    settle(shift[3:])
    for k in range(9):
        part = pkp[k % 4] if k < 8 else pkp[4]
        if 4 <= k < 8:
            part = pltpu.roll(part, 64, 1)
        end = pkp[4] if k == 0 else pltpu.roll(pkp[4], 128 - k, 1)
        sm[k] = jnp.where(lane == 64, end, part)
    yz[...] = yz[...] - lifted(sm)
    for r in range(ROWS):
        jump[pl.ds(r, LEV, stride=ROWS), :] = yz[r, 0:LEV, :]
    out2 = pltpu.make_async_copy(jump, jump_hbm, load.at[7])
    out2.start()
    for c in shift:
        pl.when(tm < 3)(c.wait_send)
    out.wait()
    out2.wait()


def body(forcing, vertical, lat_factor, lon_factor):
    x = forcing.reshape(LEV * ROWS, COLS)
    tile = (LP, 128)
    anywhere = pl.BlockSpec(memory_space=pl.ANY)
    S = pltpu.VMEM
    flat = (LEV * ROWS, COLS)
    scratch = [
        S(flat, F32), S((BANDS, LEV, LEV), F32), S((8, 8), F32), S((32, 32), F32), S(CB.shape, BF), S(EXT.shape, F32),
        S(flat, F32), S(flat, F32),
        S((ROWS,) + tile, F32), S((39,) + tile, F32), S((19,) + tile, F32), S((23, LP, 256), F32),
        S((3,) + tile, F32), S((2,) + tile, F32), S((2,) + tile, F32),
        S((2,) + tile, F32), S(tile, F32), S(tile, F32), S(tile, F32), S(tile, F32), S(tile, F32),
        S((BANDS, 2 * LP, 256), BF), S((LP, 256), F32), S((2, 256, 512), BF),
        S((19, LP, 256), F32), S((23,) + tile, F32), S((17, LP, 256), F32), S((19, LP, 256), F32),
        S((3,) + tile, F32), S((3,) + tile, F32), S((3,) + tile, F32), S((3,) + tile, F32),
        S((4, FOLD, 128), F32), S((4, FOLD, 128), F32), S((8, FOLD, 128), F32),
        S((52,) + tile, F32), S((9,) + tile, F32), S((5,) + tile, F32), S((5,) + tile, F32),
        S((ROWS,) + tile, F32), S((ROWS,) + tile, F32), S((ROWS,) + tile, F32),
        pltpu.SemaphoreType.DMA((32,)), pltpu.SemaphoreType.DMA((32,)), pltpu.SemaphoreType.DMA((8,)),
    ]
    out = jax.ShapeDtypeStruct((LEV * ROWS, COLS), F32)
    inc, jump = pl.pallas_call(
        kernel,
        out_shape=(out, out),
        in_specs=[anywhere] * 6,
        out_specs=(anywhere, anywhere),
        scratch_shapes=scratch,
        compiler_params=pltpu.CompilerParams(
            collective_id=0, has_side_effects=True, vmem_limit_bytes=56 * 1024 * 1024),
    )(x, vertical, lat_factor, lon_factor, jnp.asarray(CB), jnp.asarray(EXT))
    shape = (1, LEV, ROWS, COLS)
    return inc.reshape(shape), jump.reshape(shape)


def solution(mesh):
    placed = (P("tm", None, "lat", "lon"), P(), P(), P())
    return jax.shard_map(
        body,
        mesh=mesh,
        in_specs=placed,
        out_specs=(P("tm", None, "lat", "lon"), P("tm", None, "lat", "lon")),
        check_vma=False,
    )
```

```python
import numpy as np
import jax
import jax.numpy as jnp
import ml_dtypes
from jax import lax
from jax.experimental import pallas as pl
from jax.experimental.pallas import tpu as pltpu
from jax.sharding import PartitionSpec as P

LEV, LP = 137, 144
ROWS, COLS = 16, 128
BANDS = 13
NLAT_D, NLON_D = 8, 4
MESH = pl.DeviceIdType.MESH
HIGH = lax.Precision.HIGHEST
F32, BF = jnp.float32, jnp.bfloat16

MLAT = {1: 8, 2: 4, 3: 2, 4: 1}
MLON = {1: 64, 2: 32, 3: 16, 4: 8}
DROW = {1: 0, 2: 19, 3: 30, 4: 37}
SROW = {1: 10, 2: 25, 3: 34, 4: 40}
NROWS = 42
PACK = {2: (0, 1, -1, 64), 3: (66, 2, -1, 33), 4: (101, 3, -1, 17)}
FOLD, WIDE = 16, 9
FOLD_LANES = LP // FOLD * WIDE
LEVEL_OF = {}
for _l in (1, 2, 3, 4):
    for _i in range(MLAT[_l] + 2):
        LEVEL_OF[DROW[_l] + _i] = (_l, "D", _i - 1)
    for _i in range(MLAT[_l] + 1):
        LEVEL_OF[SROW[_l] + _i] = (_l, "S", _i)


def lift(seq, size):
    lo, hi = min(seq), max(seq)
    zero = np.zeros(size)
    get = lambda table, i: table.get(i, zero)
    d, s = {}, {}
    for i in range(lo // 2 - 2, hi // 2 + 3):
        d[i] = get(seq, 2 * i + 1) - 0.5 * (get(seq, 2 * i) + get(seq, 2 * i + 2))
    for i in range(lo // 2 - 2, hi // 2 + 3):
        s[i] = get(seq, 2 * i) + 0.25 * (get(d, i - 1) + get(d, i))
    keep = lambda table: {i: v for i, v in table.items() if np.any(v)}
    return keep(s), keep(d)


INNER, OUTER = ((1, 8), (11, 17)), ((0, 1), (8, 11), (17, 19))
COARSER = ((19, 30), (30, 37), (37, 42))
MESSAGES = [[j for lo, hi in part for j in range(lo, hi)] for part in (INNER, OUTER, COARSER)]


def message_lanes():
    left, right, border = {}, {}, []
    for rows in MESSAGES:
        n = 0
        for table in (left, right):
            for j in rows:
                l, kind, _ = LEVEL_OF[j]
                if table is left:
                    names = ["dm1"] if l == 1 else (["sm", "dm1", "dm"] if kind == "D" else ["dm1", "dm"])
                else:
                    names = ["d-1", "d0"] if (l == 1 or kind == "S") else ["s0", "d-1", "d0"]
                table[j] = (n, names)
                n += len(names)
            if table is left:
                border.append(n)
        assert n <= 128
    return left, right, border


LEFT, RIGHT, BORDER = message_lanes()


def users(n):
    table = {}
    for j in MESSAGES[n]:
        l, kind, _ = LEVEL_OF[j]
        for k in ((3 * l - 2, 3 * l - 1) if kind == "D" else (3 * l - 3,)):
            table.setdefault(k, []).append(j)
    return table


def lon_tables():
    raw = {i: np.eye(256)[i] for i in range(COLS)}
    smooth, detail = {0: raw}, {}
    for l in range(1, 5):
        smooth[l], detail[l] = lift(smooth[l - 1], 256)
    ext_s = {}
    for l in (2, 3, 4):
        at, depth, lo, hi = PACK[l]
        seq = {i: np.eye(256)[128 + at + i - lo] for i in range(lo, hi + 1)}
        for k in range(l, 5):
            s, d = lift(seq, 256)
            seq = s
            ext_s[l, k] = (s, d)
    zero = np.zeros(256)
    full_s, full_d = {}, {}
    for k in range(1, 5):
        s, d = dict(smooth[k]), dict(detail[k])
        for l in range(2, k + 1):
            for table, more in ((s, ext_s[l, k][0]), (d, ext_s[l, k][1])):
                for i, v in more.items():
                    table[i] = table.get(i, zero) + v
        full_s[k], full_d[k] = s, d
    return smooth, full_s, full_d


def constants():
    smooth, fs, fd = lon_tables()
    zero = np.zeros(256)
    out = {}
    for l in (1, 2, 3, 4):
        m = MLON[l]
        w = np.zeros((256, 256))
        off = 128 if l == 1 else 64
        for i in range(0, m + 1):
            w[:, i] = fs[l].get(i, zero)
        for i in range(-1, m + 1):
            w[:, off + i + 1] = fd[l].get(i, zero)
        out["W", l] = w if l == 1 else w[:, :128]
        pick = {"sm": fs[l].get(m, zero), "dm1": fd[l].get(m - 1, zero), "dm": fd[l].get(m, zero),
                "s0": fs[l].get(0, zero), "d-1": fd[l].get(-1, zero), "d0": fd[l].get(0, zero)}
        for n, rows in enumerate(MESSAGES):
            rows = [j for j in rows if LEVEL_OF[j][0] == l]
            if not rows:
                continue
            g = np.zeros((256, 128))
            for j in rows:
                for at, names in (LEFT[j], RIGHT[j]):
                    for q, name in enumerate(names):
                        g[:, at + q] = pick[name]
            out["G", n, l] = g
            for k, js in users(n).items():
                if k // 3 != l - 1:
                    continue
                kind = k % 3
                z = np.zeros((128, 256 * ((len(js) + 1) // 2)))
                for p, j in enumerate(js):
                    smooths = np.zeros((128, 128))
                    details = np.zeros((128, 128))
                    at, names = LEFT[j]
                    for q, name in enumerate(names):
                        if name == "dm1":
                            details[at + q, 0] += 1.0
                            if l == 1:
                                smooths[at + q, 0] += 0.25
                        if name == "dm":
                            details[at + q, 1] += 1.0
                            smooths[at + q, 1] += 0.25
                        if name == "sm":
                            smooths[at + q, 0] += 1.0
                    at, names = RIGHT[j]
                    for q, name in enumerate(names):
                        if name == "s0":
                            smooths[at + q, m] += 1.0
                        if name == "d-1":
                            details[at + q, m] += 1.0
                            smooths[at + q, m - 1] += 0.25
                            if l == 1:
                                smooths[at + q, m] += -1.75
                        if name == "d0":
                            details[at + q, m + 1] += 1.0
                            if l == 1:
                                smooths[at + q, m] += 0.25
                    if l > 1:
                        details = np.roll(details, 64, axis=1)
                    z[:, 128 * p:128 * p + 128] = smooths if kind == 1 else details
                for c in range(0, z.shape[1], 256):
                    out["Z", n, k, c // 256] = z[:, c:c + 256]
        n_in = 256 if l == 1 else 128
        eye = np.eye(n_in)
        s = {i: eye[i] for i in range(0, m + 1)}
        d = {i: eye[off + i + 1] for i in range(-1, m + 1)}
        e = {i: s[i] - 0.25 * (d[i - 1] + d[i]) for i in range(0, m + 1)}
        t = np.zeros((n_in, 128))
        for i in range(0, m + 1):
            if 2 * i < 128:
                t[:, 2 * i] = e[i]
            if i < m:
                t[:, 2 * i + 1] = d[i] + 0.5 * (e[i] + e[i + 1])
        out["T", l] = t
    for l in (2, 3, 4):
        at, depth, lo, hi = PACK[l]
        sm = np.zeros((128, 128))
        for i in range(lo, hi + 1):
            sm[:, at + i - lo] = smooth[depth][i][:128]
        out["Sm", l] = sm
    c4 = np.zeros((256, 128))
    for c in range(11):
        c4[:, c] = fs[4].get(c - 1, zero)
    out["C4", 0] = c4
    return out


CONST = constants()


def pack_constants():
    tiles, where = [], {}

    def put(key, a):
        k, n = a.shape
        where[key] = (sum(t.shape[0] for t in tiles), k, n)
        if n < 256:
            a = np.concatenate([a, np.zeros((k, 256 - n), a.dtype)], 1)
        tiles.append(a)

    for key, a in CONST.items():
        if key == ("W", 1) or (key[0] == "G" and key[2] == 1):
            a = a[:128]
        hi = a.astype(ml_dtypes.bfloat16)
        lo = (a - hi.astype(np.float64)).astype(ml_dtypes.bfloat16)
        put(key + ("hi",), hi)
        if np.any(lo.astype(np.float64)):
            put(key + ("lo",), lo)
    return np.concatenate(tiles, 0), where


CB, CWHERE = pack_constants()


def ext_coefficients():
    syms = {("U", 2): 0, ("U", 3): 1, ("U", 4): 2, ("W", 2): 3, ("W", 3): 4, ("W", 4): 5}
    unit = lambda key: np.eye(6)[syms[key]]
    zero = np.zeros(6)
    s = {i: zero for i in range(9)}
    table = {}
    for l in (2, 3, 4):
        m = MLAT[l]
        d = {-1: unit(("U", l)), m: unit(("W", l))}
        for i in range(m):
            d[i] = s[2 * i + 1] - 0.5 * (s[2 * i] + s[2 * i + 2])
        s = {i: s[2 * i] + 0.25 * (d[i - 1] + d[i]) for i in range(m + 1)}
        for i in range(-1, m + 1):
            table[DROW[l] + i + 1] = d[i]
        for i in range(m + 1):
            table[SROW[l] + i] = s[i]
    out = np.zeros((48, 128), np.float32)
    for j, v in table.items():
        for l in (2, 3, 4):
            at, _, lo, hi = PACK[l]
            out[j - 19, at:at + hi - lo + 1] = v[l - 2]
            out[24 + j - 19, at:at + hi - lo + 1] = v[3 + l - 2]
    return out


EXT = ext_coefficients()


def split(a):
    hi = a.astype(BF)
    return hi, (a - hi.astype(F32)).astype(BF)


def dot(a, b):
    return jnp.dot(a, b, preferred_element_type=F32)


def kernel(x_hbm, vert_hbm, latf_hbm, lonf_hbm, cb_hbm, ext_hbm, inc_hbm, jump_hbm,
           x, vert, latf, lonf, cb, ext_c, inc, jump,
           xs, so, rw, lx, up, dn, p2, r_w, r_u, r_pw, r_pu, r_p2u, r_p2w,
           vst, vtmp, pm, o1, o2, tl, tmsg, sd, m_l, m_r, sf, mf, cbuf,
           bd, sm, pk, pkp, ys, yz, prev, send, recv, load):
    tm, lat, lon = lax.axis_index("tm"), lax.axis_index("lat"), lax.axis_index("lon")
    mu = (lat > 0).astype(F32)
    mw = (lat < NLAT_D - 1).astype(F32)
    mu2 = (lat > 1).astype(F32)
    mw2 = (lat < NLAT_D - 2).astype(F32)

    def at_lat(k):
        return (tm, lax.rem(lat + k + NLAT_D, NLAT_D), lon)

    def at_lon(k):
        return (tm, lat, lax.rem(lon + k + NLON_D, NLON_D))

    def at_tm(k):
        return (lax.rem(tm + k + 4, 4), lat, lon)

    partners = [at_lat(k) for k in range(1, 8)] + [at_lon(k) for k in range(1, 4)] + [at_tm(1), at_tm(-1)]
    barrier = pltpu.get_barrier_semaphore()
    for p in partners:
        pl.semaphore_signal(barrier, inc=1, device_id=p, device_id_type=MESH)

    loads = {}
    for n, (name, src, dst) in enumerate((("x", x_hbm, x), ("cb", cb_hbm, cb), ("ext", ext_hbm, ext_c),
                                          ("lonf", lonf_hbm, lonf), ("latf", latf_hbm, latf),
                                          ("vert", vert_hbm, vert))):
        loads[name] = pltpu.make_async_copy(src, dst, load.at[n])
        loads[name].start()

    def const(key):
        at, k, n = CWHERE[key]
        return cb[at:at + k, 0:n]

    def mm(a, *key):
        hi, lo = split(a)
        w = const(key + ("hi",))
        out = dot(hi, w) + dot(lo, w)
        if key + ("lo",) in CWHERE:
            out = out + dot(hi, const(key + ("lo",)))
        return out

    loads["x"].wait()
    for r in range(ROWS):
        xs[r, 136:144, :] = jnp.zeros((8, COLS), F32)
        xs[r, 0:LEV, :] = x[pl.ds(r, LEV, stride=ROWS), :]

    for i in range(7):
        rw[1 + i] = xs[2 * i + 1] - 0.5 * (xs[2 * i] + xs[2 * i + 2])
    dn[0] = xs[15] - 0.5 * xs[14]
    up[0] = xs[0]
    up[1] = rw[1]

    sems = iter(range(64))

    def remote(src, dst, dev, slot=None):
        k = next(sems)
        return pltpu.make_async_remote_copy(
            src_ref=src, dst_ref=dst, send_sem=send.at[k],
            recv_sem=recv.at[k], device_id=dev, device_id_type=MESH)

    copies = []

    def go(c):
        c.start()
        copies.append(c)

    so[0] = (-0.125 * mu) * xs[0]
    so[1] = 0.875 * xs[0] + 0.25 * rw[1]
    for i in range(1, 7):
        so[1 + i] = xs[2 * i] + 0.25 * (rw[i] + rw[1 + i])
    so[8] = xs[14] + 0.25 * (rw[7] + dn[0])
    so[9] = (0.25 * mw) * dn[0]
    sbase = {1: 0, 2: 10, 3: 17, 4: 22}
    dbase = {2: 26, 3: 32, 4: 36}
    for l in (2, 3, 4):
        m, a, b, d = MLAT[l], sbase[l - 1], sbase[l], dbase[l]
        S = lambda i: so[a + 1 + i]
        so[d] = S(-1) - 0.5 * S(0)
        for i in range(m):
            so[d + 1 + i] = S(2 * i + 1) - 0.5 * (S(2 * i) + S(2 * i + 2))
        so[d + 1 + m] = (-0.5 * S(2 * m)) if l == 2 else S(2 * m + 1) - 0.5 * S(2 * m)
        so[b] = (0.25 * mu) * so[d]
        for i in range(m):
            so[b + 1 + i] = S(2 * i) + 0.25 * (so[d + i] + so[d + 1 + i])
        so[b + 1 + m] = mw * (S(2 * m) + 0.25 * (so[d + m] + so[d + 1 + m]))
        so[b + 2 + m] = (0.25 * mw) * so[d + 1 + m]
    loads["cb"].wait()
    d4 = mm(so[37], "Sm", 4)
    up[2] = mm(so[27], "Sm", 2) + mm(so[33], "Sm", 3) + d4
    dn[1] = mm(so[30], "Sm", 2) + mm(so[34], "Sm", 3) + d4
    p2[0] = mm(so[38], "Sm", 4)
    p2[1] = mm(so[36], "Sm", 4)
    for i in range(1, 7):
        rw[10 + i] = xs[2 * i] + 0.25 * (rw[i] + rw[i + 1])

    lane = lax.broadcasted_iota(jnp.int32, (1, 128), 1)
    def operand(lo, hi):
        if hi <= 19:
            return rw[lo:hi].reshape((hi - lo) * LP, 128)
        return lx[lo - 19:hi - 19].reshape((hi - lo) * LP, 256)

    def message(n, groups):
        for lo, hi in groups:
            tmsg[0:hi - lo, :, 0:128] = mm(operand(lo, hi), "G", n, LEVEL_OF[lo][0]).reshape(hi - lo, LP, 128)
            v = jnp.zeros((LP, 128), F32) if lo == groups[0][0] else sd[n]
            for j in range(lo, hi):
                (a, na), (b, nb) = LEFT[j], RIGHT[j]
                keep = ((lane >= a) & (lane < a + len(na))) | ((lane >= b) & (lane < b + len(nb)))
                v = jnp.where(keep, tmsg[j - lo, :, 0:128], v)
            sd[n] = v

    def post(n):
        out = [remote(sd.at[n], m_l.at[n], at_lon(1)), remote(sd.at[n], m_r.at[n], at_lon(-1))]
        for c in out:
            c.start()
        return out

    message(0, INNER)
    pl.semaphore_wait(barrier, len(partners))
    bulk = [remote(up.at[pl.ds(0, 2)], r_w, at_lat(-1)), remote(dn.at[0], r_u, at_lat(1))]
    for c in bulk:
        c.start()
    lon0 = post(0)
    go(remote(up.at[2], r_pw, at_lat(-1)))
    go(remote(dn.at[1], r_pu, at_lat(1)))
    go(remote(p2.at[0], r_p2u, at_lat(2)))
    go(remote(p2.at[1], r_p2w, at_lat(-2)))
    packs = copies[:]
    copies.clear()

    for name in ("ext", "lonf", "latf", "vert"):
        loads[name].wait()
    vtmp[...] = jnp.zeros((LP, 256), F32)
    for k in range(BANDS):
        vtmp[0:LEV, 0:LEV] = vert[k]
        hi, lo = split(vtmp[...])
        vst[k, 0:LP, :] = hi
        vst[k, LP:2 * LP, :] = lo
    rowi = lax.broadcasted_iota(jnp.int32, (128, 32), 0)
    coli = lax.broadcasted_iota(jnp.int32, (128, 32), 1)
    mine = ((rowi < 11) & (coli == lax.rem(8 * lon + 31 + rowi, 32))).astype(F32)
    for k in range(NLON_D):
        theirs = (rowi < FOLD_LANES) & (coli == lax.rem(8 * (lon + k) + lax.rem(rowi, WIDE), 32))
        part = jnp.dot(theirs.astype(F32), lonf[...], precision=HIGH, preferred_element_type=F32)
        part = lax.dot_general(mine, part, (((1,), (1,)), ((), ())), precision=HIGH,
                               preferred_element_type=F32)
        c4 = const(("C4", 0, "hi")).astype(F32) + const(("C4", 0, "lo")).astype(F32)
        hi, lo = split(jnp.dot(c4, part, precision=HIGH, preferred_element_type=F32))
        pm[0, :, k * 128:(k + 1) * 128] = hi
        pm[1, :, k * 128:(k + 1) * 128] = lo

    low = lane < 64
    def vmul(ks, t):
        hi, lo = split(t)
        both = jnp.concatenate([hi, lo], axis=1)
        outs = []
        for k in ks:
            p = dot(vst[k][:, 0:LP], both)
            outs.append(p[0:LP, 0:128] + p[0:LP, 128:256] + p[LP:2 * LP, 0:128])
        return outs

    def settle(n):
        got = jnp.where(lane < BORDER[n], m_l[n], m_r[n])
        for k, js in users(n).items():
            hi, lo = split(vmul((k,), got)[0])
            both = jnp.concatenate([hi, lo], axis=1)
            for c in range((len(js) + 1) // 2):
                z = const(("Z", n, k, c, "hi"))
                p = dot(both, jnp.concatenate([z, z], axis=0))
                for h, j in enumerate(js[2 * c:2 * c + 2]):
                    at = j + 42 if k == 1 else j
                    bd[at] = bd[at] + p[:, 128 * h:128 * h + 128]

    def own_part(lo, hi):
        if lo < 10:
            o1[lo:hi] = mm(operand(lo, hi), "W", 1).reshape(hi - lo, LP, 256)
        else:
            h, l = split(operand(lo, hi))
            w = const(("W", 1, "hi"))[:, 128:256]
            o1[lo:hi, :, 128:256] = (dot(h, w) + dot(l, w)).reshape(hi - lo, LP, 128)

    def bands1(js):
        for j in js:
            if j < 10:
                bd[42 + j] = vmul((1,), o1[j, :, 0:128])[0]
                bd[j] = vmul((2,), o1[j, :, 128:256])[0]
            else:
                bd[j] = vmul((0,), o1[j, :, 128:256])[0]

    def bands(l):
        lo, hi = COARSER[l - 2]
        o2[lo - 19:hi - 19] = mm(operand(lo, hi), "W", l).reshape(hi - lo, LP, 128)
        for j in range(lo, hi):
            if LEVEL_OF[j][1] == "D":
                a, b = vmul((3 * l - 2, 3 * l - 1), o2[j - 19])
                bd[j] = jnp.where(low, a, b)
            else:
                bd[j] = jnp.where(low, 0.0, vmul((3 * l - 3,), o2[j - 19])[0])

    def even(i):
        tl[2 * i, :, 0:128] = -0.25 * (bd[42 + i] + bd[43 + i])
        tl[2 * i, :, 128:256] = bd[10 + i] - 0.25 * (bd[i] + bd[i + 1])

    def odd(i):
        tl[2 * i + 1, :, 0:128] = bd[43 + i] + 0.5 * (tl[2 * i, :, 0:128] + tl[2 * i + 2, :, 0:128])
        tl[2 * i + 1, :, 128:256] = bd[1 + i] + 0.5 * (tl[2 * i, :, 128:256] + tl[2 * i + 2, :, 128:256])

    def level1(lo, hi):
        ys[lo:hi] = mm(tl[lo:hi].reshape((hi - lo) * LP, 256), "T", 1).reshape(hi - lo, LP, 128)

    def to_next(src, dst):
        c = remote(src, dst, at_tm(1))

        @pl.when(tm < 3)
        def _():
            c.start()

        return c

    @pl.when(tm == 0)
    def _():
        prev[...] = jnp.zeros((ROWS, LP, 128), F32)
        pkp[...] = jnp.zeros((5, LP, 128), F32)

    for lo, hi in INNER:
        own_part(lo, hi)
    bands1(MESSAGES[0])
    for c in lon0:
        c.wait()
    settle(0)
    for i in range(1, 7):
        even(i)
    for i in range(1, 6):
        odd(i)
    level1(2, 13)
    shift = [to_next(ys.at[pl.ds(2, 11)], prev.at[pl.ds(2, 11)])]

    for c in bulk:
        c.wait()
    x16 = lambda: mw * r_w[0]
    rw[0] = mu * r_u[...] - 0.5 * xs[0]
    rw[8] = dn[0] - 0.5 * x16()
    rw[9] = mw * r_w[1]
    rw[10] = xs[0] + 0.25 * (rw[0] + rw[1])
    rw[17] = xs[14] + 0.25 * (rw[7] + rw[8])
    rw[18] = x16() + (0.25 * mw) * (rw[8] + rw[9])
    rw[0] = mu * rw[0]
    message(1, OUTER)
    lon1 = post(1)
    for lo, hi in OUTER:
        own_part(lo, hi)
    bands1(MESSAGES[1])

    for c in packs:
        c.wait()
    raw = lambda j: rw[j] if j < 19 else lx[j - 19, :, 0:128]
    for l in (2, 3, 4):
        m, a, d, b = MLAT[l], SROW[l - 1], DROW[l], SROW[l]
        lx[d - 19, :, 0:128] = so[dbase[l]]
        lx[d + m + 1 - 19, :, 0:128] = so[dbase[l] + m + 1]
        for i in range(m):
            lx[d + 1 + i - 19, :, 0:128] = raw(a + 2 * i + 1) - 0.5 * (raw(a + 2 * i) + raw(a + 2 * i + 2))
        for i in range(m + 1):
            v = raw(a + 2 * i) + 0.25 * (raw(d + i) + raw(d + i + 1))
            lx[b + i - 19, :, 0:128] = mw * v if i == m else v
    r_pu[...] = mu * r_pu[...] + mu2 * r_p2u[...]
    r_pw[...] = mw * r_pw[...] + mw2 * r_p2w[...]
    for j in range(19, NROWS):
        cu, cw = ext_c[j - 19:j - 18, :], ext_c[24 + j - 19:24 + j - 18, :]
        l, kind, i = LEVEL_OF[j]
        if kind == "S" and i == MLAT[l]:
            cu, cw = cu * mw, cw * mw
        lx[j - 19, :, 128:256] = r_pu[...] * cu + r_pw[...] * cw
    for l in (2, 3, 4):
        lx[DROW[l] - 19] = mu * lx[DROW[l] - 19]

    hi, lo = split(lx[SROW[4] - 19])
    fold = dot(hi, pm[0]) + dot(lo, pm[0]) + dot(hi, pm[1])
    for k in range(NLON_D):
        acc = jnp.zeros((FOLD, 128), F32)
        for g in range(LP // FOLD):
            acc = jnp.where((lane >= g * WIDE) & (lane < (g + 1) * WIDE),
                            fold[g * FOLD:(g + 1) * FOLD, k * 128:(k + 1) * 128], acc)
        sf[k] = acc
    for k in range(1, NLON_D):
        go(remote(sf.at[k], mf.at[k], at_lon(k)))
    coarse = copies[:]
    copies.clear()

    message(2, COARSER)
    lon2 = post(2)
    bands(4)
    bands(3)

    for c in coarse:
        c.wait()
    row = sf[0] + mf[1] + mf[2] + mf[3]
    sf[0] = row
    cbuf[lat] = row
    for k in range(1, NLAT_D):
        go(remote(sf.at[0], cbuf.at[lat], at_lat(k)))
    coarse = copies[:]
    copies.clear()

    for c in lon1:
        c.wait()
    settle(1)
    for i in (0, 7, 8):
        even(i)
    for i in (0, 6, 7):
        odd(i)
    level1(0, 2)
    level1(13, 16)
    shift.append(to_next(ys.at[pl.ds(0, 2)], prev.at[pl.ds(0, 2)]))
    shift.append(to_next(ys.at[pl.ds(13, 3)], prev.at[pl.ds(13, 3)]))
    bands(2)
    for c in lon2:
        c.wait()
    settle(2)

    for c in coarse:
        c.wait()
    for rho in range(2):
        w = latf[pl.ds(jnp.minimum(lat + rho, NLAT_D - 1), 1), :]
        t = sum(cbuf[a] * w[:, a:a + 1] for a in range(NLAT_D))
        parts = [t if g == 0 else pltpu.roll(t, 128 - WIDE * g, 1) for g in range(LP // FOLD)]
        c = jnp.where(lane < WIDE, jnp.concatenate(parts, axis=0), 0.0)
        v = vmul((BANDS - 1,), c)[0]
        sm[rho] = v * mw if rho else v

    for l in (4, 3, 2):
        m, d, b = MLAT[l], DROW[l], SROW[l]
        for i in range(m + 1):
            s = bd[b + i] + sm[i]
            sm[i] = s - 0.25 * (bd[d + i] + bd[d + i + 1])
        for i in range(2 * m, -1, -1):
            if i % 2:
                h = i // 2
                tmsg[i, :, 0:128] = bd[d + 1 + h] + 0.5 * (sm[h] + sm[h + 1])
            else:
                tmsg[i, :, 0:128] = sm[i // 2]
        n = 2 * m + 1
        out = mm(tmsg[0:n, :, 0:128].reshape(n * LP, 128), "T", l).reshape(n, LP, 128)
        sm[0:n] = out
        sm[2 * m] = mw * sm[2 * m]

    last = sm[8]
    for k in range(9):
        last = jnp.where(lane == 64 + k, sm[k] if k == 0 else pltpu.roll(sm[k], k, 1), last)
    for k in range(4):
        pk[k] = jnp.where(low, sm[k], pltpu.roll(sm[k + 4], 64, 1))
    pk[4] = last
    shift.append(to_next(pk, pkp))

    def lifted(rows):
        w = const(("T", 1, "hi"))[0:128]
        for i in range(8):
            tmsg[2 * i, :, 0:128] = rows[i]
            tmsg[2 * i + 1, :, 0:128] = 0.5 * (rows[i] + rows[i + 1])
        h, l = split(tmsg[0:16, :, 0:128].reshape(16 * LP, 128))
        return (dot(h, w) + dot(l, w)).reshape(ROWS, LP, 128)

    yz[...] = ys[...] + lifted(sm)
    for r in range(ROWS):
        inc[pl.ds(r, LEV, stride=ROWS), :] = yz[r, 0:LEV, :]
    out = pltpu.make_async_copy(inc, inc_hbm, load.at[6])
    out.start()

    def land(cs):
        for c in cs:
            pl.when(tm > 0)(c.wait_recv)

    land(shift[:3])
    yz[...] = yz[...] - prev[...]
    land(shift[3:])
    for k in range(9):
        part = pkp[k % 4] if k < 8 else pkp[4]
        if 4 <= k < 8:
            part = pltpu.roll(part, 64, 1)
        end = pkp[4] if k == 0 else pltpu.roll(pkp[4], 128 - k, 1)
        sm[k] = jnp.where(lane == 64, end, part)
    yz[...] = yz[...] - lifted(sm)
    for r in range(ROWS):
        jump[pl.ds(r, LEV, stride=ROWS), :] = yz[r, 0:LEV, :]
    out2 = pltpu.make_async_copy(jump, jump_hbm, load.at[7])
    out2.start()
    for c in shift:
        pl.when(tm < 3)(c.wait_send)
    out.wait()
    out2.wait()


def body(forcing, vertical, lat_factor, lon_factor):
    x = forcing.reshape(LEV * ROWS, COLS)
    tile = (LP, 128)
    anywhere = pl.BlockSpec(memory_space=pl.ANY)
    S = pltpu.VMEM
    flat = (LEV * ROWS, COLS)
    scratch = [
        S(flat, F32), S((BANDS, LEV, LEV), F32), S((8, 8), F32), S((32, 32), F32), S(CB.shape, BF), S(EXT.shape, F32),
        S(flat, F32), S(flat, F32),
        S((ROWS,) + tile, F32), S((39,) + tile, F32), S((19,) + tile, F32), S((23, LP, 256), F32),
        S((3,) + tile, F32), S((2,) + tile, F32), S((2,) + tile, F32),
        S((2,) + tile, F32), S(tile, F32), S(tile, F32), S(tile, F32), S(tile, F32), S(tile, F32),
        S((BANDS, 2 * LP, 256), BF), S((LP, 256), F32), S((2, 256, 512), BF),
        S((19, LP, 256), F32), S((23,) + tile, F32), S((17, LP, 256), F32), S((19, LP, 256), F32),
        S((3,) + tile, F32), S((3,) + tile, F32), S((3,) + tile, F32),
        S((4, FOLD, 128), F32), S((4, FOLD, 128), F32), S((8, FOLD, 128), F32),
        S((52,) + tile, F32), S((9,) + tile, F32), S((5,) + tile, F32), S((5,) + tile, F32),
        S((ROWS,) + tile, F32), S((ROWS,) + tile, F32), S((ROWS,) + tile, F32),
        pltpu.SemaphoreType.DMA((32,)), pltpu.SemaphoreType.DMA((32,)), pltpu.SemaphoreType.DMA((8,)),
    ]
    out = jax.ShapeDtypeStruct((LEV * ROWS, COLS), F32)
    inc, jump = pl.pallas_call(
        kernel,
        out_shape=(out, out),
        in_specs=[anywhere] * 6,
        out_specs=(anywhere, anywhere),
        scratch_shapes=scratch,
        compiler_params=pltpu.CompilerParams(
            collective_id=0, has_side_effects=True, vmem_limit_bytes=56 * 1024 * 1024),
    )(x, vertical, lat_factor, lon_factor, jnp.asarray(CB), jnp.asarray(EXT))

    def settle(a, b, c, d, held, arrive, leave):
        size = LEV * ROWS // 2
        moves = []
        for k in range(2):
            for h, (src, dst) in enumerate(((a, c), (b, d))):
                part = pl.ds(k * size, size)
                moves.append((pltpu.make_async_copy(src.at[part], held.at[h, part], arrive.at[2 * k + h]),
                              pltpu.make_async_copy(held.at[h, part], dst.at[part], leave.at[2 * k + h])))
        for m, _ in moves:
            m.start()
        for m, o in moves:
            m.wait()
            o.start()
        for _, o in moves:
            o.wait()

    inc, jump = pl.pallas_call(
        settle, out_shape=(out, out), in_specs=[anywhere] * 2, out_specs=(anywhere, anywhere),
        scratch_shapes=[S((2,) + flat, F32), pltpu.SemaphoreType.DMA((4,)), pltpu.SemaphoreType.DMA((4,))],
    )(inc, jump)
    shape = (1, LEV, ROWS, COLS)
    return inc.reshape(shape), jump.reshape(shape)


def solution(mesh):
    placed = (P("tm", None, "lat", "lon"), P(), P(), P())
    return jax.shard_map(
        body,
        mesh=mesh,
        in_specs=placed,
        out_specs=(P("tm", None, "lat", "lon"), P("tm", None, "lat", "lon")),
        check_vma=False,
    )
```

```python
import numpy as np
import jax
import jax.numpy as jnp
import ml_dtypes
from jax import lax
from jax.experimental import pallas as pl
from jax.experimental.pallas import tpu as pltpu
from jax.sharding import PartitionSpec as P

LEV, LP = 137, 144
ROWS, COLS = 16, 128
BANDS = 13
NLAT_D, NLON_D = 8, 4
MESH = pl.DeviceIdType.MESH
HIGH = lax.Precision.HIGHEST
F32, BF = jnp.float32, jnp.bfloat16

MLAT = {1: 8, 2: 4, 3: 2, 4: 1}
MLON = {1: 64, 2: 32, 3: 16, 4: 8}
DROW = {1: 0, 2: 19, 3: 30, 4: 37}
SROW = {1: 10, 2: 25, 3: 34, 4: 40}
NROWS = 42
PACK = {2: (0, 1, -1, 64), 3: (66, 2, -1, 33), 4: (101, 3, -1, 17)}
FOLD, WIDE = 16, 9
FOLD_LANES = LP // FOLD * WIDE
LEVEL_OF = {}
for _l in (1, 2, 3, 4):
    for _i in range(MLAT[_l] + 2):
        LEVEL_OF[DROW[_l] + _i] = (_l, "D", _i - 1)
    for _i in range(MLAT[_l] + 1):
        LEVEL_OF[SROW[_l] + _i] = (_l, "S", _i)


def lift(seq, size):
    lo, hi = min(seq), max(seq)
    zero = np.zeros(size)
    get = lambda table, i: table.get(i, zero)
    d, s = {}, {}
    for i in range(lo // 2 - 2, hi // 2 + 3):
        d[i] = get(seq, 2 * i + 1) - 0.5 * (get(seq, 2 * i) + get(seq, 2 * i + 2))
    for i in range(lo // 2 - 2, hi // 2 + 3):
        s[i] = get(seq, 2 * i) + 0.25 * (get(d, i - 1) + get(d, i))
    keep = lambda table: {i: v for i, v in table.items() if np.any(v)}
    return keep(s), keep(d)


INNER, OUTER = ((1, 8), (11, 17)), ((0, 1), (8, 11), (17, 19))
COARSER = ((19, 30), (30, 37), (37, 42))
MESSAGES = [[j for lo, hi in part for j in range(lo, hi)] for part in (INNER, OUTER, COARSER)]


def message_lanes():
    left, right, border = {}, {}, []
    for rows in MESSAGES:
        n = 0
        for table in (left, right):
            for j in rows:
                l, kind, _ = LEVEL_OF[j]
                if table is left:
                    names = ["dm1"] if l == 1 else (["sm", "dm1", "dm"] if kind == "D" else ["dm1", "dm"])
                else:
                    names = ["d-1", "d0"] if (l == 1 or kind == "S") else ["s0", "d-1", "d0"]
                table[j] = (n, names)
                n += len(names)
            if table is left:
                border.append(n)
        assert n <= 128
    return left, right, border


LEFT, RIGHT, BORDER = message_lanes()


def users(n):
    table = {}
    for j in MESSAGES[n]:
        l, kind, _ = LEVEL_OF[j]
        for k in ((3 * l - 2, 3 * l - 1) if kind == "D" else (3 * l - 3,)):
            table.setdefault(k, []).append(j)
    return table


def lon_tables():
    raw = {i: np.eye(256)[i] for i in range(COLS)}
    smooth, detail = {0: raw}, {}
    for l in range(1, 5):
        smooth[l], detail[l] = lift(smooth[l - 1], 256)
    ext_s = {}
    for l in (2, 3, 4):
        at, depth, lo, hi = PACK[l]
        seq = {i: np.eye(256)[128 + at + i - lo] for i in range(lo, hi + 1)}
        for k in range(l, 5):
            s, d = lift(seq, 256)
            seq = s
            ext_s[l, k] = (s, d)
    zero = np.zeros(256)
    full_s, full_d = {}, {}
    for k in range(1, 5):
        s, d = dict(smooth[k]), dict(detail[k])
        for l in range(2, k + 1):
            for table, more in ((s, ext_s[l, k][0]), (d, ext_s[l, k][1])):
                for i, v in more.items():
                    table[i] = table.get(i, zero) + v
        full_s[k], full_d[k] = s, d
    return smooth, full_s, full_d


def constants():
    smooth, fs, fd = lon_tables()
    zero = np.zeros(256)
    out = {}
    for l in (1, 2, 3, 4):
        m = MLON[l]
        w = np.zeros((256, 256))
        off = 128 if l == 1 else 64
        for i in range(0, m + 1):
            w[:, i] = fs[l].get(i, zero)
        for i in range(-1, m + 1):
            w[:, off + i + 1] = fd[l].get(i, zero)
        out["W", l] = w if l == 1 else w[:, :128]
        pick = {"sm": fs[l].get(m, zero), "dm1": fd[l].get(m - 1, zero), "dm": fd[l].get(m, zero),
                "s0": fs[l].get(0, zero), "d-1": fd[l].get(-1, zero), "d0": fd[l].get(0, zero)}
        for n, rows in enumerate(MESSAGES):
            rows = [j for j in rows if LEVEL_OF[j][0] == l]
            if not rows:
                continue
            g = np.zeros((256, 128))
            for j in rows:
                for at, names in (LEFT[j], RIGHT[j]):
                    for q, name in enumerate(names):
                        g[:, at + q] = pick[name]
            out["G", n, l] = g
            for k, js in users(n).items():
                if k // 3 != l - 1:
                    continue
                kind = k % 3
                z = np.zeros((128, 256 * ((len(js) + 1) // 2)))
                for p, j in enumerate(js):
                    smooths = np.zeros((128, 128))
                    details = np.zeros((128, 128))
                    at, names = LEFT[j]
                    for q, name in enumerate(names):
                        if name == "dm1":
                            details[at + q, 0] += 1.0
                            if l == 1:
                                smooths[at + q, 0] += 0.25
                        if name == "dm":
                            details[at + q, 1] += 1.0
                            smooths[at + q, 1] += 0.25
                        if name == "sm":
                            smooths[at + q, 0] += 1.0
                    at, names = RIGHT[j]
                    for q, name in enumerate(names):
                        if name == "s0":
                            smooths[at + q, m] += 1.0
                        if name == "d-1":
                            details[at + q, m] += 1.0
                            smooths[at + q, m - 1] += 0.25
                            if l == 1:
                                smooths[at + q, m] += -1.75
                        if name == "d0":
                            details[at + q, m + 1] += 1.0
                            if l == 1:
                                smooths[at + q, m] += 0.25
                    if l > 1:
                        details = np.roll(details, 64, axis=1)
                    z[:, 128 * p:128 * p + 128] = smooths if kind == 1 else details
                for c in range(0, z.shape[1], 256):
                    out["Z", n, k, c // 256] = z[:, c:c + 256]
        n_in = 256 if l == 1 else 128
        eye = np.eye(n_in)
        s = {i: eye[i] for i in range(0, m + 1)}
        d = {i: eye[off + i + 1] for i in range(-1, m + 1)}
        e = {i: s[i] - 0.25 * (d[i - 1] + d[i]) for i in range(0, m + 1)}
        t = np.zeros((n_in, 128))
        for i in range(0, m + 1):
            if 2 * i < 128:
                t[:, 2 * i] = e[i]
            if i < m:
                t[:, 2 * i + 1] = d[i] + 0.5 * (e[i] + e[i + 1])
        out["T", l] = t
    for l in (2, 3, 4):
        at, depth, lo, hi = PACK[l]
        sm = np.zeros((128, 128))
        for i in range(lo, hi + 1):
            sm[:, at + i - lo] = smooth[depth][i][:128]
        out["Sm", l] = sm
    c4 = np.zeros((256, 128))
    for c in range(11):
        c4[:, c] = fs[4].get(c - 1, zero)
    out["C4", 0] = c4
    return out


CONST = constants()


def pack_constants():
    tiles, where = [], {}

    def put(key, a):
        k, n = a.shape
        where[key] = (sum(t.shape[0] for t in tiles), k, n)
        if n < 256:
            a = np.concatenate([a, np.zeros((k, 256 - n), a.dtype)], 1)
        tiles.append(a)

    for key, a in CONST.items():
        if key == ("W", 1) or (key[0] == "G" and key[2] == 1):
            a = a[:128]
        hi = a.astype(ml_dtypes.bfloat16)
        lo = (a - hi.astype(np.float64)).astype(ml_dtypes.bfloat16)
        put(key + ("hi",), hi)
        if np.any(lo.astype(np.float64)):
            put(key + ("lo",), lo)
    return np.concatenate(tiles, 0), where


CB, CWHERE = pack_constants()


def ext_coefficients():
    syms = {("U", 2): 0, ("U", 3): 1, ("U", 4): 2, ("W", 2): 3, ("W", 3): 4, ("W", 4): 5}
    unit = lambda key: np.eye(6)[syms[key]]
    zero = np.zeros(6)
    s = {i: zero for i in range(9)}
    table = {}
    for l in (2, 3, 4):
        m = MLAT[l]
        d = {-1: unit(("U", l)), m: unit(("W", l))}
        for i in range(m):
            d[i] = s[2 * i + 1] - 0.5 * (s[2 * i] + s[2 * i + 2])
        s = {i: s[2 * i] + 0.25 * (d[i - 1] + d[i]) for i in range(m + 1)}
        for i in range(-1, m + 1):
            table[DROW[l] + i + 1] = d[i]
        for i in range(m + 1):
            table[SROW[l] + i] = s[i]
    out = np.zeros((48, 128), np.float32)
    for j, v in table.items():
        for l in (2, 3, 4):
            at, _, lo, hi = PACK[l]
            out[j - 19, at:at + hi - lo + 1] = v[l - 2]
            out[24 + j - 19, at:at + hi - lo + 1] = v[3 + l - 2]
    return out


EXT = ext_coefficients()


def split(a):
    hi = a.astype(BF)
    return hi, (a - hi.astype(F32)).astype(BF)


def dot(a, b):
    return jnp.dot(a, b, preferred_element_type=F32)


def kernel(x_hbm, vert_hbm, latf_hbm, lonf_hbm, cb_hbm, ext_hbm, inc_hbm, jump_hbm,
           x, vert, latf, lonf, cb, ext_c, inc, jump,
           xs, so, rw, lx, up, dn, p2, r_w, r_u, r_pw, r_pu, r_p2u, r_p2w,
           vst, vtmp, pm, o1, o2, tl, tmsg, sd, m_l, m_r, sf, mf, cbuf,
           bd, sm, pk, pkp, ys, yz, prev, way, send, recv, load):
    tm, lat, lon = lax.axis_index("tm"), lax.axis_index("lat"), lax.axis_index("lon")
    mu = (lat > 0).astype(F32)
    mw = (lat < NLAT_D - 1).astype(F32)
    mu2 = (lat > 1).astype(F32)
    mw2 = (lat < NLAT_D - 2).astype(F32)

    def at_lat(k):
        return (tm, lax.rem(lat + k + NLAT_D, NLAT_D), lon)

    def at_lon(k):
        return (tm, lat, lax.rem(lon + k + NLON_D, NLON_D))

    across = lat + 1 - 2 * lax.rem(lat, 2)

    def at(window, row):
        return (window, row, lon)

    def at_tm(k):
        return (lax.rem(tm + k + 4, 4), lat, lon)

    partners = [at_lat(k) for k in range(1, 8)] + [at_lon(k) for k in range(1, 4)] + [at_tm(1), at_tm(-1), at(lax.rem(tm + 2, 4), across)]
    barrier = pltpu.get_barrier_semaphore()
    for p in partners:
        pl.semaphore_signal(barrier, inc=1, device_id=p, device_id_type=MESH)

    loads = {}
    for n, (name, src, dst) in enumerate((("x", x_hbm, x), ("cb", cb_hbm, cb), ("ext", ext_hbm, ext_c),
                                          ("lonf", lonf_hbm, lonf), ("latf", latf_hbm, latf),
                                          ("vert", vert_hbm, vert))):
        loads[name] = pltpu.make_async_copy(src, dst, load.at[n])
        loads[name].start()

    def const(key):
        at, k, n = CWHERE[key]
        return cb[at:at + k, 0:n]

    def mm(a, *key):
        hi, lo = split(a)
        w = const(key + ("hi",))
        out = dot(hi, w) + dot(lo, w)
        if key + ("lo",) in CWHERE:
            out = out + dot(hi, const(key + ("lo",)))
        return out

    loads["x"].wait()
    for r in range(ROWS):
        xs[r, 136:144, :] = jnp.zeros((8, COLS), F32)
        xs[r, 0:LEV, :] = x[pl.ds(r, LEV, stride=ROWS), :]

    for i in range(7):
        rw[1 + i] = xs[2 * i + 1] - 0.5 * (xs[2 * i] + xs[2 * i + 2])
    dn[0] = xs[15] - 0.5 * xs[14]
    up[0] = xs[0]
    up[1] = rw[1]

    sems = iter(range(48))

    def remote(src, dst, dev, slot=None):
        k = next(sems)
        return pltpu.make_async_remote_copy(
            src_ref=src, dst_ref=dst, send_sem=send.at[k],
            recv_sem=recv.at[k], device_id=dev, device_id_type=MESH)

    copies = []

    def go(c):
        c.start()
        copies.append(c)

    so[0] = (-0.125 * mu) * xs[0]
    so[1] = 0.875 * xs[0] + 0.25 * rw[1]
    for i in range(1, 7):
        so[1 + i] = xs[2 * i] + 0.25 * (rw[i] + rw[1 + i])
    so[8] = xs[14] + 0.25 * (rw[7] + dn[0])
    so[9] = (0.25 * mw) * dn[0]
    sbase = {1: 0, 2: 10, 3: 17, 4: 22}
    dbase = {2: 26, 3: 32, 4: 36}
    for l in (2, 3, 4):
        m, a, b, d = MLAT[l], sbase[l - 1], sbase[l], dbase[l]
        S = lambda i: so[a + 1 + i]
        so[d] = S(-1) - 0.5 * S(0)
        for i in range(m):
            so[d + 1 + i] = S(2 * i + 1) - 0.5 * (S(2 * i) + S(2 * i + 2))
        so[d + 1 + m] = (-0.5 * S(2 * m)) if l == 2 else S(2 * m + 1) - 0.5 * S(2 * m)
        so[b] = (0.25 * mu) * so[d]
        for i in range(m):
            so[b + 1 + i] = S(2 * i) + 0.25 * (so[d + i] + so[d + 1 + i])
        so[b + 1 + m] = mw * (S(2 * m) + 0.25 * (so[d + m] + so[d + 1 + m]))
        so[b + 2 + m] = (0.25 * mw) * so[d + 1 + m]
    loads["cb"].wait()
    d4 = mm(so[37], "Sm", 4)
    up[2] = mm(so[27], "Sm", 2) + mm(so[33], "Sm", 3) + d4
    dn[1] = mm(so[30], "Sm", 2) + mm(so[34], "Sm", 3) + d4
    p2[0] = mm(so[38], "Sm", 4)
    p2[1] = mm(so[36], "Sm", 4)
    for i in range(1, 7):
        rw[10 + i] = xs[2 * i] + 0.25 * (rw[i] + rw[i + 1])

    lane = lax.broadcasted_iota(jnp.int32, (1, 128), 1)
    def operand(lo, hi):
        if hi <= 19:
            return rw[lo:hi].reshape((hi - lo) * LP, 128)
        return lx[lo - 19:hi - 19].reshape((hi - lo) * LP, 256)

    def message(n, groups):
        for lo, hi in groups:
            tmsg[0:hi - lo, :, 0:128] = mm(operand(lo, hi), "G", n, LEVEL_OF[lo][0]).reshape(hi - lo, LP, 128)
            v = jnp.zeros((LP, 128), F32) if lo == groups[0][0] else sd[n]
            for j in range(lo, hi):
                (a, na), (b, nb) = LEFT[j], RIGHT[j]
                keep = ((lane >= a) & (lane < a + len(na))) | ((lane >= b) & (lane < b + len(nb)))
                v = jnp.where(keep, tmsg[j - lo, :, 0:128], v)
            sd[n] = v

    def post(n):
        out = [remote(sd.at[n], m_l.at[n], at_lon(1)), remote(sd.at[n], m_r.at[n], at_lon(-1))]
        for c in out:
            c.start()
        return out

    message(0, INNER)
    pl.semaphore_wait(barrier, len(partners))
    bulk = [remote(up.at[pl.ds(0, 2)], r_w, at_lat(-1)), remote(dn.at[0], r_u, at_lat(1))]
    for c in bulk:
        c.start()
    lon0 = post(0)
    go(remote(up.at[2], r_pw, at_lat(-1)))
    go(remote(dn.at[1], r_pu, at_lat(1)))
    go(remote(p2.at[0], r_p2u, at_lat(2)))
    go(remote(p2.at[1], r_p2w, at_lat(-2)))
    packs = copies[:]
    copies.clear()

    for name in ("ext", "lonf", "latf", "vert"):
        loads[name].wait()
    vtmp[...] = jnp.zeros((LP, 256), F32)
    for k in range(BANDS):
        vtmp[0:LEV, 0:LEV] = vert[k]
        hi, lo = split(vtmp[...])
        vst[k, 0:LP, :] = hi
        vst[k, LP:2 * LP, :] = lo
    rowi = lax.broadcasted_iota(jnp.int32, (128, 32), 0)
    coli = lax.broadcasted_iota(jnp.int32, (128, 32), 1)
    mine = ((rowi < 11) & (coli == lax.rem(8 * lon + 31 + rowi, 32))).astype(F32)
    for k in range(NLON_D):
        theirs = (rowi < FOLD_LANES) & (coli == lax.rem(8 * (lon + k) + lax.rem(rowi, WIDE), 32))
        part = jnp.dot(theirs.astype(F32), lonf[...], precision=HIGH, preferred_element_type=F32)
        part = lax.dot_general(mine, part, (((1,), (1,)), ((), ())), precision=HIGH,
                               preferred_element_type=F32)
        c4 = const(("C4", 0, "hi")).astype(F32) + const(("C4", 0, "lo")).astype(F32)
        hi, lo = split(jnp.dot(c4, part, precision=HIGH, preferred_element_type=F32))
        pm[0, :, k * 128:(k + 1) * 128] = hi
        pm[1, :, k * 128:(k + 1) * 128] = lo

    low = lane < 64
    def vmul(ks, t):
        hi, lo = split(t)
        both = jnp.concatenate([hi, lo], axis=1)
        outs = []
        for k in ks:
            p = dot(vst[k][:, 0:LP], both)
            outs.append(p[0:LP, 0:128] + p[0:LP, 128:256] + p[LP:2 * LP, 0:128])
        return outs

    def settle(n):
        got = jnp.where(lane < BORDER[n], m_l[n], m_r[n])
        for k, js in users(n).items():
            hi, lo = split(vmul((k,), got)[0])
            both = jnp.concatenate([hi, lo], axis=1)
            for c in range((len(js) + 1) // 2):
                z = const(("Z", n, k, c, "hi"))
                p = dot(both, jnp.concatenate([z, z], axis=0))
                for h, j in enumerate(js[2 * c:2 * c + 2]):
                    at = j + 42 if k == 1 else j
                    bd[at] = bd[at] + p[:, 128 * h:128 * h + 128]

    def own_part(lo, hi):
        if lo < 10:
            o1[lo:hi] = mm(operand(lo, hi), "W", 1).reshape(hi - lo, LP, 256)
        else:
            h, l = split(operand(lo, hi))
            w = const(("W", 1, "hi"))[:, 128:256]
            o1[lo:hi, :, 128:256] = (dot(h, w) + dot(l, w)).reshape(hi - lo, LP, 128)

    def bands1(js):
        for j in js:
            if j < 10:
                bd[42 + j] = vmul((1,), o1[j, :, 0:128])[0]
                bd[j] = vmul((2,), o1[j, :, 128:256])[0]
            else:
                bd[j] = vmul((0,), o1[j, :, 128:256])[0]

    def bands(l):
        lo, hi = COARSER[l - 2]
        o2[lo - 19:hi - 19] = mm(operand(lo, hi), "W", l).reshape(hi - lo, LP, 128)
        for j in range(lo, hi):
            if LEVEL_OF[j][1] == "D":
                a, b = vmul((3 * l - 2, 3 * l - 1), o2[j - 19])
                bd[j] = jnp.where(low, a, b)
            else:
                bd[j] = jnp.where(low, 0.0, vmul((3 * l - 3,), o2[j - 19])[0])

    def even(i):
        tl[2 * i, :, 0:128] = -0.25 * (bd[42 + i] + bd[43 + i])
        tl[2 * i, :, 128:256] = bd[10 + i] - 0.25 * (bd[i] + bd[i + 1])

    def odd(i):
        tl[2 * i + 1, :, 0:128] = bd[43 + i] + 0.5 * (tl[2 * i, :, 0:128] + tl[2 * i + 2, :, 0:128])
        tl[2 * i + 1, :, 128:256] = bd[1 + i] + 0.5 * (tl[2 * i, :, 128:256] + tl[2 * i + 2, :, 128:256])

    def level1(lo, hi):
        ys[lo:hi] = mm(tl[lo:hi].reshape((hi - lo) * LP, 256), "T", 1).reshape(hi - lo, LP, 128)

    def to_next(src, dst):
        c = remote(src, dst, at_tm(1))

        @pl.when(tm < 3)
        def _():
            c.start()

        return c

    @pl.when(tm == 0)
    def _():
        prev[...] = jnp.zeros((ROWS, LP, 128), F32)
        pkp[...] = jnp.zeros((5, LP, 128), F32)

    for lo, hi in INNER:
        own_part(lo, hi)
    bands1(MESSAGES[0])
    for c in lon0:
        c.wait()
    settle(0)
    for i in range(1, 7):
        even(i)
    for i in range(1, 6):
        odd(i)
    level1(2, 13)
    shift = [to_next(ys.at[pl.ds(2, 7)], prev.at[pl.ds(2, 7)])]
    straight = remote(ys.at[pl.ds(9, 4)], prev.at[pl.ds(9, 4)], at_tm(1))
    hops = []
    for q in range(2):
        mine, kept, there = ys.at[pl.ds(9 + 2 * q, 2)], way.at[pl.ds(2 * q, 2)], prev.at[pl.ds(9 + 2 * q, 2)]
        hops.append((remote(mine, kept, at(3, across)), remote(kept, kept, at(0, lat)),
                     remote(kept, there, at(2, across))))

    @pl.when((tm == 0) | (tm == 2))
    def _():
        straight.start()

    @pl.when(tm == 1)
    def _():
        for q in range(2):
            hops[q][0].start()

    def forward(window, hop):
        @pl.when(tm == window)
        def _():
            for q in range(2):
                hops[q][hop].wait_recv()
                hops[q][hop + 1].start()

    for c in bulk:
        c.wait()
    x16 = lambda: mw * r_w[0]
    rw[0] = mu * r_u[...] - 0.5 * xs[0]
    rw[8] = dn[0] - 0.5 * x16()
    rw[9] = mw * r_w[1]
    rw[10] = xs[0] + 0.25 * (rw[0] + rw[1])
    rw[17] = xs[14] + 0.25 * (rw[7] + rw[8])
    rw[18] = x16() + (0.25 * mw) * (rw[8] + rw[9])
    rw[0] = mu * rw[0]
    message(1, OUTER)
    lon1 = post(1)
    for lo, hi in OUTER:
        own_part(lo, hi)
    bands1(MESSAGES[1])

    for c in packs:
        c.wait()
    raw = lambda j: rw[j] if j < 19 else lx[j - 19, :, 0:128]
    for l in (2, 3, 4):
        m, a, d, b = MLAT[l], SROW[l - 1], DROW[l], SROW[l]
        lx[d - 19, :, 0:128] = so[dbase[l]]
        lx[d + m + 1 - 19, :, 0:128] = so[dbase[l] + m + 1]
        for i in range(m):
            lx[d + 1 + i - 19, :, 0:128] = raw(a + 2 * i + 1) - 0.5 * (raw(a + 2 * i) + raw(a + 2 * i + 2))
        for i in range(m + 1):
            v = raw(a + 2 * i) + 0.25 * (raw(d + i) + raw(d + i + 1))
            lx[b + i - 19, :, 0:128] = mw * v if i == m else v
    r_pu[...] = mu * r_pu[...] + mu2 * r_p2u[...]
    r_pw[...] = mw * r_pw[...] + mw2 * r_p2w[...]
    for j in range(19, NROWS):
        cu, cw = ext_c[j - 19:j - 18, :], ext_c[24 + j - 19:24 + j - 18, :]
        l, kind, i = LEVEL_OF[j]
        if kind == "S" and i == MLAT[l]:
            cu, cw = cu * mw, cw * mw
        lx[j - 19, :, 128:256] = r_pu[...] * cu + r_pw[...] * cw
    for l in (2, 3, 4):
        lx[DROW[l] - 19] = mu * lx[DROW[l] - 19]

    hi, lo = split(lx[SROW[4] - 19])
    fold = dot(hi, pm[0]) + dot(lo, pm[0]) + dot(hi, pm[1])
    for k in range(NLON_D):
        acc = jnp.zeros((FOLD, 128), F32)
        for g in range(LP // FOLD):
            acc = jnp.where((lane >= g * WIDE) & (lane < (g + 1) * WIDE),
                            fold[g * FOLD:(g + 1) * FOLD, k * 128:(k + 1) * 128], acc)
        sf[k] = acc
    for k in range(1, NLON_D):
        go(remote(sf.at[k], mf.at[k], at_lon(k)))
    coarse = copies[:]
    copies.clear()

    message(2, COARSER)
    lon2 = post(2)
    bands(4)
    bands(3)

    forward(3, 0)

    for c in coarse:
        c.wait()
    row = sf[0] + mf[1] + mf[2] + mf[3]
    sf[0] = row
    cbuf[lat] = row
    for k in range(1, NLAT_D):
        go(remote(sf.at[0], cbuf.at[lat], at_lat(k)))
    coarse = copies[:]
    copies.clear()

    for c in lon1:
        c.wait()
    settle(1)
    for i in (0, 7, 8):
        even(i)
    for i in (0, 6, 7):
        odd(i)
    level1(0, 2)
    level1(13, 16)
    shift.append(to_next(ys.at[pl.ds(0, 2)], prev.at[pl.ds(0, 2)]))
    shift.append(to_next(ys.at[pl.ds(13, 3)], prev.at[pl.ds(13, 3)]))
    bands(2)
    for c in lon2:
        c.wait()
    settle(2)
    forward(0, 1)

    for c in coarse:
        c.wait()
    for rho in range(2):
        w = latf[pl.ds(jnp.minimum(lat + rho, NLAT_D - 1), 1), :]
        t = sum(cbuf[a] * w[:, a:a + 1] for a in range(NLAT_D))
        parts = [t if g == 0 else pltpu.roll(t, 128 - WIDE * g, 1) for g in range(LP // FOLD)]
        c = jnp.where(lane < WIDE, jnp.concatenate(parts, axis=0), 0.0)
        v = vmul((BANDS - 1,), c)[0]
        sm[rho] = v * mw if rho else v

    for l in (4, 3, 2):
        m, d, b = MLAT[l], DROW[l], SROW[l]
        for i in range(m + 1):
            s = bd[b + i] + sm[i]
            sm[i] = s - 0.25 * (bd[d + i] + bd[d + i + 1])
        for i in range(2 * m, -1, -1):
            if i % 2:
                h = i // 2
                tmsg[i, :, 0:128] = bd[d + 1 + h] + 0.5 * (sm[h] + sm[h + 1])
            else:
                tmsg[i, :, 0:128] = sm[i // 2]
        n = 2 * m + 1
        out = mm(tmsg[0:n, :, 0:128].reshape(n * LP, 128), "T", l).reshape(n, LP, 128)
        sm[0:n] = out
        sm[2 * m] = mw * sm[2 * m]

    last = sm[8]
    for k in range(9):
        last = jnp.where(lane == 64 + k, sm[k] if k == 0 else pltpu.roll(sm[k], k, 1), last)
    for k in range(4):
        pk[k] = jnp.where(low, sm[k], pltpu.roll(sm[k + 4], 64, 1))
    pk[4] = last
    shift.append(to_next(pk, pkp))

    def lifted(rows):
        w = const(("T", 1, "hi"))[0:128]
        for i in range(8):
            tmsg[2 * i, :, 0:128] = rows[i]
            tmsg[2 * i + 1, :, 0:128] = 0.5 * (rows[i] + rows[i + 1])
        h, l = split(tmsg[0:16, :, 0:128].reshape(16 * LP, 128))
        return (dot(h, w) + dot(l, w)).reshape(ROWS, LP, 128)

    yz[...] = ys[...] + lifted(sm)
    for r in range(ROWS):
        inc[pl.ds(r, LEV, stride=ROWS), :] = yz[r, 0:LEV, :]
    out = pltpu.make_async_copy(inc, inc_hbm, load.at[6])
    out.start()

    def land(cs):
        for c in cs:
            pl.when(tm > 0)(c.wait_recv)

    land(shift[:3])
    pl.when((tm == 1) | (tm == 3))(straight.wait_recv)

    @pl.when(tm == 2)
    def _():
        for q in range(2):
            hops[q][2].wait_recv()

    yz[...] = yz[...] - prev[...]
    land(shift[3:])
    for k in range(9):
        part = pkp[k % 4] if k < 8 else pkp[4]
        if 4 <= k < 8:
            part = pltpu.roll(part, 64, 1)
        end = pkp[4] if k == 0 else pltpu.roll(pkp[4], 128 - k, 1)
        sm[k] = jnp.where(lane == 64, end, part)
    yz[...] = yz[...] - lifted(sm)
    for r in range(ROWS):
        jump[pl.ds(r, LEV, stride=ROWS), :] = yz[r, 0:LEV, :]
    out2 = pltpu.make_async_copy(jump, jump_hbm, load.at[7])
    out2.start()
    for c in shift:
        pl.when(tm < 3)(c.wait_send)
    pl.when((tm == 0) | (tm == 2))(straight.wait_send)
    for window, hop in ((1, 0), (3, 1), (0, 2)):
        @pl.when(tm == window)
        def _(hop=hop):
            for q in range(2):
                hops[q][hop].wait_send()

    out.wait()
    out2.wait()


def body(forcing, vertical, lat_factor, lon_factor):
    x = forcing.reshape(LEV * ROWS, COLS)
    tile = (LP, 128)
    anywhere = pl.BlockSpec(memory_space=pl.ANY)
    S = pltpu.VMEM
    flat = (LEV * ROWS, COLS)
    scratch = [
        S(flat, F32), S((BANDS, LEV, LEV), F32), S((8, 8), F32), S((32, 32), F32), S(CB.shape, BF), S(EXT.shape, F32),
        S(flat, F32), S(flat, F32),
        S((ROWS,) + tile, F32), S((39,) + tile, F32), S((19,) + tile, F32), S((23, LP, 256), F32),
        S((3,) + tile, F32), S((2,) + tile, F32), S((2,) + tile, F32),
        S((2,) + tile, F32), S(tile, F32), S(tile, F32), S(tile, F32), S(tile, F32), S(tile, F32),
        S((BANDS, 2 * LP, 256), BF), S((LP, 256), F32), S((2, 256, 512), BF),
        S((19, LP, 256), F32), S((23,) + tile, F32), S((17, LP, 256), F32), S((19, LP, 256), F32),
        S((3,) + tile, F32), S((3,) + tile, F32), S((3,) + tile, F32),
        S((4, FOLD, 128), F32), S((4, FOLD, 128), F32), S((8, FOLD, 128), F32),
        S((52,) + tile, F32), S((9,) + tile, F32), S((5,) + tile, F32), S((5,) + tile, F32),
        S((ROWS,) + tile, F32), S((ROWS,) + tile, F32), S((ROWS,) + tile, F32), S((4,) + tile, F32),
        pltpu.SemaphoreType.DMA((48,)), pltpu.SemaphoreType.DMA((48,)), pltpu.SemaphoreType.DMA((8,)),
    ]
    out = jax.ShapeDtypeStruct((LEV * ROWS, COLS), F32)
    inc, jump = pl.pallas_call(
        kernel,
        out_shape=(out, out),
        in_specs=[anywhere] * 6,
        out_specs=(anywhere, anywhere),
        scratch_shapes=scratch,
        compiler_params=pltpu.CompilerParams(
            collective_id=0, has_side_effects=True, vmem_limit_bytes=56 * 1024 * 1024),
    )(x, vertical, lat_factor, lon_factor, jnp.asarray(CB), jnp.asarray(EXT))

    def settle(a, b, c, d, held, arrive, leave):
        size = LEV * ROWS // 2
        moves = []
        for k in range(2):
            for h, (src, dst) in enumerate(((a, c), (b, d))):
                part = pl.ds(k * size, size)
                moves.append((pltpu.make_async_copy(src.at[part], held.at[h, part], arrive.at[2 * k + h]),
                              pltpu.make_async_copy(held.at[h, part], dst.at[part], leave.at[2 * k + h])))
        for m, _ in moves:
            m.start()
        for m, o in moves:
            m.wait()
            o.start()
        for _, o in moves:
            o.wait()

    inc, jump = pl.pallas_call(
        settle, out_shape=(out, out), in_specs=[anywhere] * 2, out_specs=(anywhere, anywhere),
        scratch_shapes=[S((2,) + flat, F32), pltpu.SemaphoreType.DMA((4,)), pltpu.SemaphoreType.DMA((4,))],
    )(inc, jump)
    shape = (1, LEV, ROWS, COLS)
    return inc.reshape(shape), jump.reshape(shape)


def solution(mesh):
    placed = (P("tm", None, "lat", "lon"), P(), P(), P())
    return jax.shard_map(
        body,
        mesh=mesh,
        in_specs=placed,
        out_specs=(P("tm", None, "lat", "lon"), P("tm", None, "lat", "lon")),
        check_vma=False,
    )
```

```python
import numpy as np
import jax
import jax.numpy as jnp
import ml_dtypes
from jax import lax
from jax.experimental import pallas as pl
from jax.experimental.pallas import tpu as pltpu
from jax.sharding import PartitionSpec as P

LEV, LP = 137, 144
ROWS, COLS = 16, 128
BANDS = 13
NLAT_D, NLON_D = 8, 4
MESH = pl.DeviceIdType.MESH
HIGH = lax.Precision.HIGHEST
F32, BF = jnp.float32, jnp.bfloat16

MLAT = {1: 8, 2: 4, 3: 2, 4: 1}
MLON = {1: 64, 2: 32, 3: 16, 4: 8}
DROW = {1: 0, 2: 19, 3: 30, 4: 37}
SROW = {1: 10, 2: 25, 3: 34, 4: 40}
NROWS = 42
PACK = {2: (0, 1, -1, 64), 3: (66, 2, -1, 33), 4: (101, 3, -1, 17)}
FOLD, WIDE = 16, 9
FOLD_LANES = LP // FOLD * WIDE
LEVEL_OF = {}
for _l in (1, 2, 3, 4):
    for _i in range(MLAT[_l] + 2):
        LEVEL_OF[DROW[_l] + _i] = (_l, "D", _i - 1)
    for _i in range(MLAT[_l] + 1):
        LEVEL_OF[SROW[_l] + _i] = (_l, "S", _i)


def lift(seq, size):
    lo, hi = min(seq), max(seq)
    zero = np.zeros(size)
    get = lambda table, i: table.get(i, zero)
    d, s = {}, {}
    for i in range(lo // 2 - 2, hi // 2 + 3):
        d[i] = get(seq, 2 * i + 1) - 0.5 * (get(seq, 2 * i) + get(seq, 2 * i + 2))
    for i in range(lo // 2 - 2, hi // 2 + 3):
        s[i] = get(seq, 2 * i) + 0.25 * (get(d, i - 1) + get(d, i))
    keep = lambda table: {i: v for i, v in table.items() if np.any(v)}
    return keep(s), keep(d)


INNER, OUTER = ((1, 8), (11, 17)), ((0, 1), (8, 11), (17, 19))
COARSER = ((19, 30), (30, 37), (37, 42))
MESSAGES = [[j for lo, hi in part for j in range(lo, hi)] for part in (INNER, OUTER, COARSER)]


def message_lanes():
    left, right, border = {}, {}, []
    for rows in MESSAGES:
        n = 0
        for table in (left, right):
            for j in rows:
                l, kind, _ = LEVEL_OF[j]
                if table is left:
                    names = ["dm1"] if l == 1 else (["sm", "dm1", "dm"] if kind == "D" else ["dm1", "dm"])
                else:
                    names = ["d-1", "d0"] if (l == 1 or kind == "S") else ["s0", "d-1", "d0"]
                table[j] = (n, names)
                n += len(names)
            if table is left:
                border.append(n)
        assert n <= 128
    return left, right, border


LEFT, RIGHT, BORDER = message_lanes()


def users(n):
    table = {}
    for j in MESSAGES[n]:
        l, kind, _ = LEVEL_OF[j]
        for k in ((3 * l - 2, 3 * l - 1) if kind == "D" else (3 * l - 3,)):
            table.setdefault(k, []).append(j)
    return table


def lon_tables():
    raw = {i: np.eye(256)[i] for i in range(COLS)}
    smooth, detail = {0: raw}, {}
    for l in range(1, 5):
        smooth[l], detail[l] = lift(smooth[l - 1], 256)
    ext_s = {}
    for l in (2, 3, 4):
        at, depth, lo, hi = PACK[l]
        seq = {i: np.eye(256)[128 + at + i - lo] for i in range(lo, hi + 1)}
        for k in range(l, 5):
            s, d = lift(seq, 256)
            seq = s
            ext_s[l, k] = (s, d)
    zero = np.zeros(256)
    full_s, full_d = {}, {}
    for k in range(1, 5):
        s, d = dict(smooth[k]), dict(detail[k])
        for l in range(2, k + 1):
            for table, more in ((s, ext_s[l, k][0]), (d, ext_s[l, k][1])):
                for i, v in more.items():
                    table[i] = table.get(i, zero) + v
        full_s[k], full_d[k] = s, d
    return smooth, full_s, full_d


def constants():
    smooth, fs, fd = lon_tables()
    zero = np.zeros(256)
    out = {}
    for l in (1, 2, 3, 4):
        m = MLON[l]
        w = np.zeros((256, 256))
        off = 128 if l == 1 else 64
        for i in range(0, m + 1):
            w[:, i] = fs[l].get(i, zero)
        for i in range(-1, m + 1):
            w[:, off + i + 1] = fd[l].get(i, zero)
        out["W", l] = w if l == 1 else w[:, :128]
        pick = {"sm": fs[l].get(m, zero), "dm1": fd[l].get(m - 1, zero), "dm": fd[l].get(m, zero),
                "s0": fs[l].get(0, zero), "d-1": fd[l].get(-1, zero), "d0": fd[l].get(0, zero)}
        for n, rows in enumerate(MESSAGES):
            rows = [j for j in rows if LEVEL_OF[j][0] == l]
            if not rows:
                continue
            g = np.zeros((256, 128))
            for j in rows:
                for at, names in (LEFT[j], RIGHT[j]):
                    for q, name in enumerate(names):
                        g[:, at + q] = pick[name]
            out["G", n, l] = g
            for k, js in users(n).items():
                if k // 3 != l - 1:
                    continue
                kind = k % 3
                z = np.zeros((128, 256 * ((len(js) + 1) // 2)))
                for p, j in enumerate(js):
                    smooths = np.zeros((128, 128))
                    details = np.zeros((128, 128))
                    at, names = LEFT[j]
                    for q, name in enumerate(names):
                        if name == "dm1":
                            details[at + q, 0] += 1.0
                            if l == 1:
                                smooths[at + q, 0] += 0.25
                        if name == "dm":
                            details[at + q, 1] += 1.0
                            smooths[at + q, 1] += 0.25
                        if name == "sm":
                            smooths[at + q, 0] += 1.0
                    at, names = RIGHT[j]
                    for q, name in enumerate(names):
                        if name == "s0":
                            smooths[at + q, m] += 1.0
                        if name == "d-1":
                            details[at + q, m] += 1.0
                            smooths[at + q, m - 1] += 0.25
                            if l == 1:
                                smooths[at + q, m] += -1.75
                        if name == "d0":
                            details[at + q, m + 1] += 1.0
                            if l == 1:
                                smooths[at + q, m] += 0.25
                    if l > 1:
                        details = np.roll(details, 64, axis=1)
                    z[:, 128 * p:128 * p + 128] = smooths if kind == 1 else details
                for c in range(0, z.shape[1], 256):
                    out["Z", n, k, c // 256] = z[:, c:c + 256]
        n_in = 256 if l == 1 else 128
        eye = np.eye(n_in)
        s = {i: eye[i] for i in range(0, m + 1)}
        d = {i: eye[off + i + 1] for i in range(-1, m + 1)}
        e = {i: s[i] - 0.25 * (d[i - 1] + d[i]) for i in range(0, m + 1)}
        t = np.zeros((n_in, 128))
        for i in range(0, m + 1):
            if 2 * i < 128:
                t[:, 2 * i] = e[i]
            if i < m:
                t[:, 2 * i + 1] = d[i] + 0.5 * (e[i] + e[i + 1])
        out["T", l] = t
    for l in (2, 3, 4):
        at, depth, lo, hi = PACK[l]
        sm = np.zeros((128, 128))
        for i in range(lo, hi + 1):
            sm[:, at + i - lo] = smooth[depth][i][:128]
        out["Sm", l] = sm
    c4 = np.zeros((256, 128))
    for c in range(11):
        c4[:, c] = fs[4].get(c - 1, zero)
    out["C4", 0] = c4
    return out


CONST = constants()


def pack_constants():
    tiles, where = [], {}

    def put(key, a):
        k, n = a.shape
        where[key] = (sum(t.shape[0] for t in tiles), k, n)
        if n < 256:
            a = np.concatenate([a, np.zeros((k, 256 - n), a.dtype)], 1)
        tiles.append(a)

    for key, a in CONST.items():
        if key == ("W", 1) or (key[0] == "G" and key[2] == 1):
            a = a[:128]
        hi = a.astype(ml_dtypes.bfloat16)
        lo = (a - hi.astype(np.float64)).astype(ml_dtypes.bfloat16)
        put(key + ("hi",), hi)
        if np.any(lo.astype(np.float64)):
            put(key + ("lo",), lo)
    return np.concatenate(tiles, 0), where


CB, CWHERE = pack_constants()


def ext_coefficients():
    syms = {("U", 2): 0, ("U", 3): 1, ("U", 4): 2, ("W", 2): 3, ("W", 3): 4, ("W", 4): 5}
    unit = lambda key: np.eye(6)[syms[key]]
    zero = np.zeros(6)
    s = {i: zero for i in range(9)}
    table = {}
    for l in (2, 3, 4):
        m = MLAT[l]
        d = {-1: unit(("U", l)), m: unit(("W", l))}
        for i in range(m):
            d[i] = s[2 * i + 1] - 0.5 * (s[2 * i] + s[2 * i + 2])
        s = {i: s[2 * i] + 0.25 * (d[i - 1] + d[i]) for i in range(m + 1)}
        for i in range(-1, m + 1):
            table[DROW[l] + i + 1] = d[i]
        for i in range(m + 1):
            table[SROW[l] + i] = s[i]
    out = np.zeros((48, 128), np.float32)
    for j, v in table.items():
        for l in (2, 3, 4):
            at, _, lo, hi = PACK[l]
            out[j - 19, at:at + hi - lo + 1] = v[l - 2]
            out[24 + j - 19, at:at + hi - lo + 1] = v[3 + l - 2]
    return out


EXT = ext_coefficients()


def split(a):
    hi = a.astype(BF)
    return hi, (a - hi.astype(F32)).astype(BF)


def dot(a, b):
    return jnp.dot(a, b, preferred_element_type=F32)


def kernel(x_hbm, vert_hbm, latf_hbm, lonf_hbm, cb_hbm, ext_hbm, inc_hbm, yz_hbm, pk_hbm,
           x, vert, latf, lonf, cb, ext_c, inc,
           xs, so, rw, lx, up, dn, p2, r_w, r_u, r_pw, r_pu, r_p2u, r_p2w,
           vst, vtmp, pm, o1, o2, tl, tmsg, sd, m_l, m_r, sf, mf, cbuf,
           bd, sm, smc, pk, fo, fop, ys, yz, prev, way, send, recv, load):
    tm, lat, lon = lax.axis_index("tm"), lax.axis_index("lat"), lax.axis_index("lon")
    mu = (lat > 0).astype(F32)
    mw = (lat < NLAT_D - 1).astype(F32)
    mu2 = (lat > 1).astype(F32)
    mw2 = (lat < NLAT_D - 2).astype(F32)

    def at_lat(k):
        return (tm, lax.rem(lat + k + NLAT_D, NLAT_D), lon)

    def at_lon(k):
        return (tm, lat, lax.rem(lon + k + NLON_D, NLON_D))

    across = lat + 1 - 2 * lax.rem(lat, 2)

    def at(window, row):
        return (window, row, lon)

    def at_tm(k):
        return (lax.rem(tm + k + 4, 4), lat, lon)

    partners = [at_lat(k) for k in range(1, 8)] + [at_lon(k) for k in range(1, 4)] + [at_tm(1), at_tm(-1), at(lax.rem(tm + 2, 4), across)]
    barrier = pltpu.get_barrier_semaphore()
    for p in partners:
        pl.semaphore_signal(barrier, inc=1, device_id=p, device_id_type=MESH)

    loads = {}
    for n, (name, src, dst) in enumerate((("x", x_hbm, x), ("cb", cb_hbm, cb), ("ext", ext_hbm, ext_c),
                                          ("lonf", lonf_hbm, lonf), ("latf", latf_hbm, latf),
                                          ("vert", vert_hbm, vert))):
        loads[name] = pltpu.make_async_copy(src, dst, load.at[n])
        loads[name].start()

    def const(key):
        at, k, n = CWHERE[key]
        return cb[at:at + k, 0:n]

    def mm(a, *key):
        hi, lo = split(a)
        w = const(key + ("hi",))
        out = dot(hi, w) + dot(lo, w)
        if key + ("lo",) in CWHERE:
            out = out + dot(hi, const(key + ("lo",)))
        return out

    loads["x"].wait()
    for r in range(ROWS):
        xs[r, 136:144, :] = jnp.zeros((8, COLS), F32)
        xs[r, 0:LEV, :] = x[pl.ds(r, LEV, stride=ROWS), :]

    for i in range(7):
        rw[1 + i] = xs[2 * i + 1] - 0.5 * (xs[2 * i] + xs[2 * i + 2])
    dn[0] = xs[15] - 0.5 * xs[14]
    up[0] = xs[0]
    up[1] = rw[1]

    sems = iter(range(48))

    def remote(src, dst, dev, slot=None):
        k = next(sems)
        return pltpu.make_async_remote_copy(
            src_ref=src, dst_ref=dst, send_sem=send.at[k],
            recv_sem=recv.at[k], device_id=dev, device_id_type=MESH)

    copies = []

    def go(c):
        c.start()
        copies.append(c)

    so[0] = (-0.125 * mu) * xs[0]
    so[1] = 0.875 * xs[0] + 0.25 * rw[1]
    for i in range(1, 7):
        so[1 + i] = xs[2 * i] + 0.25 * (rw[i] + rw[1 + i])
    so[8] = xs[14] + 0.25 * (rw[7] + dn[0])
    so[9] = (0.25 * mw) * dn[0]
    sbase = {1: 0, 2: 10, 3: 17, 4: 22}
    dbase = {2: 26, 3: 32, 4: 36}
    for l in (2, 3, 4):
        m, a, b, d = MLAT[l], sbase[l - 1], sbase[l], dbase[l]
        S = lambda i: so[a + 1 + i]
        so[d] = S(-1) - 0.5 * S(0)
        for i in range(m):
            so[d + 1 + i] = S(2 * i + 1) - 0.5 * (S(2 * i) + S(2 * i + 2))
        so[d + 1 + m] = (-0.5 * S(2 * m)) if l == 2 else S(2 * m + 1) - 0.5 * S(2 * m)
        so[b] = (0.25 * mu) * so[d]
        for i in range(m):
            so[b + 1 + i] = S(2 * i) + 0.25 * (so[d + i] + so[d + 1 + i])
        so[b + 1 + m] = mw * (S(2 * m) + 0.25 * (so[d + m] + so[d + 1 + m]))
        so[b + 2 + m] = (0.25 * mw) * so[d + 1 + m]
    loads["cb"].wait()
    d4 = mm(so[37], "Sm", 4)
    up[2] = mm(so[27], "Sm", 2) + mm(so[33], "Sm", 3) + d4
    dn[1] = mm(so[30], "Sm", 2) + mm(so[34], "Sm", 3) + d4
    p2[0] = mm(so[38], "Sm", 4)
    p2[1] = mm(so[36], "Sm", 4)
    for i in range(1, 7):
        rw[10 + i] = xs[2 * i] + 0.25 * (rw[i] + rw[i + 1])

    lane = lax.broadcasted_iota(jnp.int32, (1, 128), 1)
    def operand(lo, hi):
        if hi <= 19:
            return rw[lo:hi].reshape((hi - lo) * LP, 128)
        return lx[lo - 19:hi - 19].reshape((hi - lo) * LP, 256)

    def message(n, groups):
        for lo, hi in groups:
            tmsg[0:hi - lo, :, 0:128] = mm(operand(lo, hi), "G", n, LEVEL_OF[lo][0]).reshape(hi - lo, LP, 128)
            v = jnp.zeros((LP, 128), F32) if lo == groups[0][0] else sd[n]
            for j in range(lo, hi):
                (a, na), (b, nb) = LEFT[j], RIGHT[j]
                keep = ((lane >= a) & (lane < a + len(na))) | ((lane >= b) & (lane < b + len(nb)))
                v = jnp.where(keep, tmsg[j - lo, :, 0:128], v)
            sd[n] = v

    def post(n):
        out = [remote(sd.at[n], m_l.at[n], at_lon(1)), remote(sd.at[n], m_r.at[n], at_lon(-1))]
        for c in out:
            c.start()
        return out

    message(0, INNER)
    pl.semaphore_wait(barrier, len(partners))
    bulk = [remote(up.at[pl.ds(0, 2)], r_w, at_lat(-1)), remote(dn.at[0], r_u, at_lat(1))]
    for c in bulk:
        c.start()
    lon0 = post(0)
    go(remote(up.at[2], r_pw, at_lat(-1)))
    go(remote(dn.at[1], r_pu, at_lat(1)))
    go(remote(p2.at[0], r_p2u, at_lat(2)))
    go(remote(p2.at[1], r_p2w, at_lat(-2)))
    packs = copies[:]
    copies.clear()

    for name in ("ext", "lonf", "latf", "vert"):
        loads[name].wait()
    vtmp[...] = jnp.zeros((LP, 256), F32)
    for k in range(BANDS):
        vtmp[0:LEV, 0:LEV] = vert[k]
        hi, lo = split(vtmp[...])
        vst[k, 0:LP, :] = hi
        vst[k, LP:2 * LP, :] = lo
    rowi = lax.broadcasted_iota(jnp.int32, (128, 32), 0)
    coli = lax.broadcasted_iota(jnp.int32, (128, 32), 1)
    mine = ((rowi < 11) & (coli == lax.rem(8 * lon + 31 + rowi, 32))).astype(F32)
    for k in range(NLON_D):
        theirs = (rowi < FOLD_LANES) & (coli == lax.rem(8 * (lon + k) + lax.rem(rowi, WIDE), 32))
        part = jnp.dot(theirs.astype(F32), lonf[...], precision=HIGH, preferred_element_type=F32)
        part = lax.dot_general(mine, part, (((1,), (1,)), ((), ())), precision=HIGH,
                               preferred_element_type=F32)
        c4 = const(("C4", 0, "hi")).astype(F32) + const(("C4", 0, "lo")).astype(F32)
        hi, lo = split(jnp.dot(c4, part, precision=HIGH, preferred_element_type=F32))
        pm[0, :, k * 128:(k + 1) * 128] = hi
        pm[1, :, k * 128:(k + 1) * 128] = lo

    low = lane < 64
    def vmul(ks, t):
        hi, lo = split(t)
        both = jnp.concatenate([hi, lo], axis=1)
        outs = []
        for k in ks:
            p = dot(vst[k][:, 0:LP], both)
            outs.append(p[0:LP, 0:128] + p[0:LP, 128:256] + p[LP:2 * LP, 0:128])
        return outs

    def settle(n):
        got = jnp.where(lane < BORDER[n], m_l[n], m_r[n])
        for k, js in users(n).items():
            hi, lo = split(vmul((k,), got)[0])
            both = jnp.concatenate([hi, lo], axis=1)
            for c in range((len(js) + 1) // 2):
                z = const(("Z", n, k, c, "hi"))
                p = dot(both, jnp.concatenate([z, z], axis=0))
                for h, j in enumerate(js[2 * c:2 * c + 2]):
                    at = j + 42 if k == 1 else j
                    bd[at] = bd[at] + p[:, 128 * h:128 * h + 128]

    def own_part(lo, hi):
        if lo < 10:
            o1[lo:hi] = mm(operand(lo, hi), "W", 1).reshape(hi - lo, LP, 256)
        else:
            h, l = split(operand(lo, hi))
            w = const(("W", 1, "hi"))[:, 128:256]
            o1[lo:hi, :, 128:256] = (dot(h, w) + dot(l, w)).reshape(hi - lo, LP, 128)

    def bands1(js):
        for j in js:
            if j < 10:
                bd[42 + j] = vmul((1,), o1[j, :, 0:128])[0]
                bd[j] = vmul((2,), o1[j, :, 128:256])[0]
            else:
                bd[j] = vmul((0,), o1[j, :, 128:256])[0]

    def bands(l):
        lo, hi = COARSER[l - 2]
        o2[lo - 19:hi - 19] = mm(operand(lo, hi), "W", l).reshape(hi - lo, LP, 128)
        for j in range(lo, hi):
            if LEVEL_OF[j][1] == "D":
                a, b = vmul((3 * l - 2, 3 * l - 1), o2[j - 19])
                bd[j] = jnp.where(low, a, b)
            else:
                bd[j] = jnp.where(low, 0.0, vmul((3 * l - 3,), o2[j - 19])[0])

    def even(i):
        tl[2 * i, :, 0:128] = -0.25 * (bd[42 + i] + bd[43 + i])
        tl[2 * i, :, 128:256] = bd[10 + i] - 0.25 * (bd[i] + bd[i + 1])

    def odd(i):
        tl[2 * i + 1, :, 0:128] = bd[43 + i] + 0.5 * (tl[2 * i, :, 0:128] + tl[2 * i + 2, :, 0:128])
        tl[2 * i + 1, :, 128:256] = bd[1 + i] + 0.5 * (tl[2 * i, :, 128:256] + tl[2 * i + 2, :, 128:256])

    def level1(lo, hi):
        ys[lo:hi] = mm(tl[lo:hi].reshape((hi - lo) * LP, 256), "T", 1).reshape(hi - lo, LP, 128)

    def to_next(src, dst):
        c = remote(src, dst, at_tm(1))

        @pl.when(tm < 3)
        def _():
            c.start()

        return c

    @pl.when(tm == 0)
    def _():
        prev[...] = jnp.zeros((ROWS, LP, 128), F32)
        fop[...] = jnp.zeros((2, FOLD, 128), F32)
        pk[...] = jnp.zeros((5, LP, 128), F32)
        blank = pltpu.make_async_copy(pk, pk_hbm, load.at[7])
        blank.start()
        blank.wait()

    for lo, hi in INNER:
        own_part(lo, hi)
    bands1(MESSAGES[0])
    for c in lon0:
        c.wait()
    settle(0)
    for i in range(1, 7):
        even(i)
    for i in range(1, 6):
        odd(i)
    level1(2, 13)
    for c in bulk:
        c.wait()
    x16 = lambda: mw * r_w[0]
    rw[0] = mu * r_u[...] - 0.5 * xs[0]
    rw[8] = dn[0] - 0.5 * x16()
    rw[9] = mw * r_w[1]
    rw[10] = xs[0] + 0.25 * (rw[0] + rw[1])
    rw[17] = xs[14] + 0.25 * (rw[7] + rw[8])
    rw[18] = x16() + (0.25 * mw) * (rw[8] + rw[9])
    rw[0] = mu * rw[0]
    message(1, OUTER)
    lon1 = post(1)
    for lo, hi in OUTER:
        own_part(lo, hi)
    bands1(MESSAGES[1])

    for c in packs:
        c.wait()

    shift = [to_next(ys.at[pl.ds(2, 7)], prev.at[pl.ds(2, 7)])]
    straight = remote(ys.at[pl.ds(9, 4)], prev.at[pl.ds(9, 4)], at_tm(1))
    hops = []
    for q in range(2):
        mine, kept, there = ys.at[pl.ds(9 + 2 * q, 2)], way.at[pl.ds(2 * q, 2)], prev.at[pl.ds(9 + 2 * q, 2)]
        hops.append((remote(mine, kept, at(3, across)), remote(kept, kept, at(0, lat)),
                     remote(kept, there, at(2, across))))

    @pl.when((tm == 0) | (tm == 2))
    def _():
        straight.start()

    @pl.when(tm == 1)
    def _():
        for q in range(2):
            hops[q][0].start()

    def forward(window, hop):
        @pl.when(tm == window)
        def _():
            for q in range(2):
                hops[q][hop].wait_recv()
                hops[q][hop + 1].start()

    raw = lambda j: rw[j] if j < 19 else lx[j - 19, :, 0:128]
    for l in (2, 3, 4):
        m, a, d, b = MLAT[l], SROW[l - 1], DROW[l], SROW[l]
        lx[d - 19, :, 0:128] = so[dbase[l]]
        lx[d + m + 1 - 19, :, 0:128] = so[dbase[l] + m + 1]
        for i in range(m):
            lx[d + 1 + i - 19, :, 0:128] = raw(a + 2 * i + 1) - 0.5 * (raw(a + 2 * i) + raw(a + 2 * i + 2))
        for i in range(m + 1):
            v = raw(a + 2 * i) + 0.25 * (raw(d + i) + raw(d + i + 1))
            lx[b + i - 19, :, 0:128] = mw * v if i == m else v
    r_pu[...] = mu * r_pu[...] + mu2 * r_p2u[...]
    r_pw[...] = mw * r_pw[...] + mw2 * r_p2w[...]
    for j in range(19, NROWS):
        cu, cw = ext_c[j - 19:j - 18, :], ext_c[24 + j - 19:24 + j - 18, :]
        l, kind, i = LEVEL_OF[j]
        if kind == "S" and i == MLAT[l]:
            cu, cw = cu * mw, cw * mw
        lx[j - 19, :, 128:256] = r_pu[...] * cu + r_pw[...] * cw
    for l in (2, 3, 4):
        lx[DROW[l] - 19] = mu * lx[DROW[l] - 19]

    hi, lo = split(lx[SROW[4] - 19])
    fold = dot(hi, pm[0]) + dot(lo, pm[0]) + dot(hi, pm[1])
    for k in range(NLON_D):
        acc = jnp.zeros((FOLD, 128), F32)
        for g in range(LP // FOLD):
            acc = jnp.where((lane >= g * WIDE) & (lane < (g + 1) * WIDE),
                            fold[g * FOLD:(g + 1) * FOLD, k * 128:(k + 1) * 128], acc)
        sf[k] = acc
    for k in range(1, NLON_D):
        go(remote(sf.at[k], mf.at[k], at_lon(k)))
    coarse = copies[:]
    copies.clear()

    message(2, COARSER)
    lon2 = post(2)
    bands(4)
    bands(3)

    forward(3, 0)

    for c in coarse:
        c.wait()
    row = sf[0] + mf[1] + mf[2] + mf[3]
    sf[0] = row
    cbuf[lat] = row
    for k in range(1, NLAT_D):
        go(remote(sf.at[0], cbuf.at[lat], at_lat(k)))
    coarse = copies[:]
    copies.clear()

    for c in lon1:
        c.wait()
    settle(1)
    for i in (0, 7, 8):
        even(i)
    for i in (0, 6, 7):
        odd(i)
    level1(0, 2)
    level1(13, 16)
    shift.append(to_next(ys.at[pl.ds(0, 2)], prev.at[pl.ds(0, 2)]))
    shift.append(to_next(ys.at[pl.ds(13, 3)], prev.at[pl.ds(13, 3)]))
    bands(2)
    for c in lon2:
        c.wait()
    settle(2)

    for l in (4, 3, 2):
        m, d, b = MLAT[l], DROW[l], SROW[l]
        for i in range(m + 1):
            part = bd[b + i] if l == 4 else bd[b + i] + sm[i]
            sm[i] = part - 0.25 * (bd[d + i] + bd[d + i + 1])
        for i in range(2 * m, -1, -1):
            if i % 2:
                h = i // 2
                tmsg[i, :, 0:128] = bd[d + 1 + h] + 0.5 * (sm[h] + sm[h + 1])
            else:
                tmsg[i, :, 0:128] = sm[i // 2]
        n = 2 * m + 1
        out = mm(tmsg[0:n, :, 0:128].reshape(n * LP, 128), "T", l).reshape(n, LP, 128)
        sm[0:n] = out
        sm[2 * m] = mw * sm[2 * m]

    last = sm[8]
    for k in range(9):
        last = jnp.where(lane == 64 + k, sm[k] if k == 0 else pltpu.roll(sm[k], k, 1), last)
    for k in range(4):
        pk[k] = jnp.where(low, sm[k], pltpu.roll(sm[k + 4], 64, 1))
    pk[4] = last
    shift.append(to_next(pk, pk_hbm))
    forward(0, 1)

    for c in coarse:
        c.wait()
    for rho in range(2):
        w = latf[pl.ds(jnp.minimum(lat + rho, NLAT_D - 1), 1), :]
        fo[rho] = sum(cbuf[a] * w[:, a:a + 1] for a in range(NLAT_D))
    shift.append(to_next(fo, fop))

    def climb(folded):
        for rho in range(2):
            t = folded[rho]
            parts = [t if g == 0 else pltpu.roll(t, 128 - WIDE * g, 1) for g in range(LP // FOLD)]
            c = jnp.where(lane < WIDE, jnp.concatenate(parts, axis=0), 0.0)
            v = vmul((BANDS - 1,), c)[0]
            smc[rho] = v * mw if rho else v
        for l in (4, 3, 2):
            m = MLAT[l]
            n = 2 * m + 1
            for i in range(n):
                h = i // 2
                tmsg[i, :, 0:128] = 0.5 * (smc[h] + smc[h + 1]) if i % 2 else smc[h]
            out = mm(tmsg[0:n, :, 0:128].reshape(n * LP, 128), "T", l).reshape(n, LP, 128)
            smc[0:n] = out
            smc[2 * m] = mw * smc[2 * m]

    def lifted(rows):
        w = const(("T", 1, "hi"))[0:128]
        for i in range(8):
            tmsg[2 * i, :, 0:128] = rows[i]
            tmsg[2 * i + 1, :, 0:128] = 0.5 * (rows[i] + rows[i + 1])
        h, l = split(tmsg[0:16, :, 0:128].reshape(16 * LP, 128))
        return (dot(h, w) + dot(l, w)).reshape(ROWS, LP, 128)

    climb(fo)
    sm[...] = sm[...] + smc[...]
    yz[...] = ys[...] + lifted(sm)
    for r in range(ROWS):
        inc[pl.ds(r, LEV, stride=ROWS), :] = yz[r, 0:LEV, :]
    out = pltpu.make_async_copy(inc, inc_hbm, load.at[6])
    out.start()

    pl.when(tm > 0)(shift[4].wait_recv)
    climb(fop)
    yz[...] = yz[...] - lifted(smc)
    for c in shift[:3]:
        pl.when(tm > 0)(c.wait_recv)
    pl.when((tm == 1) | (tm == 3))(straight.wait_recv)

    @pl.when(tm == 2)
    def _():
        for q in range(2):
            hops[q][2].wait_recv()

    yz[...] = yz[...] - prev[...]
    out2 = pltpu.make_async_copy(yz, yz_hbm, load.at[7])
    out2.start()
    for c in shift:
        pl.when(tm < 3)(c.wait_send)
    pl.when((tm == 0) | (tm == 2))(straight.wait_send)
    for window, hop in ((1, 0), (3, 1), (0, 2)):
        @pl.when(tm == window)
        def _(hop=hop):
            for q in range(2):
                hops[q][hop].wait_send()

    out.wait()
    out2.wait()
    pl.when(tm > 0)(shift[3].wait_recv)


def finish(inc_hbm, yz_hbm, pk_hbm, t_hbm, inc_out, jump_out, inc, yz, pk, t, lift, jump, arrive, leave):
    loads = [pltpu.make_async_copy(src, dst, arrive.at[n])
             for n, (src, dst) in enumerate(((pk_hbm, pk), (t_hbm, t), (yz_hbm, yz), (inc_hbm, inc)))]
    for c in loads:
        c.start()
    loads[0].wait()
    lane = lax.broadcasted_iota(jnp.int32, (1, 128), 1)
    for k in range(9):
        part = pk[k % 4] if k < 8 else pk[4]
        if 4 <= k < 8:
            part = pltpu.roll(part, 64, 1)
        end = pk[4] if k == 0 else pltpu.roll(pk[4], 128 - k, 1)
        row = jnp.where(lane == 64, end, part)
        if k < 8:
            lift[2 * k] = row
        if k:
            lift[2 * k - 1] = 0.5 * (lift[2 * k - 2] + row)
    loads[1].wait()
    h, l = split(lift[...].reshape(ROWS * LP, 128))
    w = t[...]
    loads[2].wait()
    lift[...] = yz[...] - (dot(h, w) + dot(l, w)).reshape(ROWS, LP, 128)
    loads[3].wait()
    out = pltpu.make_async_copy(inc, inc_out, leave.at[0])
    out.start()
    for r in range(ROWS):
        jump[pl.ds(r, LEV, stride=ROWS), :] = lift[r, 0:LEV, :]
    out2 = pltpu.make_async_copy(jump, jump_out, leave.at[1])
    out2.start()
    out.wait()
    out2.wait()


def body(forcing, vertical, lat_factor, lon_factor):
    x = forcing.reshape(LEV * ROWS, COLS)
    tile = (LP, 128)
    anywhere = pl.BlockSpec(memory_space=pl.ANY)
    S = pltpu.VMEM
    flat = (LEV * ROWS, COLS)
    scratch = [
        S(flat, F32), S((BANDS, LEV, LEV), F32), S((8, 8), F32), S((32, 32), F32), S(CB.shape, BF), S(EXT.shape, F32),
        S(flat, F32),
        S((ROWS,) + tile, F32), S((39,) + tile, F32), S((19,) + tile, F32), S((23, LP, 256), F32),
        S((3,) + tile, F32), S((2,) + tile, F32), S((2,) + tile, F32),
        S((2,) + tile, F32), S(tile, F32), S(tile, F32), S(tile, F32), S(tile, F32), S(tile, F32),
        S((BANDS, 2 * LP, 256), BF), S((LP, 256), F32), S((2, 256, 512), BF),
        S((19, LP, 256), F32), S((23,) + tile, F32), S((17, LP, 256), F32), S((19, LP, 256), F32),
        S((3,) + tile, F32), S((3,) + tile, F32), S((3,) + tile, F32),
        S((4, FOLD, 128), F32), S((4, FOLD, 128), F32), S((8, FOLD, 128), F32),
        S((52,) + tile, F32), S((9,) + tile, F32), S((9,) + tile, F32), S((5,) + tile, F32),
        S((2, FOLD, 128), F32), S((2, FOLD, 128), F32),
        S((ROWS,) + tile, F32), S((ROWS,) + tile, F32), S((ROWS,) + tile, F32), S((4,) + tile, F32),
        pltpu.SemaphoreType.DMA((48,)), pltpu.SemaphoreType.DMA((48,)), pltpu.SemaphoreType.DMA((8,)),
    ]
    out = jax.ShapeDtypeStruct((LEV * ROWS, COLS), F32)
    inc, yz, pk = pl.pallas_call(
        kernel,
        out_shape=(out, jax.ShapeDtypeStruct((ROWS,) + tile, F32), jax.ShapeDtypeStruct((5,) + tile, F32)),
        in_specs=[anywhere] * 6,
        out_specs=(anywhere,) * 3,
        scratch_shapes=scratch,
        compiler_params=pltpu.CompilerParams(
            collective_id=0, has_side_effects=True, vmem_limit_bytes=56 * 1024 * 1024),
    )(x, vertical, lat_factor, lon_factor, jnp.asarray(CB), jnp.asarray(EXT))
    inc, jump = pl.pallas_call(
        finish, out_shape=(out, out), in_specs=[anywhere] * 4, out_specs=(anywhere, anywhere),
        scratch_shapes=[S(flat, F32), S((ROWS,) + tile, F32), S((5,) + tile, F32), S((128, 128), BF),
                        S((ROWS,) + tile, F32), S(flat, F32),
                        pltpu.SemaphoreType.DMA((4,)), pltpu.SemaphoreType.DMA((2,))],
        compiler_params=pltpu.CompilerParams(vmem_limit_bytes=40 * 1024 * 1024),
    )(inc, yz, pk, jnp.asarray(CONST["T", 1][:128].astype(ml_dtypes.bfloat16)))
    shape = (1, LEV, ROWS, COLS)
    return inc.reshape(shape), jump.reshape(shape)


def solution(mesh):
    placed = (P("tm", None, "lat", "lon"), P(), P(), P())
    return jax.shard_map(
        body,
        mesh=mesh,
        in_specs=placed,
        out_specs=(P("tm", None, "lat", "lon"), P("tm", None, "lat", "lon")),
        check_vma=False,
    )
```

```python
import numpy as np
import jax
import jax.numpy as jnp
import ml_dtypes
from jax import lax
from jax.experimental import pallas as pl
from jax.experimental.pallas import tpu as pltpu
from jax.sharding import PartitionSpec as P

LEV, LP = 137, 144
ROWS, COLS = 16, 128
BANDS = 13
NLAT_D, NLON_D = 8, 4
MESH = pl.DeviceIdType.MESH
HIGH = lax.Precision.HIGHEST
F32, BF = jnp.float32, jnp.bfloat16

MLAT = {1: 8, 2: 4, 3: 2, 4: 1}
MLON = {1: 64, 2: 32, 3: 16, 4: 8}
DROW = {1: 0, 2: 19, 3: 30, 4: 37}
SROW = {1: 10, 2: 25, 3: 34, 4: 40}
NROWS = 42
PACK = {2: (0, 1, -1, 64), 3: (66, 2, -1, 33), 4: (101, 3, -1, 17)}
FOLD, WIDE = 16, 9
CHUNKS = 2
DIRECT = 11 - 2 * CHUNKS
FOLD_LANES = LP // FOLD * WIDE
LEVEL_OF = {}
for _l in (1, 2, 3, 4):
    for _i in range(MLAT[_l] + 2):
        LEVEL_OF[DROW[_l] + _i] = (_l, "D", _i - 1)
    for _i in range(MLAT[_l] + 1):
        LEVEL_OF[SROW[_l] + _i] = (_l, "S", _i)


def lift(seq, size):
    lo, hi = min(seq), max(seq)
    zero = np.zeros(size)
    get = lambda table, i: table.get(i, zero)
    d, s = {}, {}
    for i in range(lo // 2 - 2, hi // 2 + 3):
        d[i] = get(seq, 2 * i + 1) - 0.5 * (get(seq, 2 * i) + get(seq, 2 * i + 2))
    for i in range(lo // 2 - 2, hi // 2 + 3):
        s[i] = get(seq, 2 * i) + 0.25 * (get(d, i - 1) + get(d, i))
    keep = lambda table: {i: v for i, v in table.items() if np.any(v)}
    return keep(s), keep(d)


INNER, OUTER = ((1, 8), (11, 17)), ((0, 1), (8, 11), (17, 19))
COARSER = ((19, 30), (30, 37), (37, 42))
MESSAGES = [[j for lo, hi in part for j in range(lo, hi)] for part in (INNER, OUTER, COARSER)]


def message_lanes():
    left, right, border = {}, {}, []
    for rows in MESSAGES:
        n = 0
        for table in (left, right):
            for j in rows:
                l, kind, _ = LEVEL_OF[j]
                if table is left:
                    names = ["dm1"] if l == 1 else (["sm", "dm1", "dm"] if kind == "D" else ["dm1", "dm"])
                else:
                    names = ["d-1", "d0"] if (l == 1 or kind == "S") else ["s0", "d-1", "d0"]
                table[j] = (n, names)
                n += len(names)
            if table is left:
                border.append(n)
        assert n <= 128
    return left, right, border


LEFT, RIGHT, BORDER = message_lanes()


def users(n):
    table = {}
    for j in MESSAGES[n]:
        l, kind, _ = LEVEL_OF[j]
        for k in ((3 * l - 2, 3 * l - 1) if kind == "D" else (3 * l - 3,)):
            table.setdefault(k, []).append(j)
    return table


def lon_tables():
    raw = {i: np.eye(256)[i] for i in range(COLS)}
    smooth, detail = {0: raw}, {}
    for l in range(1, 5):
        smooth[l], detail[l] = lift(smooth[l - 1], 256)
    ext_s = {}
    for l in (2, 3, 4):
        at, depth, lo, hi = PACK[l]
        seq = {i: np.eye(256)[128 + at + i - lo] for i in range(lo, hi + 1)}
        for k in range(l, 5):
            s, d = lift(seq, 256)
            seq = s
            ext_s[l, k] = (s, d)
    zero = np.zeros(256)
    full_s, full_d = {}, {}
    for k in range(1, 5):
        s, d = dict(smooth[k]), dict(detail[k])
        for l in range(2, k + 1):
            for table, more in ((s, ext_s[l, k][0]), (d, ext_s[l, k][1])):
                for i, v in more.items():
                    table[i] = table.get(i, zero) + v
        full_s[k], full_d[k] = s, d
    return smooth, full_s, full_d


def constants():
    smooth, fs, fd = lon_tables()
    zero = np.zeros(256)
    out = {}
    for l in (1, 2, 3, 4):
        m = MLON[l]
        w = np.zeros((256, 256))
        off = 128 if l == 1 else 64
        for i in range(0, m + 1):
            w[:, i] = fs[l].get(i, zero)
        for i in range(-1, m + 1):
            w[:, off + i + 1] = fd[l].get(i, zero)
        out["W", l] = w if l == 1 else w[:, :128]
        pick = {"sm": fs[l].get(m, zero), "dm1": fd[l].get(m - 1, zero), "dm": fd[l].get(m, zero),
                "s0": fs[l].get(0, zero), "d-1": fd[l].get(-1, zero), "d0": fd[l].get(0, zero)}
        for n, rows in enumerate(MESSAGES):
            rows = [j for j in rows if LEVEL_OF[j][0] == l]
            if not rows:
                continue
            g = np.zeros((256, 128))
            for j in rows:
                for at, names in (LEFT[j], RIGHT[j]):
                    for q, name in enumerate(names):
                        g[:, at + q] = pick[name]
            out["G", n, l] = g
            for k, js in users(n).items():
                if k // 3 != l - 1:
                    continue
                kind = k % 3
                z = np.zeros((128, 256 * ((len(js) + 1) // 2)))
                for p, j in enumerate(js):
                    smooths = np.zeros((128, 128))
                    details = np.zeros((128, 128))
                    at, names = LEFT[j]
                    for q, name in enumerate(names):
                        if name == "dm1":
                            details[at + q, 0] += 1.0
                            if l == 1:
                                smooths[at + q, 0] += 0.25
                        if name == "dm":
                            details[at + q, 1] += 1.0
                            smooths[at + q, 1] += 0.25
                        if name == "sm":
                            smooths[at + q, 0] += 1.0
                    at, names = RIGHT[j]
                    for q, name in enumerate(names):
                        if name == "s0":
                            smooths[at + q, m] += 1.0
                        if name == "d-1":
                            details[at + q, m] += 1.0
                            smooths[at + q, m - 1] += 0.25
                            if l == 1:
                                smooths[at + q, m] += -1.75
                        if name == "d0":
                            details[at + q, m + 1] += 1.0
                            if l == 1:
                                smooths[at + q, m] += 0.25
                    if l > 1:
                        details = np.roll(details, 64, axis=1)
                    z[:, 128 * p:128 * p + 128] = smooths if kind == 1 else details
                for c in range(0, z.shape[1], 256):
                    out["Z", n, k, c // 256] = z[:, c:c + 256]
        n_in = 256 if l == 1 else 128
        eye = np.eye(n_in)
        s = {i: eye[i] for i in range(0, m + 1)}
        d = {i: eye[off + i + 1] for i in range(-1, m + 1)}
        e = {i: s[i] - 0.25 * (d[i - 1] + d[i]) for i in range(0, m + 1)}
        t = np.zeros((n_in, 128))
        for i in range(0, m + 1):
            if 2 * i < 128:
                t[:, 2 * i] = e[i]
            if i < m:
                t[:, 2 * i + 1] = d[i] + 0.5 * (e[i] + e[i + 1])
        out["T", l] = t
    for l in (2, 3, 4):
        at, depth, lo, hi = PACK[l]
        sm = np.zeros((128, 128))
        for i in range(lo, hi + 1):
            sm[:, at + i - lo] = smooth[depth][i][:128]
        out["Sm", l] = sm
    c4 = np.zeros((256, 128))
    for c in range(11):
        c4[:, c] = fs[4].get(c - 1, zero)
    out["C4", 0] = c4
    return out


CONST = constants()


def pack_constants():
    tiles, where = [], {}

    def put(key, a):
        k, n = a.shape
        where[key] = (sum(t.shape[0] for t in tiles), k, n)
        if n < 256:
            a = np.concatenate([a, np.zeros((k, 256 - n), a.dtype)], 1)
        tiles.append(a)

    for key, a in CONST.items():
        if key == ("W", 1) or (key[0] == "G" and key[2] == 1):
            a = a[:128]
        hi = a.astype(ml_dtypes.bfloat16)
        lo = (a - hi.astype(np.float64)).astype(ml_dtypes.bfloat16)
        put(key + ("hi",), hi)
        if np.any(lo.astype(np.float64)):
            put(key + ("lo",), lo)
    return np.concatenate(tiles, 0), where


CB, CWHERE = pack_constants()


def ext_coefficients():
    syms = {("U", 2): 0, ("U", 3): 1, ("U", 4): 2, ("W", 2): 3, ("W", 3): 4, ("W", 4): 5}
    unit = lambda key: np.eye(6)[syms[key]]
    zero = np.zeros(6)
    s = {i: zero for i in range(9)}
    table = {}
    for l in (2, 3, 4):
        m = MLAT[l]
        d = {-1: unit(("U", l)), m: unit(("W", l))}
        for i in range(m):
            d[i] = s[2 * i + 1] - 0.5 * (s[2 * i] + s[2 * i + 2])
        s = {i: s[2 * i] + 0.25 * (d[i - 1] + d[i]) for i in range(m + 1)}
        for i in range(-1, m + 1):
            table[DROW[l] + i + 1] = d[i]
        for i in range(m + 1):
            table[SROW[l] + i] = s[i]
    out = np.zeros((48, 128), np.float32)
    for j, v in table.items():
        for l in (2, 3, 4):
            at, _, lo, hi = PACK[l]
            out[j - 19, at:at + hi - lo + 1] = v[l - 2]
            out[24 + j - 19, at:at + hi - lo + 1] = v[3 + l - 2]
    return out


EXT = ext_coefficients()


def split(a):
    hi = a.astype(BF)
    return hi, (a - hi.astype(F32)).astype(BF)


def dot(a, b):
    return jnp.dot(a, b, preferred_element_type=F32)


def both(hi, lo, w):
    if hi.shape[1] == 128:
        return dot(jnp.concatenate([hi, lo], axis=1), jnp.concatenate([w, w], axis=0))
    return dot(hi, w) + dot(lo, w)


def kernel(x_hbm, vert_hbm, latf_hbm, lonf_hbm, cb_hbm, ext_hbm, inc_hbm, jump_hbm,
           x, vert, latf, lonf, cb, ext_c, inc, jump,
           xs, so, rw, lx, up, dn, p2, r_w, r_u, r_pw, r_pu, r_p2u, r_p2w,
           vst, vtmp, pm, o1, o2, tl, tmsg, sd, m_l, m_r, sf, mf, cbuf,
           bd, sm, pk, pkp, ys, yz, prev, way, send, recv, load):
    tm, lat, lon = lax.axis_index("tm"), lax.axis_index("lat"), lax.axis_index("lon")
    mu = (lat > 0).astype(F32)
    mw = (lat < NLAT_D - 1).astype(F32)
    mu2 = (lat > 1).astype(F32)
    mw2 = (lat < NLAT_D - 2).astype(F32)

    def at_lat(k):
        return (tm, lax.rem(lat + k + NLAT_D, NLAT_D), lon)

    def at_lon(k):
        return (tm, lat, lax.rem(lon + k + NLON_D, NLON_D))

    across = lat + 1 - 2 * lax.rem(lat, 2)

    def at(window, row):
        return (window, row, lon)

    def at_tm(k):
        return (lax.rem(tm + k + 4, 4), lat, lon)

    partners = [at_lat(k) for k in range(1, 8)] + [at_lon(k) for k in range(1, 4)] + [at_tm(1), at_tm(-1), at(lax.rem(tm + 2, 4), across)]
    barrier = pltpu.get_barrier_semaphore()
    for p in partners:
        pl.semaphore_signal(barrier, inc=1, device_id=p, device_id_type=MESH)

    loads = {}
    for n, (name, src, dst) in enumerate((("x", x_hbm, x), ("cb", cb_hbm, cb), ("ext", ext_hbm, ext_c),
                                          ("lonf", lonf_hbm, lonf), ("latf", latf_hbm, latf),
                                          ("vert", vert_hbm, vert))):
        loads[name] = pltpu.make_async_copy(src, dst, load.at[n])
        loads[name].start()

    def const(key):
        at, k, n = CWHERE[key]
        return cb[at:at + k, 0:n]

    def mm(a, *key):
        hi, lo = split(a)
        w = const(key + ("hi",))
        out = both(hi, lo, w)
        if key + ("lo",) in CWHERE:
            out = out + dot(hi, const(key + ("lo",)))
        return out

    loads["x"].wait()
    for r in range(ROWS):
        xs[r, 136:144, :] = jnp.zeros((8, COLS), F32)
        xs[r, 0:LEV, :] = x[pl.ds(r, LEV, stride=ROWS), :]

    for i in range(7):
        rw[1 + i] = xs[2 * i + 1] - 0.5 * (xs[2 * i] + xs[2 * i + 2])
    dn[0] = xs[15] - 0.5 * xs[14]
    up[0] = xs[0]
    up[1] = rw[1]

    sems = iter(range(48))

    def remote(src, dst, dev, slot=None):
        k = next(sems)
        return pltpu.make_async_remote_copy(
            src_ref=src, dst_ref=dst, send_sem=send.at[k],
            recv_sem=recv.at[k], device_id=dev, device_id_type=MESH)

    copies = []

    def go(c):
        c.start()
        copies.append(c)

    so[0] = (-0.125 * mu) * xs[0]
    so[1] = 0.875 * xs[0] + 0.25 * rw[1]
    for i in range(1, 7):
        so[1 + i] = xs[2 * i] + 0.25 * (rw[i] + rw[1 + i])
    so[8] = xs[14] + 0.25 * (rw[7] + dn[0])
    so[9] = (0.25 * mw) * dn[0]
    sbase = {1: 0, 2: 10, 3: 17, 4: 22}
    dbase = {2: 26, 3: 32, 4: 36}
    for l in (2, 3, 4):
        m, a, b, d = MLAT[l], sbase[l - 1], sbase[l], dbase[l]
        S = lambda i: so[a + 1 + i]
        so[d] = S(-1) - 0.5 * S(0)
        for i in range(m):
            so[d + 1 + i] = S(2 * i + 1) - 0.5 * (S(2 * i) + S(2 * i + 2))
        so[d + 1 + m] = (-0.5 * S(2 * m)) if l == 2 else S(2 * m + 1) - 0.5 * S(2 * m)
        so[b] = (0.25 * mu) * so[d]
        for i in range(m):
            so[b + 1 + i] = S(2 * i) + 0.25 * (so[d + i] + so[d + 1 + i])
        so[b + 1 + m] = mw * (S(2 * m) + 0.25 * (so[d + m] + so[d + 1 + m]))
        so[b + 2 + m] = (0.25 * mw) * so[d + 1 + m]
    loads["cb"].wait()
    d4 = mm(so[37], "Sm", 4)
    up[2] = mm(so[27], "Sm", 2) + mm(so[33], "Sm", 3) + d4
    dn[1] = mm(so[30], "Sm", 2) + mm(so[34], "Sm", 3) + d4
    p2[0] = mm(so[38], "Sm", 4)
    p2[1] = mm(so[36], "Sm", 4)
    for i in range(1, 7):
        rw[10 + i] = xs[2 * i] + 0.25 * (rw[i] + rw[i + 1])

    lane = lax.broadcasted_iota(jnp.int32, (1, 128), 1)
    def operand(lo, hi):
        if hi <= 19:
            return rw[lo:hi].reshape((hi - lo) * LP, 128)
        return lx[lo - 19:hi - 19].reshape((hi - lo) * LP, 256)

    def message(n, groups):
        for lo, hi in groups:
            tmsg[0:hi - lo, :, 0:128] = mm(operand(lo, hi), "G", n, LEVEL_OF[lo][0]).reshape(hi - lo, LP, 128)
            v = jnp.zeros((LP, 128), F32) if lo == groups[0][0] else sd[n]
            for j in range(lo, hi):
                (a, na), (b, nb) = LEFT[j], RIGHT[j]
                keep = ((lane >= a) & (lane < a + len(na))) | ((lane >= b) & (lane < b + len(nb)))
                v = jnp.where(keep, tmsg[j - lo, :, 0:128], v)
            sd[n] = v

    def post(n):
        out = [remote(sd.at[n], m_l.at[n], at_lon(1)), remote(sd.at[n], m_r.at[n], at_lon(-1))]
        for c in out:
            c.start()
        return out

    message(0, INNER)
    pl.semaphore_wait(barrier, len(partners))
    bulk = [remote(up.at[pl.ds(0, 2)], r_w, at_lat(-1)), remote(dn.at[0], r_u, at_lat(1))]
    for c in bulk:
        c.start()
    lon0 = post(0)
    go(remote(up.at[2], r_pw, at_lat(-1)))
    go(remote(dn.at[1], r_pu, at_lat(1)))
    go(remote(p2.at[0], r_p2u, at_lat(2)))
    go(remote(p2.at[1], r_p2w, at_lat(-2)))
    packs = copies[:]
    copies.clear()

    for name in ("ext", "lonf", "latf", "vert"):
        loads[name].wait()
    vtmp[...] = jnp.zeros((LP, 256), F32)
    for k in range(BANDS):
        vtmp[0:LEV, 0:LEV] = vert[k]
        hi, lo = split(vtmp[...])
        vst[k, 0:LP, :] = hi
        vst[k, LP:2 * LP, :] = lo
    rowi = lax.broadcasted_iota(jnp.int32, (128, 32), 0)
    coli = lax.broadcasted_iota(jnp.int32, (128, 32), 1)
    mine = ((rowi < 11) & (coli == lax.rem(8 * lon + 31 + rowi, 32))).astype(F32)
    for k in range(NLON_D):
        theirs = (rowi < FOLD_LANES) & (coli == lax.rem(8 * (lon + k) + lax.rem(rowi, WIDE), 32))
        part = jnp.dot(theirs.astype(F32), lonf[...], precision=HIGH, preferred_element_type=F32)
        part = lax.dot_general(mine, part, (((1,), (1,)), ((), ())), precision=HIGH,
                               preferred_element_type=F32)
        c4 = const(("C4", 0, "hi")).astype(F32) + const(("C4", 0, "lo")).astype(F32)
        hi, lo = split(jnp.dot(c4, part, precision=HIGH, preferred_element_type=F32))
        pm[0, :, k * 128:(k + 1) * 128] = hi
        pm[1, :, k * 128:(k + 1) * 128] = lo

    low = lane < 64
    def vmul(ks, t):
        hi, lo = split(t)
        pair = jnp.concatenate([hi, lo], axis=1)
        outs = []
        for k in ks:
            p = dot(vst[k][:, 0:LP], pair)
            outs.append(p[0:LP, 0:128] + p[0:LP, 128:256] + p[LP:2 * LP, 0:128])
        return outs

    def settle(n):
        got = jnp.where(lane < BORDER[n], m_l[n], m_r[n])
        for k, js in users(n).items():
            hi, lo = split(vmul((k,), got)[0])
            for c in range((len(js) + 1) // 2):
                p = both(hi, lo, const(("Z", n, k, c, "hi")))
                for h, j in enumerate(js[2 * c:2 * c + 2]):
                    at = j + 42 if k == 1 else j
                    bd[at] = bd[at] + p[:, 128 * h:128 * h + 128]

    def own_part(lo, hi):
        if lo < 10:
            o1[lo:hi] = mm(operand(lo, hi), "W", 1).reshape(hi - lo, LP, 256)
        else:
            h, l = split(operand(lo, hi))
            w = const(("W", 1, "hi"))[:, 128:256]
            o1[lo:hi, :, 128:256] = both(h, l, w).reshape(hi - lo, LP, 128)

    def bands1(js):
        for j in js:
            if j < 10:
                bd[42 + j] = vmul((1,), o1[j, :, 0:128])[0]
                bd[j] = vmul((2,), o1[j, :, 128:256])[0]
            else:
                bd[j] = vmul((0,), o1[j, :, 128:256])[0]

    def bands(l):
        lo, hi = COARSER[l - 2]
        o2[lo - 19:hi - 19] = mm(operand(lo, hi), "W", l).reshape(hi - lo, LP, 128)
        for j in range(lo, hi):
            if LEVEL_OF[j][1] == "D":
                a, b = vmul((3 * l - 2, 3 * l - 1), o2[j - 19])
                bd[j] = jnp.where(low, a, b)
            else:
                bd[j] = jnp.where(low, 0.0, vmul((3 * l - 3,), o2[j - 19])[0])

    def even(i):
        tl[2 * i, :, 0:128] = -0.25 * (bd[42 + i] + bd[43 + i])
        tl[2 * i, :, 128:256] = bd[10 + i] - 0.25 * (bd[i] + bd[i + 1])

    def odd(i):
        tl[2 * i + 1, :, 0:128] = bd[43 + i] + 0.5 * (tl[2 * i, :, 0:128] + tl[2 * i + 2, :, 0:128])
        tl[2 * i + 1, :, 128:256] = bd[1 + i] + 0.5 * (tl[2 * i, :, 128:256] + tl[2 * i + 2, :, 128:256])

    def level1(lo, hi):
        ys[lo:hi] = mm(tl[lo:hi].reshape((hi - lo) * LP, 256), "T", 1).reshape(hi - lo, LP, 128)

    def to_next(src, dst):
        c = remote(src, dst, at_tm(1))

        @pl.when(tm < 3)
        def _():
            c.start()

        return c

    @pl.when(tm == 0)
    def _():
        prev[...] = jnp.zeros((ROWS, LP, 128), F32)
        pkp[...] = jnp.zeros((5, LP, 128), F32)

    for lo, hi in INNER:
        own_part(lo, hi)
    bands1(MESSAGES[0])
    for c in lon0:
        c.wait()
    settle(0)
    for i in range(1, 7):
        even(i)
    for i in range(1, 6):
        odd(i)
    level1(2, 13)
    for c in bulk:
        c.wait()
    x16 = lambda: mw * r_w[0]
    rw[0] = mu * r_u[...] - 0.5 * xs[0]
    rw[8] = dn[0] - 0.5 * x16()
    rw[9] = mw * r_w[1]
    rw[10] = xs[0] + 0.25 * (rw[0] + rw[1])
    rw[17] = xs[14] + 0.25 * (rw[7] + rw[8])
    rw[18] = x16() + (0.25 * mw) * (rw[8] + rw[9])
    rw[0] = mu * rw[0]
    message(1, OUTER)
    lon1 = post(1)
    for lo, hi in OUTER:
        own_part(lo, hi)
    bands1(MESSAGES[1])

    for c in packs:
        c.wait()

    shift = [to_next(ys.at[pl.ds(2, DIRECT)], prev.at[pl.ds(2, DIRECT)])]
    straight = remote(ys.at[pl.ds(2 + DIRECT, 2 * CHUNKS)], prev.at[pl.ds(2 + DIRECT, 2 * CHUNKS)], at_tm(1))
    hops = []
    for q in range(CHUNKS):
        mine, kept, there = ys.at[pl.ds(2 + DIRECT + 2 * q, 2)], way.at[pl.ds(2 * q, 2)], prev.at[pl.ds(2 + DIRECT + 2 * q, 2)]
        hops.append((remote(mine, kept, at(3, across)), remote(kept, kept, at(0, lat)),
                     remote(kept, there, at(2, across))))

    @pl.when((tm == 0) | (tm == 2))
    def _():
        straight.start()

    @pl.when(tm == 1)
    def _():
        for q in range(CHUNKS):
            hops[q][0].start()

    def forward(window, hop):
        @pl.when(tm == window)
        def _():
            for q in range(CHUNKS):
                hops[q][hop].wait_recv()
                hops[q][hop + 1].start()

    raw = lambda j: rw[j] if j < 19 else lx[j - 19, :, 0:128]
    for l in (2, 3, 4):
        m, a, d, b = MLAT[l], SROW[l - 1], DROW[l], SROW[l]
        lx[d - 19, :, 0:128] = so[dbase[l]]
        lx[d + m + 1 - 19, :, 0:128] = so[dbase[l] + m + 1]
        for i in range(m):
            lx[d + 1 + i - 19, :, 0:128] = raw(a + 2 * i + 1) - 0.5 * (raw(a + 2 * i) + raw(a + 2 * i + 2))
        for i in range(m + 1):
            v = raw(a + 2 * i) + 0.25 * (raw(d + i) + raw(d + i + 1))
            lx[b + i - 19, :, 0:128] = mw * v if i == m else v
    r_pu[...] = mu * r_pu[...] + mu2 * r_p2u[...]
    r_pw[...] = mw * r_pw[...] + mw2 * r_p2w[...]
    for j in range(19, NROWS):
        cu, cw = ext_c[j - 19:j - 18, :], ext_c[24 + j - 19:24 + j - 18, :]
        l, kind, i = LEVEL_OF[j]
        if kind == "S" and i == MLAT[l]:
            cu, cw = cu * mw, cw * mw
        lx[j - 19, :, 128:256] = r_pu[...] * cu + r_pw[...] * cw
    for l in (2, 3, 4):
        lx[DROW[l] - 19] = mu * lx[DROW[l] - 19]

    hi, lo = split(lx[SROW[4] - 19])
    fold = dot(hi, pm[0]) + dot(lo, pm[0]) + dot(hi, pm[1])
    for k in range(NLON_D):
        acc = jnp.zeros((FOLD, 128), F32)
        for g in range(LP // FOLD):
            acc = jnp.where((lane >= g * WIDE) & (lane < (g + 1) * WIDE),
                            fold[g * FOLD:(g + 1) * FOLD, k * 128:(k + 1) * 128], acc)
        sf[k] = acc
    for k in range(1, NLON_D):
        go(remote(sf.at[k], mf.at[k], at_lon(k)))
    coarse = copies[:]
    copies.clear()

    message(2, COARSER)
    lon2 = post(2)
    bands(4)
    bands(3)

    forward(3, 0)

    for c in coarse:
        c.wait()
    row = sf[0] + mf[1] + mf[2] + mf[3]
    sf[0] = row
    cbuf[lat] = row
    for k in range(1, NLAT_D):
        go(remote(sf.at[0], cbuf.at[lat], at_lat(k)))
    coarse = copies[:]
    copies.clear()

    for c in lon1:
        c.wait()
    settle(1)
    for i in (0, 7, 8):
        even(i)
    for i in (0, 6, 7):
        odd(i)
    level1(0, 2)
    level1(13, 16)
    shift.append(to_next(ys.at[pl.ds(0, 2)], prev.at[pl.ds(0, 2)]))
    shift.append(to_next(ys.at[pl.ds(13, 3)], prev.at[pl.ds(13, 3)]))
    bands(2)
    for c in lon2:
        c.wait()
    settle(2)
    forward(0, 1)

    for c in coarse:
        c.wait()
    for rho in range(2):
        w = latf[pl.ds(jnp.minimum(lat + rho, NLAT_D - 1), 1), :]
        t = sum(cbuf[a] * w[:, a:a + 1] for a in range(NLAT_D))
        parts = [t if g == 0 else pltpu.roll(t, 128 - WIDE * g, 1) for g in range(LP // FOLD)]
        c = jnp.where(lane < WIDE, jnp.concatenate(parts, axis=0), 0.0)
        v = vmul((BANDS - 1,), c)[0]
        sm[rho] = v * mw if rho else v

    for l in (4, 3, 2):
        m, d, b = MLAT[l], DROW[l], SROW[l]
        for i in range(m + 1):
            s = bd[b + i] + sm[i]
            sm[i] = s - 0.25 * (bd[d + i] + bd[d + i + 1])
        for i in range(2 * m, -1, -1):
            if i % 2:
                h = i // 2
                tmsg[i, :, 0:128] = bd[d + 1 + h] + 0.5 * (sm[h] + sm[h + 1])
            else:
                tmsg[i, :, 0:128] = sm[i // 2]
        n = 2 * m + 1
        out = mm(tmsg[0:n, :, 0:128].reshape(n * LP, 128), "T", l).reshape(n, LP, 128)
        sm[0:n] = out
        sm[2 * m] = mw * sm[2 * m]

    last = sm[8]
    for k in range(9):
        last = jnp.where(lane == 64 + k, sm[k] if k == 0 else pltpu.roll(sm[k], k, 1), last)
    for k in range(4):
        pk[k] = jnp.where(low, sm[k], pltpu.roll(sm[k + 4], 64, 1))
    pk[4] = last
    shift.append(to_next(pk, pkp))

    def lifted(rows):
        w = const(("T", 1, "hi"))[0:128]
        for i in range(8):
            tmsg[2 * i, :, 0:128] = rows[i]
            tmsg[2 * i + 1, :, 0:128] = 0.5 * (rows[i] + rows[i + 1])
        h, l = split(tmsg[0:16, :, 0:128].reshape(16 * LP, 128))
        return both(h, l, w).reshape(ROWS, LP, 128)

    yz[...] = ys[...] + lifted(sm)
    for r in range(ROWS):
        inc[pl.ds(r, LEV, stride=ROWS), :] = yz[r, 0:LEV, :]
    out = pltpu.make_async_copy(inc, inc_hbm, load.at[6])
    out.start()

    def land(cs):
        for c in cs:
            pl.when(tm > 0)(c.wait_recv)

    land(shift[:3])
    pl.when((tm == 1) | (tm == 3))(straight.wait_recv)

    @pl.when(tm == 2)
    def _():
        for q in range(CHUNKS):
            hops[q][2].wait_recv()

    yz[...] = yz[...] - prev[...]
    land(shift[3:])
    for k in range(9):
        part = pkp[k % 4] if k < 8 else pkp[4]
        if 4 <= k < 8:
            part = pltpu.roll(part, 64, 1)
        end = pkp[4] if k == 0 else pltpu.roll(pkp[4], 128 - k, 1)
        sm[k] = jnp.where(lane == 64, end, part)
    less = lifted(sm)
    for r in range(ROWS):
        jump[pl.ds(r, LEV, stride=ROWS), :] = yz[r, 0:LEV, :] - less[r, 0:LEV, :]
    out2 = pltpu.make_async_copy(jump, jump_hbm, load.at[7])
    out2.start()
    for c in shift:
        pl.when(tm < 3)(c.wait_send)
    pl.when((tm == 0) | (tm == 2))(straight.wait_send)
    for window, hop in ((1, 0), (3, 1), (0, 2)):
        @pl.when(tm == window)
        def _(hop=hop):
            for q in range(CHUNKS):
                hops[q][hop].wait_send()

    out.wait()
    out2.wait()


def body(forcing, vertical, lat_factor, lon_factor):
    x = forcing.reshape(LEV * ROWS, COLS)
    tile = (LP, 128)
    anywhere = pl.BlockSpec(memory_space=pl.ANY)
    S = pltpu.VMEM
    flat = (LEV * ROWS, COLS)
    scratch = [
        S(flat, F32), S((BANDS, LEV, LEV), F32), S((8, 8), F32), S((32, 32), F32), S(CB.shape, BF), S(EXT.shape, F32),
        S(flat, F32), S(flat, F32),
        S((ROWS,) + tile, F32), S((39,) + tile, F32), S((19,) + tile, F32), S((23, LP, 256), F32),
        S((3,) + tile, F32), S((2,) + tile, F32), S((2,) + tile, F32),
        S((2,) + tile, F32), S(tile, F32), S(tile, F32), S(tile, F32), S(tile, F32), S(tile, F32),
        S((BANDS, 2 * LP, 256), BF), S((LP, 256), F32), S((2, 256, 512), BF),
        S((19, LP, 256), F32), S((23,) + tile, F32), S((17, LP, 256), F32), S((19, LP, 256), F32),
        S((3,) + tile, F32), S((3,) + tile, F32), S((3,) + tile, F32),
        S((4, FOLD, 128), F32), S((4, FOLD, 128), F32), S((8, FOLD, 128), F32),
        S((52,) + tile, F32), S((9,) + tile, F32), S((5,) + tile, F32), S((5,) + tile, F32),
        S((ROWS,) + tile, F32), S((ROWS,) + tile, F32), S((ROWS,) + tile, F32), S((2 * CHUNKS,) + tile, F32),
        pltpu.SemaphoreType.DMA((48,)), pltpu.SemaphoreType.DMA((48,)), pltpu.SemaphoreType.DMA((8,)),
    ]
    out = jax.ShapeDtypeStruct((LEV * ROWS, COLS), F32)
    inc, jump = pl.pallas_call(
        kernel,
        out_shape=(out, out),
        in_specs=[anywhere] * 6,
        out_specs=(anywhere, anywhere),
        scratch_shapes=scratch,
        compiler_params=pltpu.CompilerParams(
            collective_id=0, has_side_effects=True, vmem_limit_bytes=56 * 1024 * 1024),
    )(x, vertical, lat_factor, lon_factor, jnp.asarray(CB), jnp.asarray(EXT))

    def settle(a, b, c, d, held, arrive, leave):
        size = LEV * ROWS // 2
        moves = []
        for k in range(2):
            for h, (src, dst) in enumerate(((a, c), (b, d))):
                part = pl.ds(k * size, size)
                moves.append((pltpu.make_async_copy(src.at[part], held.at[h, part], arrive.at[2 * k + h]),
                              pltpu.make_async_copy(held.at[h, part], dst.at[part], leave.at[2 * k + h])))
        for m, _ in moves:
            m.start()
        for m, o in moves:
            m.wait()
            o.start()
        for _, o in moves:
            o.wait()

    inc, jump = pl.pallas_call(
        settle, out_shape=(out, out), in_specs=[anywhere] * 2, out_specs=(anywhere, anywhere),
        scratch_shapes=[S((2,) + flat, F32), pltpu.SemaphoreType.DMA((4,)), pltpu.SemaphoreType.DMA((4,))],
    )(inc, jump)
    shape = (1, LEV, ROWS, COLS)
    return inc.reshape(shape), jump.reshape(shape)


def solution(mesh):
    placed = (P("tm", None, "lat", "lon"), P(), P(), P())
    return jax.shard_map(
        body,
        mesh=mesh,
        in_specs=placed,
        out_specs=(P("tm", None, "lat", "lon"), P("tm", None, "lat", "lon")),
        check_vma=False,
    )
```

```python
import numpy as np
import jax
import jax.numpy as jnp
import ml_dtypes
from jax import lax
from jax.experimental import pallas as pl
from jax.experimental.pallas import tpu as pltpu
from jax.sharding import PartitionSpec as P

LEV, LP = 137, 144
ROWS, COLS = 16, 128
BANDS = 13
NLAT_D, NLON_D = 8, 4
MESH = pl.DeviceIdType.MESH
HIGH = lax.Precision.HIGHEST
F32, BF = jnp.float32, jnp.bfloat16

MLAT = {1: 8, 2: 4, 3: 2, 4: 1}
MLON = {1: 64, 2: 32, 3: 16, 4: 8}
DROW = {1: 0, 2: 19, 3: 30, 4: 37}
SROW = {1: 10, 2: 25, 3: 34, 4: 40}
NROWS = 42
PACK = {2: (0, 1, -1, 64), 3: (66, 2, -1, 33), 4: (101, 3, -1, 17)}
FOLD, WIDE = 16, 9
CHUNKS = 2
DIRECT = 11 - 2 * CHUNKS
FOLD_LANES = LP // FOLD * WIDE
LEVEL_OF = {}
for _l in (1, 2, 3, 4):
    for _i in range(MLAT[_l] + 2):
        LEVEL_OF[DROW[_l] + _i] = (_l, "D", _i - 1)
    for _i in range(MLAT[_l] + 1):
        LEVEL_OF[SROW[_l] + _i] = (_l, "S", _i)


def lift(seq, size):
    lo, hi = min(seq), max(seq)
    zero = np.zeros(size)
    get = lambda table, i: table.get(i, zero)
    d, s = {}, {}
    for i in range(lo // 2 - 2, hi // 2 + 3):
        d[i] = get(seq, 2 * i + 1) - 0.5 * (get(seq, 2 * i) + get(seq, 2 * i + 2))
    for i in range(lo // 2 - 2, hi // 2 + 3):
        s[i] = get(seq, 2 * i) + 0.25 * (get(d, i - 1) + get(d, i))
    keep = lambda table: {i: v for i, v in table.items() if np.any(v)}
    return keep(s), keep(d)


INNER, OUTER = ((1, 8), (11, 17)), ((0, 1), (8, 11), (17, 19))
COARSER = ((19, 30), (30, 37), (37, 42))
MESSAGES = [[j for lo, hi in part for j in range(lo, hi)] for part in (INNER, OUTER, COARSER)]


def message_lanes():
    left, right, border = {}, {}, []
    for rows in MESSAGES:
        n = 0
        for table in (left, right):
            for j in rows:
                l, kind, _ = LEVEL_OF[j]
                if table is left:
                    names = ["dm1"] if l == 1 else (["sm", "dm1", "dm"] if kind == "D" else ["dm1", "dm"])
                else:
                    names = ["d-1", "d0"] if (l == 1 or kind == "S") else ["s0", "d-1", "d0"]
                table[j] = (n, names)
                n += len(names)
            if table is left:
                border.append(n)
        assert n <= 128
    return left, right, border


LEFT, RIGHT, BORDER = message_lanes()


def users(n):
    table = {}
    for j in MESSAGES[n]:
        l, kind, _ = LEVEL_OF[j]
        for k in ((3 * l - 2, 3 * l - 1) if kind == "D" else (3 * l - 3,)):
            table.setdefault(k, []).append(j)
    return table


def lon_tables():
    raw = {i: np.eye(256)[i] for i in range(COLS)}
    smooth, detail = {0: raw}, {}
    for l in range(1, 5):
        smooth[l], detail[l] = lift(smooth[l - 1], 256)
    ext_s = {}
    for l in (2, 3, 4):
        at, depth, lo, hi = PACK[l]
        seq = {i: np.eye(256)[128 + at + i - lo] for i in range(lo, hi + 1)}
        for k in range(l, 5):
            s, d = lift(seq, 256)
            seq = s
            ext_s[l, k] = (s, d)
    zero = np.zeros(256)
    full_s, full_d = {}, {}
    for k in range(1, 5):
        s, d = dict(smooth[k]), dict(detail[k])
        for l in range(2, k + 1):
            for table, more in ((s, ext_s[l, k][0]), (d, ext_s[l, k][1])):
                for i, v in more.items():
                    table[i] = table.get(i, zero) + v
        full_s[k], full_d[k] = s, d
    return smooth, full_s, full_d


def constants():
    smooth, fs, fd = lon_tables()
    zero = np.zeros(256)
    out = {}
    for l in (1, 2, 3, 4):
        m = MLON[l]
        w = np.zeros((256, 256))
        off = 128 if l == 1 else 64
        for i in range(0, m + 1):
            w[:, i] = fs[l].get(i, zero)
        for i in range(-1, m + 1):
            w[:, off + i + 1] = fd[l].get(i, zero)
        out["W", l] = w if l == 1 else w[:, :128]
        pick = {"sm": fs[l].get(m, zero), "dm1": fd[l].get(m - 1, zero), "dm": fd[l].get(m, zero),
                "s0": fs[l].get(0, zero), "d-1": fd[l].get(-1, zero), "d0": fd[l].get(0, zero)}
        for n, rows in enumerate(MESSAGES):
            rows = [j for j in rows if LEVEL_OF[j][0] == l]
            if not rows:
                continue
            g = np.zeros((256, 128))
            for j in rows:
                for at, names in (LEFT[j], RIGHT[j]):
                    for q, name in enumerate(names):
                        g[:, at + q] = pick[name]
            out["G", n, l] = g
            for k, js in users(n).items():
                if k // 3 != l - 1:
                    continue
                kind = k % 3
                z = np.zeros((128, 256 * ((len(js) + 1) // 2)))
                for p, j in enumerate(js):
                    smooths = np.zeros((128, 128))
                    details = np.zeros((128, 128))
                    at, names = LEFT[j]
                    for q, name in enumerate(names):
                        if name == "dm1":
                            details[at + q, 0] += 1.0
                            if l == 1:
                                smooths[at + q, 0] += 0.25
                        if name == "dm":
                            details[at + q, 1] += 1.0
                            smooths[at + q, 1] += 0.25
                        if name == "sm":
                            smooths[at + q, 0] += 1.0
                    at, names = RIGHT[j]
                    for q, name in enumerate(names):
                        if name == "s0":
                            smooths[at + q, m] += 1.0
                        if name == "d-1":
                            details[at + q, m] += 1.0
                            smooths[at + q, m - 1] += 0.25
                            if l == 1:
                                smooths[at + q, m] += -1.75
                        if name == "d0":
                            details[at + q, m + 1] += 1.0
                            if l == 1:
                                smooths[at + q, m] += 0.25
                    if l > 1:
                        details = np.roll(details, 64, axis=1)
                    z[:, 128 * p:128 * p + 128] = smooths if kind == 1 else details
                for c in range(0, z.shape[1], 256):
                    out["Z", n, k, c // 256] = z[:, c:c + 256]
        n_in = 256 if l == 1 else 128
        eye = np.eye(n_in)
        s = {i: eye[i] for i in range(0, m + 1)}
        d = {i: eye[off + i + 1] for i in range(-1, m + 1)}
        e = {i: s[i] - 0.25 * (d[i - 1] + d[i]) for i in range(0, m + 1)}
        t = np.zeros((n_in, 128))
        for i in range(0, m + 1):
            if 2 * i < 128:
                t[:, 2 * i] = e[i]
            if i < m:
                t[:, 2 * i + 1] = d[i] + 0.5 * (e[i] + e[i + 1])
        out["T", l] = t
    for l in (2, 3, 4):
        at, depth, lo, hi = PACK[l]
        sm = np.zeros((128, 128))
        for i in range(lo, hi + 1):
            sm[:, at + i - lo] = smooth[depth][i][:128]
        out["Sm", l] = sm
    c4 = np.zeros((256, 128))
    for c in range(11):
        c4[:, c] = fs[4].get(c - 1, zero)
    out["C4", 0] = c4
    return out


CONST = constants()


def pack_constants():
    tiles, where = [], {}

    def put(key, a):
        k, n = a.shape
        where[key] = (sum(t.shape[0] for t in tiles), k, n)
        if n < 256:
            a = np.concatenate([a, np.zeros((k, 256 - n), a.dtype)], 1)
        tiles.append(a)

    for key, a in CONST.items():
        if key == ("W", 1) or (key[0] == "G" and key[2] == 1):
            a = a[:128]
        hi = a.astype(ml_dtypes.bfloat16)
        lo = (a - hi.astype(np.float64)).astype(ml_dtypes.bfloat16)
        put(key + ("hi",), hi)
        if np.any(lo.astype(np.float64)):
            put(key + ("lo",), lo)
    return np.concatenate(tiles, 0), where


CB, CWHERE = pack_constants()


def ext_coefficients():
    syms = {("U", 2): 0, ("U", 3): 1, ("U", 4): 2, ("W", 2): 3, ("W", 3): 4, ("W", 4): 5}
    unit = lambda key: np.eye(6)[syms[key]]
    zero = np.zeros(6)
    s = {i: zero for i in range(9)}
    table = {}
    for l in (2, 3, 4):
        m = MLAT[l]
        d = {-1: unit(("U", l)), m: unit(("W", l))}
        for i in range(m):
            d[i] = s[2 * i + 1] - 0.5 * (s[2 * i] + s[2 * i + 2])
        s = {i: s[2 * i] + 0.25 * (d[i - 1] + d[i]) for i in range(m + 1)}
        for i in range(-1, m + 1):
            table[DROW[l] + i + 1] = d[i]
        for i in range(m + 1):
            table[SROW[l] + i] = s[i]
    out = np.zeros((48, 128), np.float32)
    for j, v in table.items():
        for l in (2, 3, 4):
            at, _, lo, hi = PACK[l]
            out[j - 19, at:at + hi - lo + 1] = v[l - 2]
            out[24 + j - 19, at:at + hi - lo + 1] = v[3 + l - 2]
    return out


EXT = ext_coefficients()


def split(a):
    hi = a.astype(BF)
    return hi, (a - hi.astype(F32)).astype(BF)


def dot(a, b):
    return jnp.dot(a, b, preferred_element_type=F32)


def both(hi, lo, w):
    if hi.shape[1] == 128:
        return dot(jnp.concatenate([hi, lo], axis=1), jnp.concatenate([w, w], axis=0))
    return dot(hi, w) + dot(lo, w)


def kernel(x_hbm, vert_hbm, latf_hbm, lonf_hbm, cb_hbm, ext_hbm, inc_hbm, jump_hbm,
           x, vert, latf, lonf, cb, ext_c, inc, jump,
           xs, so, rw, lx, up, dn, p2, r_w, r_u, r_pw, r_pu, r_p2u, r_p2w,
           vst, vtmp, pm, o1, o2, tl, tmsg, sd, m_l, m_r, sf, mf, cbuf,
           bd, sm, pk, pkp, ys, yz, prev, way, send, recv, load):
    tm, lat, lon = lax.axis_index("tm"), lax.axis_index("lat"), lax.axis_index("lon")
    mu = (lat > 0).astype(F32)
    mw = (lat < NLAT_D - 1).astype(F32)
    mu2 = (lat > 1).astype(F32)
    mw2 = (lat < NLAT_D - 2).astype(F32)

    def at_lat(k):
        return (tm, lax.rem(lat + k + NLAT_D, NLAT_D), lon)

    def at_lon(k):
        return (tm, lat, lax.rem(lon + k + NLON_D, NLON_D))

    across = lat + 1 - 2 * lax.rem(lat, 2)

    def at(window, row):
        return (window, row, lon)

    def at_tm(k):
        return (lax.rem(tm + k + 4, 4), lat, lon)

    partners = [at_lat(k) for k in range(1, 8)] + [at_lon(k) for k in range(1, 4)] + [at_tm(1), at_tm(-1), at(lax.rem(tm + 2, 4), across)]
    barrier = pltpu.get_barrier_semaphore()
    for p in partners:
        pl.semaphore_signal(barrier, inc=1, device_id=p, device_id_type=MESH)

    loads = {}
    for n, (name, src, dst) in enumerate((("x", x_hbm, x.at[pl.ds(0, LEV * ROWS)]), ("cb", cb_hbm, cb), ("ext", ext_hbm, ext_c),
                                          ("lonf", lonf_hbm, lonf), ("latf", latf_hbm, latf),
                                          ("vert", vert_hbm, vert))):
        loads[name] = pltpu.make_async_copy(src, dst, load.at[n])
        loads[name].start()

    def const(key):
        at, k, n = CWHERE[key]
        return cb[at:at + k, 0:n]

    def mm(a, *key):
        hi, lo = split(a)
        w = const(key + ("hi",))
        out = both(hi, lo, w)
        if key + ("lo",) in CWHERE:
            out = out + dot(hi, const(key + ("lo",)))
        return out

    loads["x"].wait()
    for r in range(ROWS):
        xs[r, 136:144, :] = jnp.zeros((8, COLS), F32)
        xs[r, 0:LEV, :] = x[pl.ds(r, LEV, stride=ROWS), :]

    for i in range(7):
        rw[1 + i] = xs[2 * i + 1] - 0.5 * (xs[2 * i] + xs[2 * i + 2])
    dn[0] = xs[15] - 0.5 * xs[14]
    up[0] = xs[0]
    up[1] = rw[1]

    sems = iter(range(48))

    def remote(src, dst, dev, slot=None):
        k = next(sems)
        return pltpu.make_async_remote_copy(
            src_ref=src, dst_ref=dst, send_sem=send.at[k],
            recv_sem=recv.at[k], device_id=dev, device_id_type=MESH)

    copies = []

    def go(c):
        c.start()
        copies.append(c)

    so[0] = (-0.125 * mu) * xs[0]
    so[1] = 0.875 * xs[0] + 0.25 * rw[1]
    for i in range(1, 7):
        so[1 + i] = xs[2 * i] + 0.25 * (rw[i] + rw[1 + i])
    so[8] = xs[14] + 0.25 * (rw[7] + dn[0])
    so[9] = (0.25 * mw) * dn[0]
    sbase = {1: 0, 2: 10, 3: 17, 4: 22}
    dbase = {2: 26, 3: 32, 4: 36}
    for l in (2, 3, 4):
        m, a, b, d = MLAT[l], sbase[l - 1], sbase[l], dbase[l]
        S = lambda i: so[a + 1 + i]
        so[d] = S(-1) - 0.5 * S(0)
        for i in range(m):
            so[d + 1 + i] = S(2 * i + 1) - 0.5 * (S(2 * i) + S(2 * i + 2))
        so[d + 1 + m] = (-0.5 * S(2 * m)) if l == 2 else S(2 * m + 1) - 0.5 * S(2 * m)
        so[b] = (0.25 * mu) * so[d]
        for i in range(m):
            so[b + 1 + i] = S(2 * i) + 0.25 * (so[d + i] + so[d + 1 + i])
        so[b + 1 + m] = mw * (S(2 * m) + 0.25 * (so[d + m] + so[d + 1 + m]))
        so[b + 2 + m] = (0.25 * mw) * so[d + 1 + m]
    loads["cb"].wait()
    d4 = mm(so[37], "Sm", 4)
    up[2] = mm(so[27], "Sm", 2) + mm(so[33], "Sm", 3) + d4
    dn[1] = mm(so[30], "Sm", 2) + mm(so[34], "Sm", 3) + d4
    p2[0] = mm(so[38], "Sm", 4)
    p2[1] = mm(so[36], "Sm", 4)
    for i in range(1, 7):
        rw[10 + i] = xs[2 * i] + 0.25 * (rw[i] + rw[i + 1])

    lane = lax.broadcasted_iota(jnp.int32, (1, 128), 1)
    def operand(lo, hi):
        if hi <= 19:
            return rw[lo:hi].reshape((hi - lo) * LP, 128)
        return lx[lo - 19:hi - 19].reshape((hi - lo) * LP, 256)

    def message(n, groups):
        for lo, hi in groups:
            tmsg[0:hi - lo, :, 0:128] = mm(operand(lo, hi), "G", n, LEVEL_OF[lo][0]).reshape(hi - lo, LP, 128)
            v = jnp.zeros((LP, 128), F32) if lo == groups[0][0] else sd[n]
            for j in range(lo, hi):
                (a, na), (b, nb) = LEFT[j], RIGHT[j]
                keep = ((lane >= a) & (lane < a + len(na))) | ((lane >= b) & (lane < b + len(nb)))
                v = jnp.where(keep, tmsg[j - lo, :, 0:128], v)
            sd[n] = v

    def post(n):
        out = [remote(sd.at[n], m_l.at[n], at_lon(1)), remote(sd.at[n], m_r.at[n], at_lon(-1))]
        for c in out:
            c.start()
        return out

    message(0, INNER)
    pl.semaphore_wait(barrier, len(partners))
    bulk = [remote(up.at[pl.ds(0, 2)], r_w, at_lat(-1)), remote(dn.at[0], r_u, at_lat(1))]
    for c in bulk:
        c.start()
    lon0 = post(0)
    go(remote(up.at[2], r_pw, at_lat(-1)))
    go(remote(dn.at[1], r_pu, at_lat(1)))
    go(remote(p2.at[0], r_p2u, at_lat(2)))
    go(remote(p2.at[1], r_p2w, at_lat(-2)))
    packs = copies[:]
    copies.clear()

    for name in ("ext", "lonf", "latf", "vert"):
        loads[name].wait()
    vtmp[...] = jnp.zeros((LP, 256), F32)
    for k in range(BANDS):
        vtmp[0:LEV, 0:LEV] = vert[k]
        hi, lo = split(vtmp[...])
        vst[k, 0:LP, :] = hi
        vst[k, LP:2 * LP, :] = lo
    rowi = lax.broadcasted_iota(jnp.int32, (128, 32), 0)
    coli = lax.broadcasted_iota(jnp.int32, (128, 32), 1)
    mine = ((rowi < 11) & (coli == lax.rem(8 * lon + 31 + rowi, 32))).astype(F32)
    for k in range(NLON_D):
        theirs = (rowi < FOLD_LANES) & (coli == lax.rem(8 * (lon + k) + lax.rem(rowi, WIDE), 32))
        part = jnp.dot(theirs.astype(F32), lonf[...], precision=HIGH, preferred_element_type=F32)
        part = lax.dot_general(mine, part, (((1,), (1,)), ((), ())), precision=HIGH,
                               preferred_element_type=F32)
        c4 = const(("C4", 0, "hi")).astype(F32) + const(("C4", 0, "lo")).astype(F32)
        hi, lo = split(jnp.dot(c4, part, precision=HIGH, preferred_element_type=F32))
        pm[0, :, k * 128:(k + 1) * 128] = hi
        pm[1, :, k * 128:(k + 1) * 128] = lo

    low = lane < 64
    def vmul(ks, t):
        hi, lo = split(t)
        pair = jnp.concatenate([hi, lo], axis=1)
        outs = []
        for k in ks:
            p = dot(vst[k][:, 0:LP], pair)
            outs.append(p[0:LP, 0:128] + p[0:LP, 128:256] + p[LP:2 * LP, 0:128])
        return outs

    def settle(n):
        got = jnp.where(lane < BORDER[n], m_l[n], m_r[n])
        for k, js in users(n).items():
            hi, lo = split(vmul((k,), got)[0])
            for c in range((len(js) + 1) // 2):
                p = both(hi, lo, const(("Z", n, k, c, "hi")))
                for h, j in enumerate(js[2 * c:2 * c + 2]):
                    at = j + 42 if k == 1 else j
                    bd[at] = bd[at] + p[:, 128 * h:128 * h + 128]

    def own_part(lo, hi):
        if lo < 10:
            o1[lo:hi] = mm(operand(lo, hi), "W", 1).reshape(hi - lo, LP, 256)
        else:
            h, l = split(operand(lo, hi))
            w = const(("W", 1, "hi"))[:, 128:256]
            o1[lo:hi, :, 128:256] = both(h, l, w).reshape(hi - lo, LP, 128)

    def bands1(js):
        for j in js:
            if j < 10:
                bd[42 + j] = vmul((1,), o1[j, :, 0:128])[0]
                bd[j] = vmul((2,), o1[j, :, 128:256])[0]
            else:
                bd[j] = vmul((0,), o1[j, :, 128:256])[0]

    def bands(l):
        lo, hi = COARSER[l - 2]
        o2[lo - 19:hi - 19] = mm(operand(lo, hi), "W", l).reshape(hi - lo, LP, 128)
        for j in range(lo, hi):
            if LEVEL_OF[j][1] == "D":
                a, b = vmul((3 * l - 2, 3 * l - 1), o2[j - 19])
                bd[j] = jnp.where(low, a, b)
            else:
                bd[j] = jnp.where(low, 0.0, vmul((3 * l - 3,), o2[j - 19])[0])

    def even(i):
        tl[2 * i, :, 0:128] = -0.25 * (bd[42 + i] + bd[43 + i])
        tl[2 * i, :, 128:256] = bd[10 + i] - 0.25 * (bd[i] + bd[i + 1])

    def odd(i):
        tl[2 * i + 1, :, 0:128] = bd[43 + i] + 0.5 * (tl[2 * i, :, 0:128] + tl[2 * i + 2, :, 0:128])
        tl[2 * i + 1, :, 128:256] = bd[1 + i] + 0.5 * (tl[2 * i, :, 128:256] + tl[2 * i + 2, :, 128:256])

    def level1(lo, hi):
        ys[lo:hi] = mm(tl[lo:hi].reshape((hi - lo) * LP, 256), "T", 1).reshape(hi - lo, LP, 128)

    def to_next(src, dst):
        c = remote(src, dst, at_tm(1))

        @pl.when(tm < 3)
        def _():
            c.start()

        return c

    @pl.when(tm == 0)
    def _():
        prev[...] = jnp.zeros((ROWS, LP, 128), F32)
        pkp[...] = jnp.zeros((5, LP, 128), F32)

    for lo, hi in INNER:
        own_part(lo, hi)
    bands1(MESSAGES[0])
    for c in lon0:
        c.wait()
    settle(0)
    for i in range(1, 7):
        even(i)
    for i in range(1, 6):
        odd(i)
    level1(2, 13)
    for c in bulk:
        c.wait()
    x16 = lambda: mw * r_w[0]
    rw[0] = mu * r_u[...] - 0.5 * xs[0]
    rw[8] = dn[0] - 0.5 * x16()
    rw[9] = mw * r_w[1]
    rw[10] = xs[0] + 0.25 * (rw[0] + rw[1])
    rw[17] = xs[14] + 0.25 * (rw[7] + rw[8])
    rw[18] = x16() + (0.25 * mw) * (rw[8] + rw[9])
    rw[0] = mu * rw[0]
    message(1, OUTER)
    lon1 = post(1)
    for lo, hi in OUTER:
        own_part(lo, hi)
    bands1(MESSAGES[1])

    for c in packs:
        c.wait()

    shift = [to_next(ys.at[pl.ds(2, DIRECT)], prev.at[pl.ds(2, DIRECT)])]
    straight = remote(ys.at[pl.ds(2 + DIRECT, 2 * CHUNKS)], prev.at[pl.ds(2 + DIRECT, 2 * CHUNKS)], at_tm(1))
    hops = []
    for q in range(CHUNKS):
        mine, kept, there = ys.at[pl.ds(2 + DIRECT + 2 * q, 2)], way.at[pl.ds(2 * q, 2)], prev.at[pl.ds(2 + DIRECT + 2 * q, 2)]
        hops.append((remote(mine, kept, at(3, across)), remote(kept, kept, at(0, lat)),
                     remote(kept, there, at(2, across))))

    @pl.when((tm == 0) | (tm == 2))
    def _():
        straight.start()

    @pl.when(tm == 1)
    def _():
        for q in range(CHUNKS):
            hops[q][0].start()

    def forward(window, hop):
        @pl.when(tm == window)
        def _():
            for q in range(CHUNKS):
                hops[q][hop].wait_recv()
                hops[q][hop + 1].start()

    raw = lambda j: rw[j] if j < 19 else lx[j - 19, :, 0:128]
    for l in (2, 3, 4):
        m, a, d, b = MLAT[l], SROW[l - 1], DROW[l], SROW[l]
        lx[d - 19, :, 0:128] = so[dbase[l]]
        lx[d + m + 1 - 19, :, 0:128] = so[dbase[l] + m + 1]
        for i in range(m):
            lx[d + 1 + i - 19, :, 0:128] = raw(a + 2 * i + 1) - 0.5 * (raw(a + 2 * i) + raw(a + 2 * i + 2))
        for i in range(m + 1):
            v = raw(a + 2 * i) + 0.25 * (raw(d + i) + raw(d + i + 1))
            lx[b + i - 19, :, 0:128] = mw * v if i == m else v
    r_pu[...] = mu * r_pu[...] + mu2 * r_p2u[...]
    r_pw[...] = mw * r_pw[...] + mw2 * r_p2w[...]
    for j in range(19, NROWS):
        cu, cw = ext_c[j - 19:j - 18, :], ext_c[24 + j - 19:24 + j - 18, :]
        l, kind, i = LEVEL_OF[j]
        if kind == "S" and i == MLAT[l]:
            cu, cw = cu * mw, cw * mw
        lx[j - 19, :, 128:256] = r_pu[...] * cu + r_pw[...] * cw
    for l in (2, 3, 4):
        lx[DROW[l] - 19] = mu * lx[DROW[l] - 19]

    hi, lo = split(lx[SROW[4] - 19])
    fold = dot(hi, pm[0]) + dot(lo, pm[0]) + dot(hi, pm[1])
    for k in range(NLON_D):
        acc = jnp.zeros((FOLD, 128), F32)
        for g in range(LP // FOLD):
            acc = jnp.where((lane >= g * WIDE) & (lane < (g + 1) * WIDE),
                            fold[g * FOLD:(g + 1) * FOLD, k * 128:(k + 1) * 128], acc)
        sf[k] = acc
    for k in range(1, NLON_D):
        go(remote(sf.at[k], mf.at[k], at_lon(k)))
    coarse = copies[:]
    copies.clear()

    message(2, COARSER)
    lon2 = post(2)
    bands(4)
    bands(3)

    forward(3, 0)

    for c in coarse:
        c.wait()
    row = sf[0] + mf[1] + mf[2] + mf[3]
    sf[0] = row
    cbuf[lat] = row
    for k in range(1, NLAT_D):
        go(remote(sf.at[0], cbuf.at[lat], at_lat(k)))
    coarse = copies[:]
    copies.clear()

    for c in lon1:
        c.wait()
    settle(1)
    for i in (0, 7, 8):
        even(i)
    for i in (0, 6, 7):
        odd(i)
    level1(0, 2)
    level1(13, 16)
    shift.append(to_next(ys.at[pl.ds(0, 2)], prev.at[pl.ds(0, 2)]))
    shift.append(to_next(ys.at[pl.ds(13, 3)], prev.at[pl.ds(13, 3)]))
    bands(2)
    for c in lon2:
        c.wait()
    settle(2)
    forward(0, 1)

    for c in coarse:
        c.wait()
    for rho in range(2):
        w = latf[pl.ds(jnp.minimum(lat + rho, NLAT_D - 1), 1), :]
        t = sum(cbuf[a] * w[:, a:a + 1] for a in range(NLAT_D))
        parts = [t if g == 0 else pltpu.roll(t, 128 - WIDE * g, 1) for g in range(LP // FOLD)]
        c = jnp.where(lane < WIDE, jnp.concatenate(parts, axis=0), 0.0)
        v = vmul((BANDS - 1,), c)[0]
        sm[rho] = v * mw if rho else v

    for l in (4, 3, 2):
        m, d, b = MLAT[l], DROW[l], SROW[l]
        for i in range(m + 1):
            s = bd[b + i] + sm[i]
            sm[i] = s - 0.25 * (bd[d + i] + bd[d + i + 1])
        for i in range(2 * m, -1, -1):
            if i % 2:
                h = i // 2
                tmsg[i, :, 0:128] = bd[d + 1 + h] + 0.5 * (sm[h] + sm[h + 1])
            else:
                tmsg[i, :, 0:128] = sm[i // 2]
        n = 2 * m + 1
        out = mm(tmsg[0:n, :, 0:128].reshape(n * LP, 128), "T", l).reshape(n, LP, 128)
        sm[0:n] = out
        sm[2 * m] = mw * sm[2 * m]

    last = sm[8]
    for k in range(9):
        last = jnp.where(lane == 64 + k, sm[k] if k == 0 else pltpu.roll(sm[k], k, 1), last)
    for k in range(4):
        pk[k] = jnp.where(low, sm[k], pltpu.roll(sm[k + 4], 64, 1))
    pk[4] = last
    shift.append(to_next(pk, pkp))

    def lifted(rows):
        w = const(("T", 1, "hi"))[0:128]
        for i in range(8):
            tmsg[2 * i, :, 0:128] = rows[i]
            tmsg[2 * i + 1, :, 0:128] = 0.5 * (rows[i] + rows[i + 1])
        h, l = split(tmsg[0:16, :, 0:128].reshape(16 * LP, 128))
        return both(h, l, w).reshape(ROWS, LP, 128)

    yz[...] = ys[...] + lifted(sm)
    for r in range(ROWS):
        inc[pl.ds(r, LEV, stride=ROWS), :] = yz[r, 0:LEV, :]
    out = pltpu.make_async_copy(inc.at[pl.ds(0, LEV * ROWS)], inc_hbm, load.at[6])
    out.start()

    def land(cs):
        for c in cs:
            pl.when(tm > 0)(c.wait_recv)

    land(shift[:3])
    pl.when((tm == 1) | (tm == 3))(straight.wait_recv)

    @pl.when(tm == 2)
    def _():
        for q in range(CHUNKS):
            hops[q][2].wait_recv()

    yz[...] = yz[...] - prev[...]
    land(shift[3:])
    for k in range(9):
        part = pkp[k % 4] if k < 8 else pkp[4]
        if 4 <= k < 8:
            part = pltpu.roll(part, 64, 1)
        end = pkp[4] if k == 0 else pltpu.roll(pkp[4], 128 - k, 1)
        sm[k] = jnp.where(lane == 64, end, part)
    less = lifted(sm)
    for r in range(ROWS):
        jump[pl.ds(r, LEV, stride=ROWS), :] = yz[r, 0:LEV, :] - less[r, 0:LEV, :]
    out2 = pltpu.make_async_copy(jump.at[pl.ds(0, LEV * ROWS)], jump_hbm, load.at[7])
    out2.start()
    for c in shift:
        pl.when(tm < 3)(c.wait_send)
    pl.when((tm == 0) | (tm == 2))(straight.wait_send)
    for window, hop in ((1, 0), (3, 1), (0, 2)):
        @pl.when(tm == window)
        def _(hop=hop):
            for q in range(CHUNKS):
                hops[q][hop].wait_send()

    out.wait()
    out2.wait()


def body(forcing, vertical, lat_factor, lon_factor):
    x = forcing.reshape(LEV * ROWS, COLS)
    tile = (LP, 128)
    anywhere = pl.BlockSpec(memory_space=pl.ANY)
    S = pltpu.VMEM
    flat, roomy = (LEV * ROWS, COLS), (LP * ROWS, COLS)
    scratch = [
        S(roomy, F32), S((BANDS, LEV, LEV), F32), S((8, 8), F32), S((32, 32), F32), S(CB.shape, BF), S(EXT.shape, F32),
        S(roomy, F32), S(roomy, F32),
        S((ROWS,) + tile, F32), S((39,) + tile, F32), S((19,) + tile, F32), S((23, LP, 256), F32),
        S((3,) + tile, F32), S((2,) + tile, F32), S((2,) + tile, F32),
        S((2,) + tile, F32), S(tile, F32), S(tile, F32), S(tile, F32), S(tile, F32), S(tile, F32),
        S((BANDS, 2 * LP, 256), BF), S((LP, 256), F32), S((2, 256, 512), BF),
        S((19, LP, 256), F32), S((23,) + tile, F32), S((17, LP, 256), F32), S((19, LP, 256), F32),
        S((3,) + tile, F32), S((3,) + tile, F32), S((3,) + tile, F32),
        S((4, FOLD, 128), F32), S((4, FOLD, 128), F32), S((8, FOLD, 128), F32),
        S((52,) + tile, F32), S((9,) + tile, F32), S((5,) + tile, F32), S((5,) + tile, F32),
        S((ROWS,) + tile, F32), S((ROWS,) + tile, F32), S((ROWS,) + tile, F32), S((2 * CHUNKS,) + tile, F32),
        pltpu.SemaphoreType.DMA((48,)), pltpu.SemaphoreType.DMA((48,)), pltpu.SemaphoreType.DMA((8,)),
    ]
    out = jax.ShapeDtypeStruct((LEV * ROWS, COLS), F32)
    inc, jump = pl.pallas_call(
        kernel,
        out_shape=(out, out),
        in_specs=[anywhere] * 6,
        out_specs=(anywhere, anywhere),
        scratch_shapes=scratch,
        compiler_params=pltpu.CompilerParams(
            collective_id=0, has_side_effects=True, vmem_limit_bytes=56 * 1024 * 1024),
    )(x, vertical, lat_factor, lon_factor, jnp.asarray(CB), jnp.asarray(EXT))

    def settle(a, b, c, d, held, arrive, leave):
        size = LEV * ROWS // 2
        moves = []
        for k in range(2):
            for h, (src, dst) in enumerate(((a, c), (b, d))):
                part = pl.ds(k * size, size)
                moves.append((pltpu.make_async_copy(src.at[part], held.at[h, part], arrive.at[2 * k + h]),
                              pltpu.make_async_copy(held.at[h, part], dst.at[part], leave.at[2 * k + h])))
        for m, _ in moves:
            m.start()
        for m, o in moves:
            m.wait()
            o.start()
        for _, o in moves:
            o.wait()

    inc, jump = pl.pallas_call(
        settle, out_shape=(out, out), in_specs=[anywhere] * 2, out_specs=(anywhere, anywhere),
        scratch_shapes=[S((2,) + flat, F32), pltpu.SemaphoreType.DMA((4,)), pltpu.SemaphoreType.DMA((4,))],
    )(inc, jump)
    shape = (1, LEV, ROWS, COLS)
    return inc.reshape(shape), jump.reshape(shape)


def solution(mesh):
    placed = (P("tm", None, "lat", "lon"), P(), P(), P())
    return jax.shard_map(
        body,
        mesh=mesh,
        in_specs=placed,
        out_specs=(P("tm", None, "lat", "lon"), P("tm", None, "lat", "lon")),
        check_vma=False,
    )
```
